32 devices in a mesh: ctx: 8 (over z, y), head: 4 (over x, core).
Axes of the slice: x: 2, y: 2, z: 4, core: 2. Of those that a mesh axis runs over, the one named last changes fastest.
Arguments:
- query_self: bfloat16 [512, 8192], P('ctx', 'head'), may hold values from -60 to 60
- key_self: bfloat16 [512, 1024], P('ctx', 'head'), may hold values from -6 to 6
- value_self: bfloat16 [512, 1024], P('ctx', 'head'), may hold values from -6 to 6
- positions: int32 [512], P('ctx'), may hold values from 0 to 1533, as said below
- query_cross: bfloat16 [512, 8192], P('ctx', 'head'), may hold values from -60 to 60
- key_vision: bfloat16 [7168, 1024], P('ctx', 'head'), may hold values from -6 to 6
- value_vision: bfloat16 [7168, 1024], P('ctx', 'head'), may hold values from -6 to 6
- media_range: int32 [32, 2], P('ctx'), may hold values from 0 to 8, as said below
- gate_scale: float32 [1], replicated, may hold values from 0.3 to 1.5
Outputs:
- self_context: bfloat16 [512, 8192], P(('ctx', 'head'))
- cross_context: bfloat16 [512, 8192], P(('ctx', 'head'))
The draws below stay inside these ranges and needn't reach their ends.
Inputs may be any that keep to these rules, and one draw needn't show every extreme that they name: `positions`: strictly increasing along the transcript, starting at 0; gaps of 1 to 3 up to the next-to-last token, and the last token's position is exactly 1533. `media_range`: column 0 never exceeds column 1; column 1 never falls from block to block, is 0 for the leading blocks (which see no frame) and 8 for the last block.
All inputs are finite; a program needn't handle non-finite values.
Results may differ from the reference program's by a relative error of at most 0.0091.
Values may be sent and summed in bfloat16 or wider, within the bound.
No kernel may reach another device: no remote copies, remote signals or barrier semaphores. Data moves between devices by JAX's collectives and lax.ppermute only.
A program may use at most 64 MiB of HBM per device.

```python
import jax
import jax.numpy as jnp
from jax import lax

HQ = 64
KVH = 8
HD = 128
TBLOCK = 16
FRAMES = 8
FRAME_LEN = 896
TEXT = 512
BLOCKS = 32
VIS = 7168


def media_table(key):
    inner_key = jax.random.fold_in(key, 55)
    bump_draw = jax.random.randint(jax.random.fold_in(inner_key, 1), (BLOCKS,), 0, 2)
    block_index = jnp.arange(BLOCKS, dtype=jnp.int32)
    upper_frame = jnp.clip(block_index * (FRAMES + 1) // BLOCKS - 1 + bump_draw, 0, FRAMES)
    upper_frame = lax.cummax(upper_frame, axis=0)
    upper_frame = upper_frame.at[BLOCKS - 1].set(FRAMES)
    reach_frames = jax.random.randint(jax.random.fold_in(inner_key, 2), (BLOCKS,), 1, FRAMES + 1)
    lower_frame = jnp.maximum(upper_frame - reach_frames, 0)
    return jnp.stack([lower_frame, upper_frame], axis=1).astype(jnp.int32)


def base_draw(key, salt, shape, scale):
    return jnp.clip(scale * jax.random.normal(jax.random.fold_in(key, salt), shape, jnp.float32), -6.0 * scale, 6.0 * scale)


def draw_query_self(key, part):
    drawn = base_draw(key, 11, (TEXT, HQ * HD), 2.5)
    return drawn.astype(jnp.bfloat16)


def draw_key_self(key, part):
    drawn = base_draw(key, 12, (TEXT, KVH * HD), 1.0)
    return drawn.astype(jnp.bfloat16)


def draw_positions(key, part):
    gaps = jax.random.randint(jax.random.fold_in(key, 21), (TEXT,), 1, 4)
    running = jnp.cumsum(gaps)
    running = running - running[0]
    running = running.at[TEXT - 1].set(3 * (TEXT - 1))
    return running.astype(jnp.int32)


def draw_query_cross(key, part):
    drawn = base_draw(key, 14, (TEXT, HQ * HD), 2.5)
    return drawn.astype(jnp.bfloat16)


def draw_key_vision(key, part):
    drawn = base_draw(key, 13, (VIS, KVH * HD), 1.0)
    return drawn.astype(jnp.bfloat16)


def draw_media_range(key, part):
    return media_table(key)


def steps_of(key, shape, cuts, low, high):
    def one(dim, shards_of):
        steps = jax.random.uniform(jax.random.fold_in(jax.random.fold_in(key, 6), dim), (shards_of,), jnp.float32, low / len(cuts), high / len(cuts))
        return jnp.repeat(jnp.exp(steps), shape[dim] // shards_of).reshape((-1,) + (1,) * (len(shape) - dim - 1))

    gain = one(*cuts[0])
    for cut in cuts[1:]:
        gain = gain * one(*cut)
    return gain


def noise(stream_key, shape, deviation, reach, split=(), held_as=jnp.bfloat16):
    array = jax.random.normal(stream_key, shape, jnp.float32) * deviation
    if len(split) > 0:
        array = steps_of(stream_key, shape, split, -0.22, 0.18) * array
    return jnp.clip(array, min=-reach, max=reach).astype(held_as)


def setup_inputs(seed: int = 0) -> dict:
    splits = jax.random.split(jax.random.key(seed), 10)
    return {
        "query_self": draw_query_self(jax.random.fold_in(splits[9], 71), 0),
        "key_self": draw_key_self(jax.random.fold_in(splits[9], 71), 0),
        "value_self": noise(splits[2], (TEXT, KVH * HD), 1.0, 6.0, ((0, 8), (1, 4))),
        "positions": draw_positions(jax.random.fold_in(splits[9], 71), 0),
        "query_cross": draw_query_cross(jax.random.fold_in(splits[9], 71), 0),
        "key_vision": draw_key_vision(jax.random.fold_in(splits[9], 71), 0),
        "value_vision": noise(splits[6], (VIS, KVH * HD), 1.0, 6.0, ((0, 8), (1, 4))),
        "media_range": draw_media_range(jax.random.fold_in(splits[9], 71), 0),
        "gate_scale": jnp.clip(jax.random.uniform(splits[8], (1,), jnp.float32, 0.3, 1.5), 0.3, 1.5),
    }


rope_base = 500000.0
lowest = -1e30


def rotate(values, positions):
    half_width = values.shape[-1] // 2
    exponents = jnp.arange(half_width, dtype=jnp.float32) * (2.0 / values.shape[-1])
    frequency = jnp.power(rope_base, -exponents)
    angles = positions.astype(jnp.float32)[:, None] * frequency[None, :]
    cosine = jnp.cos(angles)[:, None, :]
    sine_part = jnp.sin(angles)[:, None, :]
    first_half = values[..., :half_width]
    second_half = values[..., half_width:]
    return jnp.concatenate([first_half * cosine - second_half * sine_part, second_half * cosine + first_half * sine_part], axis=-1)


def blocked(queries, key_rows, value_rows, mask_rows):
    total_rows = queries.shape[0]
    group_size = queries.shape[2]
    block_rows = 512 if total_rows % 512 == 0 else total_rows
    block_count = total_rows // block_rows
    scale_factor = HD ** -0.5

    def one_block(item_index):
        head_index = item_index // block_count
        row_begin = (item_index % block_count) * block_rows
        query_block = lax.dynamic_slice_in_dim(queries, row_begin, block_rows, 0)
        query_block = lax.dynamic_index_in_dim(query_block, head_index, 1, keepdims=False)
        key_part = lax.dynamic_index_in_dim(key_rows, head_index, 1, keepdims=False)
        value_part = lax.dynamic_index_in_dim(value_rows, head_index, 1, keepdims=False)
        allowed = mask_rows(row_begin, block_rows)[None, :, :]
        scores = jnp.einsum("rgd,md->grm", query_block.astype(jnp.float32), key_part.astype(jnp.float32)) * scale_factor
        scores = jnp.where(allowed, scores, lowest)
        row_peak = jnp.max(scores, axis=-1, keepdims=True)
        weights = jnp.where(allowed, jnp.exp(scores - row_peak), 0.0)
        totals = jnp.sum(weights, axis=-1)
        rounded = lax.optimization_barrier(weights.astype(jnp.bfloat16))
        mixed_rows = jnp.einsum("grm,md->grd", rounded.astype(jnp.float32), value_part.astype(jnp.float32))
        safe_totals = jnp.where(totals > 0.0, totals, 1.0)
        return mixed_rows / safe_totals[..., None]

    results = lax.map(one_block, jnp.arange(KVH * block_count, dtype=jnp.int32))
    results = results.reshape(KVH, block_count, group_size, block_rows, HD)
    return jnp.transpose(results, (1, 3, 0, 2, 4)).reshape(total_rows, KVH * group_size * HD)


def reference(query_self, key_self, value_self, positions, query_cross, key_vision, value_vision, media_range, gate_scale):
    group_size = HQ // KVH
    rotated_query = rotate(query_self.astype(jnp.float32).reshape(TEXT, HQ, HD), positions)
    rotated_query = rotated_query.astype(jnp.bfloat16).reshape(TEXT, KVH, group_size, HD)
    rotated_key = rotate(key_self.astype(jnp.float32).reshape(TEXT, KVH, HD), positions).astype(jnp.bfloat16)
    text_index = jnp.arange(TEXT, dtype=jnp.int32)

    def causal_rows(row_begin, block_rows):
        row_index = row_begin + jnp.arange(block_rows, dtype=jnp.int32)
        return text_index[None, :] <= row_index[:, None]

    self_context = blocked(rotated_query, rotated_key, value_self.reshape(TEXT, KVH, HD), causal_rows).astype(jnp.bfloat16)
    lower_frame = jnp.repeat(media_range[:, 0], TBLOCK)
    upper_frame = jnp.repeat(media_range[:, 1], TBLOCK)
    frame_index = jnp.arange(VIS, dtype=jnp.int32) // FRAME_LEN

    def frame_rows(row_begin, block_rows):
        lower_part = lax.dynamic_slice_in_dim(lower_frame, row_begin, block_rows, 0)
        upper_part = lax.dynamic_slice_in_dim(upper_frame, row_begin, block_rows, 0)
        return jnp.logical_and(frame_index[None, :] >= lower_part[:, None], frame_index[None, :] < upper_part[:, None])

    cross = blocked(query_cross.reshape(TEXT, KVH, group_size, HD), key_vision.reshape(VIS, KVH, HD), value_vision.reshape(VIS, KVH, HD), frame_rows)
    has_frames = upper_frame > lower_frame
    cross_context = jnp.where(has_frames[:, None], jnp.tanh(gate_scale[0]) * cross, 0.0).astype(jnp.bfloat16)
    return self_context, cross_context
```

```python
import functools

import jax
import jax.numpy as jnp
from jax import lax
from jax.experimental import pallas as pl
from jax.experimental.pallas import tpu as pltpu
from jax.sharding import PartitionSpec as P

HD = 128
TBLOCK = 16
FRAME_LEN = 896


rope_base = 500000.0
lowest = -1e30


def rotate(values, positions):
    half_width = values.shape[-1] // 2
    exponents = jnp.arange(half_width, dtype=jnp.float32) * (2.0 / values.shape[-1])
    frequency = jnp.power(rope_base, -exponents)
    angles = positions.astype(jnp.float32)[:, None] * frequency[None, :]
    cosine = jnp.cos(angles)[:, None, :]
    sine_part = jnp.sin(angles)[:, None, :]
    first_half = values[..., :half_width]
    second_half = values[..., half_width:]
    return jnp.concatenate(
        [
            first_half * cosine - second_half * sine_part,
            second_half * cosine + first_half * sine_part,
        ],
        axis=-1,
    )


def key_block(key_count):
    block_size = min(key_count, 1024)
    while key_count % block_size != 0:
        block_size = block_size - 1
    return block_size


def attend_block(state_in, queries, key_rows, value_rows, allowed):
    maxima, totals, accumulated = state_in
    scale_factor = queries.shape[-1] ** (-0.5)
    scores = (
        jnp.einsum("rkgd,nkd->kgrn", queries, key_rows, preferred_element_type=jnp.float32)
        * scale_factor
    )
    visible = allowed[None, None, :, :]
    scores = jnp.where(visible, scores, lowest)
    new_maxima = jnp.maximum(maxima, jnp.max(scores, axis=-1))
    weights = jnp.where(visible, jnp.exp(scores - new_maxima[..., None]), 0.0)
    factor = jnp.exp(maxima - new_maxima)
    totals = totals * factor + jnp.sum(weights, axis=-1)
    accumulated = accumulated * factor[..., None] + jnp.einsum(
        "kgrn,nkd->kgrd",
        weights.astype(jnp.bfloat16),
        value_rows,
        preferred_element_type=jnp.float32,
    )
    return (new_maxima, totals, accumulated)


def attend(state_in, queries, key_rows, value_rows, allowed):
    key_count = key_rows.shape[0]
    block_size = key_block(key_count)
    if block_size == key_count:
        return attend_block(state_in, queries, key_rows, value_rows, allowed)

    def step_block(block_index, state_now):
        row_begin = block_index * block_size
        key_part = lax.dynamic_slice_in_dim(key_rows, row_begin, block_size, 0)
        value_part = lax.dynamic_slice_in_dim(value_rows, row_begin, block_size, 0)
        allowed_part = lax.dynamic_slice_in_dim(allowed, row_begin, block_size, 1)
        return attend_block(state_now, queries, key_part, value_part, allowed_part)

    return lax.fori_loop(0, key_count // block_size, step_block, state_in)


def keep_state(current):
    return current


def empty_state(row_count, kv_heads, group_size, head_size):
    maxima = jnp.full((kv_heads, group_size, row_count), lowest, jnp.float32)
    totals = jnp.zeros((kv_heads, group_size, row_count), jnp.float32)
    accumulated = jnp.zeros((kv_heads, group_size, row_count, head_size), jnp.float32)
    return (maxima, totals, accumulated)


def finish(state_in):
    maxima, totals, accumulated = state_in
    safe_totals = jnp.where(totals > 0.0, totals, 1.0)
    result = accumulated / safe_totals[..., None]
    kv_heads, group_size, row_count, head_size = result.shape
    return jnp.transpose(result, (2, 0, 1, 3)).reshape(row_count, kv_heads * group_size * head_size)


def causal_group(current, group, key_rows, value_rows, key_index, offset):
    queries, row_index = group
    allowed = key_index[None, :] <= row_index[:, None]

    def causal_compute(state_in):
        return attend(state_in, queries, key_rows, value_rows, allowed)

    return lax.cond(offset <= jnp.max(row_index), causal_compute, keep_state, current)


def frame_mask(frame_index, lower_frame, upper_frame):
    return jnp.logical_and(
        frame_index[None, :] >= lower_frame[:, None], frame_index[None, :] < upper_frame[:, None]
    )


def on_device_gathered(
    query_self,
    key_self,
    value_self,
    positions,
    query_cross,
    key_vision,
    value_vision,
    media_range,
    gate_scale,
):
    head_size = HD
    kv_heads = key_self.shape[1] // head_size
    group_size = query_self.shape[1] // key_self.shape[1]
    row_count = query_self.shape[0]
    vision_count = key_vision.shape[0]
    device = lax.axis_index("ctx")
    own_rows = device * row_count + jnp.arange(row_count, dtype=jnp.int32)
    rotated_query = rotate(
        query_self.astype(jnp.float32).reshape(row_count, kv_heads * group_size, head_size),
        positions,
    )
    rotated_query = rotated_query.astype(jnp.bfloat16).reshape(
        row_count, kv_heads, group_size, head_size
    )
    rotated_key = rotate(
        key_self.astype(jnp.float32).reshape(row_count, kv_heads, head_size), positions
    ).astype(jnp.bfloat16)
    self_values = value_self.reshape(row_count, kv_heads, head_size)
    vision_keys = key_vision.reshape(vision_count, kv_heads, head_size)
    vision_values = value_vision.reshape(vision_count, kv_heads, head_size)
    cross_queries = query_cross.reshape(row_count, kv_heads, group_size, head_size)
    lower_frame = jnp.repeat(media_range[:, 0], TBLOCK)
    upper_frame = jnp.repeat(media_range[:, 1], TBLOCK)
    has_frames = upper_frame > lower_frame
    query_groups = ((rotated_query, own_rows),)
    self_start = tuple(
        (empty_state(group[1].shape[0], kv_heads, group_size, head_size) for group in query_groups)
    )
    cross_start = empty_state(row_count, kv_heads, group_size, head_size)
    offset = jnp.int32(0)
    key_rows = lax.all_gather(rotated_key, "ctx", axis=0, tiled=True)
    value_rows = lax.all_gather(self_values, "ctx", axis=0, tiled=True)
    key_index = jnp.arange(key_rows.shape[0], dtype=jnp.int32)
    updated = []
    for current, group in zip(self_start, query_groups):
        updated.append(causal_group(current, group, key_rows, value_rows, key_index, offset))
    self_states = tuple(updated)
    key_rows = lax.all_gather(vision_keys, "ctx", axis=0, tiled=True)
    value_rows = lax.all_gather(vision_values, "ctx", axis=0, tiled=True)
    frame_index = jnp.arange(key_rows.shape[0], dtype=jnp.int32) // FRAME_LEN
    allowed = frame_mask(frame_index, lower_frame, upper_frame)
    touching = jnp.logical_and(lower_frame <= frame_index[-1], upper_frame > frame_index[0])
    needed = jnp.any(jnp.logical_and(has_frames, touching))

    def fold_compute(state_in):
        return attend(state_in, cross_queries, key_rows, value_rows, allowed)

    cross_state = lax.cond(needed, fold_compute, keep_state, cross_start)
    self_rows = finish(self_states[0]).astype(jnp.bfloat16)
    cross_rows = jnp.where(
        has_frames[:, None], jnp.tanh(gate_scale[0]) * finish(cross_state), 0.0
    ).astype(jnp.bfloat16)
    self_context, cross_context = (
        lax.all_to_all(self_rows, "head", split_axis=0, concat_axis=1, tiled=True),
        lax.all_to_all(cross_rows, "head", split_axis=0, concat_axis=1, tiled=True),
    )
    return (self_context, cross_context)


log2e = 1.4426950408889634
stat_rows = 16
unseen = -1e30
contract_last = (((1,), (1,)), ((), ()))


def whole(count):
    return [pl.BlockSpec(memory_space=pltpu.VMEM)] * count


def split_heads_kernel(inner, key_ref, value_ref, keep_ref, other_ref):
    place = lax.rem(lax.axis_index("ctx"), inner)
    for slot, source in enumerate((key_ref, value_ref)):
        for side, target in enumerate((keep_ref, other_ref)):
            head = place if side == 0 else 1 - place
            target[slot] = source[:, pl.ds(pl.multiple_of(head * HD, HD), HD)]


def split_heads(keys, values, inner):
    rows, columns = keys.shape
    shape = jax.ShapeDtypeStruct((2, rows, columns // inner), keys.dtype)
    return pl.pallas_call(
        functools.partial(split_heads_kernel, inner),
        out_shape=(shape, shape),
        in_specs=whole(2),
        out_specs=whole(2),
        compiler_params=pltpu.CompilerParams(vmem_limit_bytes=24 * 2**20),
        name="split_vision_heads",
    )(keys, values)


def pack_queries_kernel(
    inner,
    query_ref,
    key_ref,
    value_ref,
    cross_ref,
    cosine_ref,
    sine_ref,
    range_ref,
    keep_ref,
    other_ref,
):
    group = query_ref.shape[1] // inner
    place = lax.rem(lax.axis_index("ctx"), inner)
    cosine = cosine_ref[...]
    sine = sine_ref[...]

    def turned(block):
        block = block.astype(jnp.float32)
        return (block * cosine + pltpu.roll(block, HD // 2, 1) * sine).astype(jnp.bfloat16)

    def head_columns(head):
        return pl.ds(pl.multiple_of(head * HD, HD), HD)

    for side, target in enumerate((keep_ref, other_ref)):
        head = place if side == 0 else 1 - place
        target[:, :group] = cross_ref[:, pl.ds(pl.multiple_of(head * group, group), group)]
        target[:, group : group + HD] = range_ref[...]
        target[:, group + HD : group + 2 * HD] = turned(key_ref[:, head_columns(head)])
        target[:, group + 2 * HD : group + 3 * HD] = value_ref[:, head_columns(head)]
        begin = group + 3 * HD
        for item in range(group // HD):
            target[:, begin + item * HD : begin + (item + 1) * HD] = turned(
                query_ref[:, head_columns(head * (group // HD) + item)]
            )


def pack_queries(query_self, key_self, value_self, query_cross, cosine, sine, ranges, inner):
    rows, columns = query_self.shape
    shape = jax.ShapeDtypeStruct((rows, 2 * (columns // inner) + 3 * HD), jnp.bfloat16)
    return pl.pallas_call(
        functools.partial(pack_queries_kernel, inner),
        out_shape=(shape, shape),
        in_specs=whole(7),
        out_specs=whole(2),
        name="rotate_and_pack",
    )(query_self, key_self, value_self, query_cross, cosine, sine, ranges)


def stack_heads(source_ref, row, column, heads, target_ref):
    for block in range(target_ref.shape[0] // (heads * TBLOCK)):
        for head in range(heads):
            begin = (block * heads + head) * TBLOCK
            target_ref[begin : begin + TBLOCK, :] = source_ref[
                row + block * TBLOCK : row + (block + 1) * TBLOCK,
                column + head * HD : column + (head + 1) * HD,
            ]


def fold_keys(keys, values_turned, stacked_ref, peak_ref, total_ref, visible):
    scale = HD**-0.5 * log2e
    width = min(256, stacked_ref.shape[0])
    spans = [slice(begin, begin + width) for begin in range(0, stacked_ref.shape[0], width)]
    scores = [
        lax.dot_general(
            keys, stacked_ref[span, :], contract_last, preferred_element_type=jnp.float32
        )
        for span in spans
    ]
    for span, score in zip(spans, scores):
        peak = peak_ref[0:1, span]
        seen = visible[:, span]
        if seen.shape[0] == 1:
            highest = jnp.max(score, axis=0, keepdims=True) * scale
            new_peak = jnp.where(seen, jnp.maximum(peak, highest), peak)
            weights = jnp.exp2(score * scale - jnp.where(seen, new_peak, -unseen))
        else:
            score = jnp.where(seen, score * scale, unseen)
            new_peak = jnp.maximum(peak, jnp.max(score, axis=0, keepdims=True))
            weights = jnp.where(seen, jnp.exp2(score - new_peak), 0.0)
        total_ref[:, span] = total_ref[:, span] * jnp.exp2(peak - new_peak) + jnp.dot(
            values_turned, weights.astype(jnp.bfloat16), preferred_element_type=jnp.float32
        )
        peak_ref[0:1, span] = new_peak


def clear(peak_ref, total_ref):
    peak_ref[...] = jnp.full(peak_ref.shape, unseen, jnp.float32)
    total_ref[...] = jnp.zeros(total_ref.shape, jnp.float32)


def finish_columns(peak_ref, total_ref):
    sums = total_ref[HD : HD + 1, :]
    some = sums > 0.0
    safe = jnp.where(some, sums, 1.0)
    log_sum = jnp.where(some, peak_ref[0:1, :] + jnp.log2(safe), unseen)
    return total_ref[:HD, :] / safe, log_sum


def turn_values(value, target_ref):
    target_ref[:HD, :] = value.T
    target_ref[HD:, :] = jnp.ones((stat_rows, target_ref.shape[1]), jnp.bfloat16)


def frame_numbers(inner):
    device = lax.axis_index("ctx")
    plane, place = device // inner, lax.rem(device, inner)
    near = plane + 1 - 2 * lax.rem(plane, 2)
    return (
        plane * inner + place,
        plane * inner + 1 - place,
        near * inner + place,
        near * inner + 1 - place,
    )


def cross_kernel(inner, heads, groups, packed, table_ref, *refs):
    query_count = 1 + max(argument for _, argument, _ in groups)
    query_refs, frame_refs = refs[:query_count], refs[query_count : query_count + 4]
    out_refs, scratch = refs[query_count + 4 : -4], refs[-4:]
    turned_ref, stacked_ref, peak_ref, total_ref = scratch
    lanes = heads * TBLOCK
    blocks = stacked_ref.shape[0] // lanes
    frames = frame_numbers(inner)
    for index in range(4):
        turn_values(frame_refs[index][1], turned_ref.at[index])
    for slot, (number, argument, row) in enumerate(groups):
        stack_heads(query_refs[argument], row, 0, heads, stacked_ref)
        clear(peak_ref, total_ref)
        for index in range(4):
            flags = []
            for block in range(blocks):
                at = 2 * (number * blocks + block)
                inside = jnp.logical_and(
                    table_ref[at] <= frames[index], frames[index] < table_ref[at + 1]
                )
                flags.append(inside.astype(jnp.int32))

            @pl.when(functools.reduce(jnp.maximum, flags) > 0)
            def _():
                visible = jnp.concatenate(
                    [jnp.full((1, lanes), flag, jnp.int32) for flag in flags], axis=1
                )
                fold_keys(
                    frame_refs[index][0],
                    turned_ref[index],
                    stacked_ref,
                    peak_ref,
                    total_ref,
                    visible > 0,
                )

        mixed, log_sum = finish_columns(peak_ref, total_ref)
        for block in range(blocks):
            span = slice(block * lanes, (block + 1) * lanes)
            part, stat = mixed[:, span], log_sum[:, span]
            if packed:
                high = stat.astype(jnp.bfloat16)
                rest = stat - high.astype(jnp.float32)
                middle = rest.astype(jnp.bfloat16)
                low = (rest - middle.astype(jnp.float32)).astype(jnp.bfloat16)
                rows = [high, middle, low, jnp.zeros((stat_rows - 3, lanes), jnp.bfloat16)]
                out_refs[0][slot * blocks + block, :HD, :] = part.astype(jnp.bfloat16)
                out_refs[0][slot * blocks + block, HD:, :] = jnp.concatenate(rows, axis=0)
            else:
                out_refs[0][slot * blocks + block] = part
                out_refs[1][slot * blocks + block] = jnp.broadcast_to(stat, (8, lanes))


def cross_part(table, queries, frames, groups, rows, inner, heads, packed):
    lanes = heads * TBLOCK
    count = len(groups) * (rows // TBLOCK)
    if packed:
        out_shape = (jax.ShapeDtypeStruct((count, HD + stat_rows, lanes), jnp.bfloat16),)
    else:
        out_shape = (
            jax.ShapeDtypeStruct((count, HD, lanes), jnp.float32),
            jax.ShapeDtypeStruct((count, 8, lanes), jnp.float32),
        )
    return pl.pallas_call(
        functools.partial(cross_kernel, inner, heads, groups, packed),
        out_shape=out_shape,
        in_specs=[pl.BlockSpec(memory_space=pltpu.SMEM)] + whole(len(queries) + 4),
        out_specs=whole(len(out_shape)),
        scratch_shapes=[
            pltpu.VMEM((4, HD + stat_rows, frames[0].shape[1]), jnp.bfloat16),
            pltpu.VMEM((rows * heads, HD), jnp.bfloat16),
            pltpu.VMEM((8, rows * heads), jnp.float32),
            pltpu.VMEM((HD + stat_rows, rows * heads), jnp.float32),
        ],
        compiler_params=pltpu.CompilerParams(vmem_limit_bytes=40 * 2**20),
        name="cross_return" if packed else "cross_own",
    )(table, *queries, *frames)


def self_kernel(
    inner, heads, own_ref, partner_ref, far_ref, across_ref, near_ref, last_ref, out_ref, *scratch
):
    key_ref, turned_ref, stacked_ref, peak_ref, total_ref = scratch
    device = lax.axis_index("ctx")
    plane, place = device // inner, lax.rem(device, inner)
    rows = own_ref.shape[0]
    lanes = heads * TBLOCK
    group = heads * HD
    first = group + HD
    key_ref[:rows, :] = own_ref[:, first : first + HD]
    key_ref[rows : 2 * rows, :] = partner_ref[:, first : first + HD]
    key_ref[2 * rows : 4 * rows, :] = near_ref[:, :HD]
    key_ref[4 * rows : 5 * rows, :] = far_ref[:, first : first + HD]
    key_ref[5 * rows : 6 * rows, :] = across_ref[:, first : first + HD]
    key_ref[6 * rows :, :] = last_ref[:, :HD]
    values = jnp.concatenate(
        [
            own_ref[:, first + HD : first + 2 * HD],
            partner_ref[:, first + HD : first + 2 * HD],
            near_ref[:, HD:],
            far_ref[:, first + HD : first + 2 * HD],
            across_ref[:, first + HD : first + 2 * HD],
            last_ref[:, HD:],
        ],
        axis=0,
    )
    turn_values(values, turned_ref)
    keys = key_ref[...]
    planes = (
        plane,
        plane + 1 - 2 * lax.rem(plane, 2),
        lax.rem(plane + 2, 4),
        3 - plane,
    )
    starts = []
    for source in planes:
        starts.append((source * inner + place) * rows)
        starts.append((source * inner + 1 - place) * rows)
    down = lax.broadcasted_iota(jnp.int32, (rows, rows * heads), 0)
    key_index = jnp.concatenate([down + start for start in starts], axis=0)
    across = lax.broadcasted_iota(jnp.int32, key_index.shape, 1)
    token = (across // lanes) * TBLOCK + lax.rem(across, TBLOCK)
    for slot, query_ref in enumerate((own_ref, partner_ref)):
        side = place if slot == 0 else 1 - place
        stack_heads(query_ref, 0, group + 3 * HD, heads, stacked_ref)
        clear(peak_ref, total_ref)
        visible = key_index <= token + (plane * inner + side) * rows
        fold_keys(keys, turned_ref[...], stacked_ref, peak_ref, total_ref, visible)
        mixed, _ = finish_columns(peak_ref, total_ref)
        blocks = rows // TBLOCK
        for block in range(blocks):
            part = mixed[:, block * lanes : (block + 1) * lanes].T.astype(jnp.bfloat16)
            for head in range(heads):
                out_ref[block * inner + side, :, head * HD : (head + 1) * HD] = part[
                    head * TBLOCK : (head + 1) * TBLOCK
                ]


def self_part(own, partner, far, far_across, near, last, inner, heads):
    rows = own.shape[0]
    return pl.pallas_call(
        functools.partial(self_kernel, inner, heads),
        out_shape=jax.ShapeDtypeStruct((inner * rows // TBLOCK, TBLOCK, heads * HD), jnp.bfloat16),
        in_specs=whole(6),
        out_specs=whole(1)[0],
        scratch_shapes=[
            pltpu.VMEM((8 * rows, HD), jnp.bfloat16),
            pltpu.VMEM((HD + stat_rows, 8 * rows), jnp.bfloat16),
            pltpu.VMEM((rows * heads, HD), jnp.bfloat16),
            pltpu.VMEM((8, rows * heads), jnp.float32),
            pltpu.VMEM((HD + stat_rows, rows * heads), jnp.float32),
        ],
        compiler_params=pltpu.CompilerParams(vmem_limit_bytes=40 * 2**20),
        name="self_attention",
    )(own, partner, far, far_across, near, last)


def combine_kernel(inner, heads, gate_ref, mixed_ref, stat_ref, returned_ref, self_ref, out_ref):
    count = mixed_ref.shape[0]
    group = heads * HD
    side = count // inner
    place = lax.rem(lax.axis_index("ctx"), inner)
    gate = jnp.tanh(jnp.full((1, heads * TBLOCK), gate_ref[0], jnp.float32))
    for block in range(count):
        target = (block % side) * inner + (place if block < side else 1 - place)
        stats = returned_ref[block, HD:, :].astype(jnp.float32)
        far_stat = stats[0:1] + stats[1:2] + stats[2:3]
        own_stat = stat_ref[block, 0:1, :]
        peak = jnp.maximum(own_stat, far_stat)
        own_weight = jnp.exp2(own_stat - peak)
        far_weight = jnp.exp2(far_stat - peak)
        ratio = gate / (own_weight + far_weight)
        mixed = mixed_ref[block] * (own_weight * ratio) + returned_ref[block, :HD, :].astype(
            jnp.float32
        ) * (far_weight * ratio)
        part = mixed.T.astype(jnp.bfloat16)
        for head in range(heads):
            out_ref[target, :, head * HD : (head + 1) * HD] = part[
                head * TBLOCK : (head + 1) * TBLOCK
            ]
    out_ref[:, :, group:] = self_ref[...]


def combine(gate_scale, mixed, stat, returned, self_rows, inner, heads):
    count = mixed.shape[0]
    return pl.pallas_call(
        functools.partial(combine_kernel, inner, heads),
        out_shape=jax.ShapeDtypeStruct((count, TBLOCK, 2 * heads * HD), jnp.bfloat16),
        in_specs=[pl.BlockSpec(memory_space=pltpu.SMEM)] + whole(4),
        out_specs=whole(1)[0],
        name="combine_planes",
    )(gate_scale, mixed, stat, returned, self_rows)


def spread_kernel(in_ref, self_ref, cross_ref):
    group = in_ref.shape[2] // 2
    for head in range(in_ref.shape[0]):
        span = slice(head * group, (head + 1) * group)
        cross_ref[:, span] = in_ref[head, :, :group]
        self_ref[:, span] = in_ref[head, :, group:]


def spread(inward):
    count, rows, columns = inward.shape
    shape = jax.ShapeDtypeStruct((rows, count * columns // 2), inward.dtype)
    return pl.pallas_call(
        spread_kernel,
        out_shape=(shape, shape),
        in_specs=whole(1),
        out_specs=whole(2),
        name="spread_heads",
    )(inward)


def on_device_split(
    axes,
    query_self,
    key_self,
    value_self,
    positions,
    query_cross,
    key_vision,
    value_vision,
    media_range,
    gate_scale,
):
    inner = key_self.shape[1] // HD
    heads = query_self.shape[1] // key_self.shape[1]
    rows = query_self.shape[0]
    group = heads * HD
    columns = axes["head"]
    devices = axes["ctx"]
    plane_count = devices // inner

    def place_of(device):
        return device // inner, device % inner

    def send(values, turn, flip, upward=False):
        pairs = []
        for device in range(devices):
            plane, place = place_of(device)
            target = plane ^ turn
            if not upward or target > plane:
                pairs.append((device, target * inner + (place ^ flip)))
        return lax.ppermute(values, "ctx", pairs)

    kept_vision, other_vision = split_heads(key_vision, value_vision, inner)
    vision_across = send(other_vision, 1, 1)
    vision_near = send(kept_vision, 1, 0)
    vision_beside = send(other_vision, 0, 1)

    exponents = jnp.arange(HD // 2, dtype=jnp.float32) * (2.0 / HD)
    frequency = jnp.power(rope_base, -exponents)
    angles = positions.astype(jnp.float32)[:, None] * frequency[None, :]
    cosine, sine = jnp.cos(angles), jnp.sin(angles)
    ranges = jnp.repeat(media_range.astype(jnp.bfloat16), TBLOCK, axis=0)
    ranges = jnp.pad(ranges, ((0, 0), (0, HD - media_range.shape[1])))
    kept, other = pack_queries(
        query_self,
        key_self,
        value_self,
        query_cross,
        jnp.concatenate([cosine, cosine], axis=1),
        jnp.concatenate([-sine, sine], axis=1),
        ranges,
        inner,
    )
    partner = send(other, 0, 1)
    first = group + HD
    last = first + 2 * HD
    far = send(kept[:, :last], 2, 0)
    far_across = send(other[:, :last], 2, 1)
    sides = (kept, partner)
    packet = jnp.concatenate([side[:, first:last] for side in sides], axis=0)
    near_self = send(packet, 1, 0, upward=True)
    last_self = send(packet, 3, 0, upward=True)

    table = [side[::TBLOCK, group : group + 2] for side in (kept, partner, far, far_across)]
    table = jnp.concatenate(table).astype(jnp.int32).reshape(-1)
    frames = (kept_vision, vision_beside, vision_near, vision_across)
    (outgoing,) = cross_part(
        table, (far, far_across), frames, ((2, 0, 0), (3, 1, 0)), rows, inner, heads, True
    )
    returned = send(outgoing, 2, 0)
    mixed, stat = cross_part(
        table, (kept, partner), frames, ((0, 0, 0), (1, 1, 0)), rows, inner, heads, False
    )
    self_rows = self_part(kept, partner, far, far_across, near_self, last_self, inner, heads)
    outward = combine(gate_scale, mixed, stat, returned, self_rows, inner, heads)
    planes = [
        [
            (plane * inner + place) * columns + column
            for column in range(columns)
            for place in range(inner)
        ]
        for plane in range(plane_count)
    ]
    inward = lax.all_to_all(
        outward.reshape(-1, 2 * group),
        ("ctx", "head"),
        0,
        0,
        axis_index_groups=planes,
        tiled=True,
    )
    return spread(inward.reshape(outward.shape))


def on_device(axes, *arguments):
    query_self, key_self, _, _, _, key_vision, _, media_range, _ = arguments
    inner = key_self.shape[1] // HD
    heads = query_self.shape[1] // key_self.shape[1]
    rows = query_self.shape[0]
    suited = (
        inner == 2
        and axes["ctx"] == 4 * inner
        and heads * TBLOCK == HD
        and key_vision.shape[0] == FRAME_LEN
        and rows == axes["head"] * TBLOCK
        and media_range.shape[0] * TBLOCK == rows
    )
    if suited:
        return on_device_split(axes, *arguments)
    return on_device_gathered(*arguments)


def solution(mesh):
    placed = (
        P("ctx", "head"),
        P("ctx", "head"),
        P("ctx", "head"),
        P("ctx"),
        P("ctx", "head"),
        P("ctx", "head"),
        P("ctx", "head"),
        P("ctx", None),
        P(),
    )
    return jax.shard_map(
        functools.partial(on_device, dict(mesh.shape)),
        mesh=mesh,
        in_specs=placed,
        out_specs=(P(("ctx", "head"), None), P(("ctx", "head"), None)),
        check_vma=False,
    )
```

```python
import functools

import jax
import jax.numpy as jnp
from jax import lax
from jax.experimental import pallas as pl
from jax.experimental.pallas import tpu as pltpu
from jax.sharding import PartitionSpec as P

HD = 128
TBLOCK = 16
FRAME_LEN = 896


rope_base = 500000.0
lowest = -1e30


def rotate(values, positions):
    half_width = values.shape[-1] // 2
    exponents = jnp.arange(half_width, dtype=jnp.float32) * (2.0 / values.shape[-1])
    frequency = jnp.power(rope_base, -exponents)
    angles = positions.astype(jnp.float32)[:, None] * frequency[None, :]
    cosine = jnp.cos(angles)[:, None, :]
    sine_part = jnp.sin(angles)[:, None, :]
    first_half = values[..., :half_width]
    second_half = values[..., half_width:]
    return jnp.concatenate(
        [
            first_half * cosine - second_half * sine_part,
            second_half * cosine + first_half * sine_part,
        ],
        axis=-1,
    )


def key_block(key_count):
    block_size = min(key_count, 1024)
    while key_count % block_size != 0:
        block_size = block_size - 1
    return block_size


def attend_block(state_in, queries, key_rows, value_rows, allowed):
    maxima, totals, accumulated = state_in
    scale_factor = queries.shape[-1] ** (-0.5)
    scores = (
        jnp.einsum("rkgd,nkd->kgrn", queries, key_rows, preferred_element_type=jnp.float32)
        * scale_factor
    )
    visible = allowed[None, None, :, :]
    scores = jnp.where(visible, scores, lowest)
    new_maxima = jnp.maximum(maxima, jnp.max(scores, axis=-1))
    weights = jnp.where(visible, jnp.exp(scores - new_maxima[..., None]), 0.0)
    factor = jnp.exp(maxima - new_maxima)
    totals = totals * factor + jnp.sum(weights, axis=-1)
    accumulated = accumulated * factor[..., None] + jnp.einsum(
        "kgrn,nkd->kgrd",
        weights.astype(jnp.bfloat16),
        value_rows,
        preferred_element_type=jnp.float32,
    )
    return (new_maxima, totals, accumulated)


def attend(state_in, queries, key_rows, value_rows, allowed):
    key_count = key_rows.shape[0]
    block_size = key_block(key_count)
    if block_size == key_count:
        return attend_block(state_in, queries, key_rows, value_rows, allowed)

    def step_block(block_index, state_now):
        row_begin = block_index * block_size
        key_part = lax.dynamic_slice_in_dim(key_rows, row_begin, block_size, 0)
        value_part = lax.dynamic_slice_in_dim(value_rows, row_begin, block_size, 0)
        allowed_part = lax.dynamic_slice_in_dim(allowed, row_begin, block_size, 1)
        return attend_block(state_now, queries, key_part, value_part, allowed_part)

    return lax.fori_loop(0, key_count // block_size, step_block, state_in)


def keep_state(current):
    return current


def empty_state(row_count, kv_heads, group_size, head_size):
    maxima = jnp.full((kv_heads, group_size, row_count), lowest, jnp.float32)
    totals = jnp.zeros((kv_heads, group_size, row_count), jnp.float32)
    accumulated = jnp.zeros((kv_heads, group_size, row_count, head_size), jnp.float32)
    return (maxima, totals, accumulated)


def finish(state_in):
    maxima, totals, accumulated = state_in
    safe_totals = jnp.where(totals > 0.0, totals, 1.0)
    result = accumulated / safe_totals[..., None]
    kv_heads, group_size, row_count, head_size = result.shape
    return jnp.transpose(result, (2, 0, 1, 3)).reshape(row_count, kv_heads * group_size * head_size)


def causal_group(current, group, key_rows, value_rows, key_index, offset):
    queries, row_index = group
    allowed = key_index[None, :] <= row_index[:, None]

    def causal_compute(state_in):
        return attend(state_in, queries, key_rows, value_rows, allowed)

    return lax.cond(offset <= jnp.max(row_index), causal_compute, keep_state, current)


def frame_mask(frame_index, lower_frame, upper_frame):
    return jnp.logical_and(
        frame_index[None, :] >= lower_frame[:, None], frame_index[None, :] < upper_frame[:, None]
    )


def on_device_gathered(
    query_self,
    key_self,
    value_self,
    positions,
    query_cross,
    key_vision,
    value_vision,
    media_range,
    gate_scale,
):
    head_size = HD
    kv_heads = key_self.shape[1] // head_size
    group_size = query_self.shape[1] // key_self.shape[1]
    row_count = query_self.shape[0]
    vision_count = key_vision.shape[0]
    device = lax.axis_index("ctx")
    own_rows = device * row_count + jnp.arange(row_count, dtype=jnp.int32)
    rotated_query = rotate(
        query_self.astype(jnp.float32).reshape(row_count, kv_heads * group_size, head_size),
        positions,
    )
    rotated_query = rotated_query.astype(jnp.bfloat16).reshape(
        row_count, kv_heads, group_size, head_size
    )
    rotated_key = rotate(
        key_self.astype(jnp.float32).reshape(row_count, kv_heads, head_size), positions
    ).astype(jnp.bfloat16)
    self_values = value_self.reshape(row_count, kv_heads, head_size)
    vision_keys = key_vision.reshape(vision_count, kv_heads, head_size)
    vision_values = value_vision.reshape(vision_count, kv_heads, head_size)
    cross_queries = query_cross.reshape(row_count, kv_heads, group_size, head_size)
    lower_frame = jnp.repeat(media_range[:, 0], TBLOCK)
    upper_frame = jnp.repeat(media_range[:, 1], TBLOCK)
    has_frames = upper_frame > lower_frame
    query_groups = ((rotated_query, own_rows),)
    self_start = tuple(
        (empty_state(group[1].shape[0], kv_heads, group_size, head_size) for group in query_groups)
    )
    cross_start = empty_state(row_count, kv_heads, group_size, head_size)
    offset = jnp.int32(0)
    key_rows = lax.all_gather(rotated_key, "ctx", axis=0, tiled=True)
    value_rows = lax.all_gather(self_values, "ctx", axis=0, tiled=True)
    key_index = jnp.arange(key_rows.shape[0], dtype=jnp.int32)
    updated = []
    for current, group in zip(self_start, query_groups):
        updated.append(causal_group(current, group, key_rows, value_rows, key_index, offset))
    self_states = tuple(updated)
    key_rows = lax.all_gather(vision_keys, "ctx", axis=0, tiled=True)
    value_rows = lax.all_gather(vision_values, "ctx", axis=0, tiled=True)
    frame_index = jnp.arange(key_rows.shape[0], dtype=jnp.int32) // FRAME_LEN
    allowed = frame_mask(frame_index, lower_frame, upper_frame)
    touching = jnp.logical_and(lower_frame <= frame_index[-1], upper_frame > frame_index[0])
    needed = jnp.any(jnp.logical_and(has_frames, touching))

    def fold_compute(state_in):
        return attend(state_in, cross_queries, key_rows, value_rows, allowed)

    cross_state = lax.cond(needed, fold_compute, keep_state, cross_start)
    self_rows = finish(self_states[0]).astype(jnp.bfloat16)
    cross_rows = jnp.where(
        has_frames[:, None], jnp.tanh(gate_scale[0]) * finish(cross_state), 0.0
    ).astype(jnp.bfloat16)
    self_context, cross_context = (
        lax.all_to_all(self_rows, "head", split_axis=0, concat_axis=1, tiled=True),
        lax.all_to_all(cross_rows, "head", split_axis=0, concat_axis=1, tiled=True),
    )
    return (self_context, cross_context)


log2e = 1.4426950408889634
stat_rows = 16
unseen = -1e30
contract_last = (((1,), (1,)), ((), ()))


def whole(count):
    return [pl.BlockSpec(memory_space=pltpu.VMEM)] * count


def prepare_kernel(
    inner,
    range_ref,
    cosine_ref,
    sine_ref,
    vision_key_ref,
    vision_value_ref,
    cross_ref,
    query_ref,
    key_ref,
    value_ref,
    near_ref,
    across_ref,
    beside_ref,
    own_ref,
    other_ref,
    own_self_ref,
    cross_rows,
    query_rows,
    key_rows,
    value_rows,
    semaphores,
):
    rows = query_rows.shape[0]
    heads = query_rows.shape[1] // inner // HD
    vision = vision_key_ref.shape[0]
    place = lax.rem(lax.axis_index("ctx"), inner)
    sides = (place, 1 - place)

    def head_columns(head):
        return pl.ds(pl.multiple_of(head * HD, HD), HD)

    copies = []
    for source, target in (
        (cross_ref, cross_rows),
        (key_ref, key_rows),
        (value_ref, value_rows),
        (query_ref, query_rows),
    ):
        copies.append(pltpu.make_async_copy(source, target, semaphores.at[len(copies)]))
    for target, head in ((near_ref, sides[0]), (across_ref, sides[1]), (beside_ref, sides[1])):
        for slot, source in enumerate((vision_key_ref, vision_value_ref)):
            copies.append(
                pltpu.make_async_copy(
                    source.at[:, head_columns(head)],
                    target.at[pl.ds(slot * vision, vision), :],
                    semaphores.at[len(copies)],
                )
            )
    for copy in copies:
        copy.start()
    cosine = jnp.concatenate([cosine_ref[...]] * 2, axis=1)
    sine = jnp.concatenate([-sine_ref[...], sine_ref[...]], axis=1)

    def turned(block):
        block = block.astype(jnp.float32)
        return (block * cosine + pltpu.roll(block, HD // 2, 1) * sine).astype(jnp.bfloat16)

    lane = lax.broadcasted_iota(jnp.int32, (TBLOCK, HD), 1)
    ranges = jnp.zeros((TBLOCK, HD), jnp.int32)
    for item in range(2 * rows // TBLOCK):
        ranges = jnp.where(lane == item, range_ref[item], ranges)
    ranges = ranges.astype(jnp.float32).astype(jnp.bfloat16)
    stacked = heads * rows

    def stack(target, begin, head, block):
        for step in range(rows // TBLOCK):
            row = begin + (step * heads + head) * TBLOCK
            target[row : row + TBLOCK, :] = block[step * TBLOCK : (step + 1) * TBLOCK]

    for copy in copies[:4]:
        copy.wait()
    for side, target in enumerate((own_ref, other_ref)):
        for head in range(heads):
            stack(target, 0, head, cross_rows[:, head_columns(sides[side] * heads + head)])
        target[stacked : stacked + rows, :] = turned(key_rows[:, head_columns(sides[side])])
        target[stacked + rows : stacked + 2 * rows, :] = value_rows[:, head_columns(sides[side])]
        target[stacked + 2 * rows :, :] = ranges
    for side, (target, begin) in enumerate(((own_self_ref, 0), (beside_ref, 2 * vision))):
        for head in range(heads):
            stack(
                target,
                begin,
                head,
                turned(query_rows[:, head_columns(sides[side] * heads + head)]),
            )
    near_ref[2 * vision :, :] = own_ref[stacked : stacked + 2 * rows, :]
    across_ref[2 * vision :, :] = other_ref[stacked : stacked + 2 * rows, :]
    for copy in copies[4:]:
        copy.wait()


def prepare(ranges, cosine, sine, vision_keys, vision_values, cross, query, key, value, inner):
    rows, columns = query.shape
    stacked = rows * (columns // inner // HD)
    vision = vision_keys.shape[0]
    counts = [2 * vision + 2 * rows] * 2 + [2 * vision + stacked]
    counts += [stacked + 2 * rows + TBLOCK] * 2 + [stacked]
    return pl.pallas_call(
        functools.partial(prepare_kernel, inner),
        out_shape=[jax.ShapeDtypeStruct((count, HD), jnp.bfloat16) for count in counts],
        in_specs=[pl.BlockSpec(memory_space=pltpu.SMEM)]
        + whole(2)
        + [pl.BlockSpec(memory_space=pltpu.HBM)] * 6,
        out_specs=whole(6),
        scratch_shapes=[
            pltpu.VMEM(cross.shape, jnp.bfloat16),
            pltpu.VMEM(query.shape, jnp.bfloat16),
            pltpu.VMEM(key.shape, jnp.bfloat16),
            pltpu.VMEM(value.shape, jnp.bfloat16),
            pltpu.SemaphoreType.DMA((10,)),
        ],
        compiler_params=pltpu.CompilerParams(vmem_limit_bytes=60 * 2**20),
        name="prepare_packets",
    )(ranges.reshape(-1), cosine, sine, vision_keys, vision_values, cross, query, key, value)


def fold_keys(keys, values_turned, stacked_ref, peak_ref, total_ref, visible):
    scale = HD**-0.5 * log2e
    width = min(256, stacked_ref.shape[0])
    spans = [slice(begin, begin + width) for begin in range(0, stacked_ref.shape[0], width)]
    scores = [
        lax.dot_general(
            keys, stacked_ref[span, :], contract_last, preferred_element_type=jnp.float32
        )
        for span in spans
    ]
    for span, score in zip(spans, scores):
        peak = peak_ref[0:1, span]
        seen = visible[:, span]
        if seen.shape[0] == 1:
            highest = jnp.max(score, axis=0, keepdims=True) * scale
            new_peak = jnp.where(seen, jnp.maximum(peak, highest), peak)
            weights = jnp.exp2(score * scale - jnp.where(seen, new_peak, -unseen))
        else:
            score = jnp.where(seen, score * scale, unseen)
            new_peak = jnp.maximum(peak, jnp.max(score, axis=0, keepdims=True))
            weights = jnp.where(seen, jnp.exp2(score - new_peak), 0.0)
        total_ref[:, span] = total_ref[:, span] * jnp.exp2(peak - new_peak) + jnp.dot(
            values_turned, weights.astype(jnp.bfloat16), preferred_element_type=jnp.float32
        )
        peak_ref[0:1, span] = new_peak


def clear(peak_ref, total_ref):
    peak_ref[...] = jnp.full(peak_ref.shape, unseen, jnp.float32)
    total_ref[...] = jnp.zeros(total_ref.shape, jnp.float32)


def finish_columns(peak_ref, total_ref):
    sums = total_ref[HD : HD + 1, :]
    some = sums > 0.0
    safe = jnp.where(some, sums, 1.0)
    log_sum = jnp.where(some, peak_ref[0:1, :] + jnp.log2(safe), unseen)
    return total_ref[:HD, :] / safe, log_sum


def turn_values(value, target_ref):
    target_ref[:HD, :] = value.T
    target_ref[HD:, :] = jnp.ones((stat_rows, target_ref.shape[1]), jnp.bfloat16)


def frame_numbers(inner):
    device = lax.axis_index("ctx")
    plane, place = device // inner, lax.rem(device, inner)
    near = plane + 1 - 2 * lax.rem(plane, 2)
    return (
        plane * inner + place,
        plane * inner + 1 - place,
        near * inner + place,
        near * inner + 1 - place,
    )


def cross_kernel(inner, heads, columns, groups, chosen, resumed, finish, table_ref, *refs):
    refs = list(refs)
    query_refs = [refs.pop(0) for _ in groups]
    frame_refs = [refs.pop(0) for _ in chosen]
    state_refs = [refs.pop(0) for _ in range(2)] if resumed else None
    out_refs, (turned_ref, peaks_ref, totals_ref) = refs[:-3], refs[-3:]
    lanes = heads * TBLOCK
    blocks = columns // lanes
    frames = frame_numbers(inner)
    vision = turned_ref.shape[2]
    for slot in range(len(chosen)):
        turn_values(frame_refs[slot][vision : 2 * vision, :], turned_ref.at[slot])
    for turn, number in enumerate(groups):
        if finish == "state":
            peak_ref, total_ref = out_refs[0].at[turn], out_refs[1].at[turn]
        else:
            peak_ref, total_ref = peaks_ref, totals_ref
        if resumed:
            peak_ref[...] = state_refs[0][number]
            total_ref[...] = state_refs[1][number]
        else:
            clear(peak_ref, total_ref)
        for slot, index in enumerate(chosen):
            flags = []
            for block in range(blocks):
                at = 2 * (number * blocks + block)
                inside = jnp.logical_and(
                    table_ref[at] <= frames[index], frames[index] < table_ref[at + 1]
                )
                flags.append(inside.astype(jnp.int32))

            @pl.when(functools.reduce(jnp.maximum, flags) > 0)
            def _():
                visible = jnp.concatenate(
                    [jnp.full((1, lanes), flag, jnp.int32) for flag in flags], axis=1
                )
                fold_keys(
                    frame_refs[slot][:vision, :],
                    turned_ref[slot],
                    query_refs[turn].at[:columns, :],
                    peak_ref,
                    total_ref,
                    visible > 0,
                )

        if finish == "state":
            continue
        mixed, log_sum = finish_columns(peak_ref, total_ref)
        for block in range(blocks):
            span = slice(block * lanes, (block + 1) * lanes)
            part, stat = mixed[:, span], log_sum[:, span]
            if finish == "packed":
                high = stat.astype(jnp.bfloat16)
                rest = stat - high.astype(jnp.float32)
                middle = rest.astype(jnp.bfloat16)
                low = (rest - middle.astype(jnp.float32)).astype(jnp.bfloat16)
                rows = [high, middle, low, jnp.zeros((stat_rows - 3, lanes), jnp.bfloat16)]
                out_refs[0][turn * blocks + block, :HD, :] = part.astype(jnp.bfloat16)
                out_refs[0][turn * blocks + block, HD:, :] = jnp.concatenate(rows, axis=0)
            else:
                out_refs[0][turn * blocks + block] = part
                out_refs[1][turn * blocks + block] = jnp.broadcast_to(stat, (8, lanes))


def cross_part(table, queries, frames, chosen, groups, state, finish, rows, inner, heads):
    lanes = heads * TBLOCK
    columns = rows * heads
    vision = FRAME_LEN
    count = len(groups) * (rows // TBLOCK)
    if finish == "state":
        out_shape = (
            jax.ShapeDtypeStruct((len(groups), 8, columns), jnp.float32),
            jax.ShapeDtypeStruct((len(groups), HD + stat_rows, columns), jnp.float32),
        )
    elif finish == "packed":
        out_shape = (jax.ShapeDtypeStruct((count, HD + stat_rows, lanes), jnp.bfloat16),)
    else:
        out_shape = (
            jax.ShapeDtypeStruct((count, HD, lanes), jnp.float32),
            jax.ShapeDtypeStruct((count, 8, lanes), jnp.float32),
        )
    arguments = [*(queries[number] for number in groups), *(frames[index] for index in chosen), *state]
    return pl.pallas_call(
        functools.partial(
            cross_kernel, inner, heads, columns, groups, chosen, len(state) > 0, finish
        ),
        out_shape=out_shape,
        in_specs=[pl.BlockSpec(memory_space=pltpu.SMEM)] + whole(len(arguments)),
        out_specs=whole(len(out_shape)),
        scratch_shapes=[
            pltpu.VMEM((len(chosen), HD + stat_rows, vision), jnp.bfloat16),
            pltpu.VMEM((8, columns), jnp.float32),
            pltpu.VMEM((HD + stat_rows, columns), jnp.float32),
        ],
        compiler_params=pltpu.CompilerParams(vmem_limit_bytes=24 * 2**20),
        name="cross_" + finish,
    )(table, *arguments)


def self_kernel(inner, heads, rows, own_ref, beside_ref, *refs):
    key_value_refs, out_ref = refs[:7], refs[7]
    key_ref, value_ref, turned_ref, peak_ref, total_ref = refs[8:]
    device = lax.axis_index("ctx")
    plane, place = device // inner, lax.rem(device, inner)
    lanes = heads * TBLOCK
    columns = rows * heads
    vision = beside_ref.shape[0] - columns
    tails = [(ref, ref.shape[0] - TBLOCK - 2 * rows) for ref in key_value_refs[:2]]
    tails += [(ref, ref.shape[0] - 2 * rows) for ref in key_value_refs[2:4]]
    tails += [(ref, ref.shape[0] - TBLOCK - 2 * rows) for ref in key_value_refs[4:6]]
    tails += [(key_value_refs[6], 0), (key_value_refs[6], 2 * rows)]
    for slot, (ref, begin) in enumerate(tails):
        span = slice(slot * rows, (slot + 1) * rows)
        key_ref[span, :] = ref[begin : begin + rows, :]
        value_ref[span, :] = ref[begin + rows : begin + 2 * rows, :]
    turn_values(value_ref[...], turned_ref)
    planes = (plane, plane + 1 - 2 * lax.rem(plane, 2), lax.rem(plane + 2, 4), 3 - plane)
    starts = []
    for source in planes:
        starts.append((source * inner + place) * rows)
        starts.append((source * inner + 1 - place) * rows)
    down = lax.broadcasted_iota(jnp.int32, (rows, columns), 0)
    key_index = jnp.concatenate([down + start for start in starts], axis=0)
    across = lax.broadcasted_iota(jnp.int32, key_index.shape, 1)
    token = (across // lanes) * TBLOCK + lax.rem(across, TBLOCK)
    queries = (own_ref, beside_ref.at[pl.ds(vision, columns), :])
    for slot, query_ref in enumerate(queries):
        side = place if slot == 0 else 1 - place
        clear(peak_ref, total_ref)
        visible = key_index <= token + (plane * inner + side) * rows
        fold_keys(key_ref[...], turned_ref[...], query_ref, peak_ref, total_ref, visible)
        mixed, _ = finish_columns(peak_ref, total_ref)
        for block in range(rows // TBLOCK):
            part = mixed[:, block * lanes : (block + 1) * lanes].T.astype(jnp.bfloat16)
            for head in range(heads):
                out_ref[block * inner + side, :, head * HD : (head + 1) * HD] = part[
                    head * TBLOCK : (head + 1) * TBLOCK
                ]


def self_part(own, beside, key_values, rows, inner, heads):
    return pl.pallas_call(
        functools.partial(self_kernel, inner, heads, rows),
        out_shape=jax.ShapeDtypeStruct((inner * rows // TBLOCK, TBLOCK, heads * HD), jnp.bfloat16),
        in_specs=whole(2 + len(key_values)),
        out_specs=whole(1)[0],
        scratch_shapes=[
            pltpu.VMEM((8 * rows, HD), jnp.bfloat16),
            pltpu.VMEM((8 * rows, HD), jnp.bfloat16),
            pltpu.VMEM((HD + stat_rows, 8 * rows), jnp.bfloat16),
            pltpu.VMEM((8, rows * heads), jnp.float32),
            pltpu.VMEM((HD + stat_rows, rows * heads), jnp.float32),
        ],
        compiler_params=pltpu.CompilerParams(vmem_limit_bytes=24 * 2**20),
        name="self_attention",
    )(own, beside, *key_values)


def combine_kernel(inner, heads, gate_ref, mixed_ref, stat_ref, returned_ref, out_ref):
    count = mixed_ref.shape[0]
    side = count // inner
    place = lax.rem(lax.axis_index("ctx"), inner)
    gate = jnp.tanh(jnp.full((1, heads * TBLOCK), gate_ref[0], jnp.float32))
    for block in range(count):
        target = (block % side) * inner + (place if block < side else 1 - place)
        stats = returned_ref[block, HD:, :].astype(jnp.float32)
        far_stat = stats[0:1] + stats[1:2] + stats[2:3]
        own_stat = stat_ref[block, 0:1, :]
        peak = jnp.maximum(own_stat, far_stat)
        own_weight = jnp.exp2(own_stat - peak)
        far_weight = jnp.exp2(far_stat - peak)
        ratio = gate / (own_weight + far_weight)
        mixed = mixed_ref[block] * (own_weight * ratio) + returned_ref[block, :HD, :].astype(
            jnp.float32
        ) * (far_weight * ratio)
        part = mixed.T.astype(jnp.bfloat16)
        for head in range(heads):
            out_ref[target, :, head * HD : (head + 1) * HD] = part[
                head * TBLOCK : (head + 1) * TBLOCK
            ]


def combine(gate_scale, mixed, stat, returned, inner, heads):
    count = mixed.shape[0]
    return pl.pallas_call(
        functools.partial(combine_kernel, inner, heads),
        out_shape=jax.ShapeDtypeStruct((count, TBLOCK, heads * HD), jnp.bfloat16),
        in_specs=[pl.BlockSpec(memory_space=pltpu.SMEM)] + whole(3),
        out_specs=whole(1)[0],
        compiler_params=pltpu.CompilerParams(vmem_limit_bytes=16 * 2**20),
        name="combine_planes",
    )(gate_scale, mixed, stat, returned)


def spread_kernel(in_ref, out_ref):
    group = in_ref.shape[2]
    for head in range(in_ref.shape[0]):
        out_ref[:, head * group : (head + 1) * group] = in_ref[head]


def spread(inward):
    count, rows, columns = inward.shape
    return pl.pallas_call(
        spread_kernel,
        out_shape=jax.ShapeDtypeStruct((rows, count * columns), inward.dtype),
        in_specs=whole(1),
        out_specs=whole(1)[0],
        compiler_params=pltpu.CompilerParams(vmem_limit_bytes=16 * 2**20),
        name="spread_heads",
    )(inward)


def on_device_split(
    axes,
    query_self,
    key_self,
    value_self,
    positions,
    query_cross,
    key_vision,
    value_vision,
    media_range,
    gate_scale,
):
    inner = key_self.shape[1] // HD
    heads = query_self.shape[1] // key_self.shape[1]
    rows = query_self.shape[0]
    group = heads * HD
    columns = axes["head"]
    devices = axes["ctx"]
    plane_count = devices // inner

    def place_of(device):
        return device // inner, device % inner

    def send(values, turn, flip, upward=False):
        pairs = []
        for device in range(devices):
            plane, place = place_of(device)
            target = plane ^ turn
            if not upward or target > plane:
                pairs.append((device, target * inner + (place ^ flip)))
        return lax.ppermute(values, "ctx", pairs)

    exponents = jnp.arange(HD // 2, dtype=jnp.float32) * (2.0 / HD)
    frequency = jnp.power(rope_base, -exponents)
    angles = positions.astype(jnp.float32)[:, None] * frequency[None, :]
    near_out, across_out, beside_out, own, other, own_self = prepare(
        media_range,
        jnp.cos(angles),
        jnp.sin(angles),
        key_vision,
        value_vision,
        query_cross,
        query_self,
        key_self,
        value_self,
        inner,
    )
    partner = send(other, 0, 1)
    far = send(own, 2, 0)
    near = send(near_out, 1, 0)
    beside_out, across_out, partner = lax.optimization_barrier((beside_out, across_out, partner))
    far_across = send(partner, 2, 0)
    across = send(across_out, 1, 1)
    beside = send(beside_out, 0, 1)
    tail = slice(rows * heads, rows * heads + 2 * rows)
    last = send(jnp.concatenate([far[tail], far_across[tail]], axis=0), 1, 0)

    queries = (own, partner, far, far_across)
    table = [values[-TBLOCK, : 2 * (rows // TBLOCK)] for values in queries]
    table = jnp.concatenate(table).astype(jnp.int32)
    frames = (near_out, beside, near, across)
    sizes = (rows, inner, heads)
    everyone = (0, 1, 2, 3)
    state = cross_part(table, queries, frames, (0, 2), everyone, (), "state", *sizes)
    state = cross_part(table, queries, frames, (3,), everyone, state, "state", *sizes)
    state, last = lax.optimization_barrier((state, last))
    (outgoing,) = cross_part(table, queries, frames, (1,), (2, 3), state, "packed", *sizes)
    returned = send(outgoing, 2, 0)
    outgoing, table, own_self = lax.optimization_barrier((outgoing, table, own_self))
    mixed, stat = cross_part(table, queries, frames, (1,), (0, 1), state, "own", *sizes)
    self_rows = self_part(
        own_self, beside, (own, partner, near, across, far, far_across, last), *sizes
    )
    planes = [
        [
            (plane * inner + place) * columns + column
            for column in range(columns)
            for place in range(inner)
        ]
        for plane in range(plane_count)
    ]

    def exchange(outward):
        inward = lax.all_to_all(
            outward.reshape(-1, outward.shape[2]),
            ("ctx", "head"),
            0,
            0,
            axis_index_groups=planes,
            tiled=True,
        )
        return spread(inward.reshape(outward.shape))

    self_context = exchange(self_rows)
    cross_context = exchange(combine(gate_scale, mixed, stat, returned, inner, heads))
    return self_context, cross_context


def on_device(axes, *arguments):
    query_self, key_self, _, _, _, key_vision, _, media_range, _ = arguments
    inner = key_self.shape[1] // HD
    heads = query_self.shape[1] // key_self.shape[1]
    rows = query_self.shape[0]
    suited = (
        inner == 2
        and axes["ctx"] == 4 * inner
        and heads * TBLOCK == HD
        and key_vision.shape[0] == FRAME_LEN
        and rows == axes["head"] * TBLOCK
        and media_range.shape[0] * TBLOCK == rows
    )
    if suited:
        return on_device_split(axes, *arguments)
    return on_device_gathered(*arguments)


def solution(mesh):
    placed = (
        P("ctx", "head"),
        P("ctx", "head"),
        P("ctx", "head"),
        P("ctx"),
        P("ctx", "head"),
        P("ctx", "head"),
        P("ctx", "head"),
        P("ctx", None),
        P(),
    )
    return jax.shard_map(
        functools.partial(on_device, dict(mesh.shape)),
        mesh=mesh,
        in_specs=placed,
        out_specs=(P(("ctx", "head"), None), P(("ctx", "head"), None)),
        check_vma=False,
    )
```

```python
import functools

import jax
import jax.numpy as jnp
import numpy as np
from jax import lax
from jax.experimental import pallas as pl
from jax.experimental.pallas import tpu as pltpu
from jax.sharding import PartitionSpec as P

HD = 128
TBLOCK = 16
FRAME_LEN = 896


rope_base = 500000.0
lowest = -1e30


def rotate(values, positions):
    half_width = values.shape[-1] // 2
    exponents = jnp.arange(half_width, dtype=jnp.float32) * (2.0 / values.shape[-1])
    frequency = jnp.power(rope_base, -exponents)
    angles = positions.astype(jnp.float32)[:, None] * frequency[None, :]
    cosine = jnp.cos(angles)[:, None, :]
    sine_part = jnp.sin(angles)[:, None, :]
    first_half = values[..., :half_width]
    second_half = values[..., half_width:]
    return jnp.concatenate(
        [
            first_half * cosine - second_half * sine_part,
            second_half * cosine + first_half * sine_part,
        ],
        axis=-1,
    )


def key_block(key_count):
    block_size = min(key_count, 1024)
    while key_count % block_size != 0:
        block_size = block_size - 1
    return block_size


def attend_block(state_in, queries, key_rows, value_rows, allowed):
    maxima, totals, accumulated = state_in
    scale_factor = queries.shape[-1] ** (-0.5)
    scores = (
        jnp.einsum("rkgd,nkd->kgrn", queries, key_rows, preferred_element_type=jnp.float32)
        * scale_factor
    )
    visible = allowed[None, None, :, :]
    scores = jnp.where(visible, scores, lowest)
    new_maxima = jnp.maximum(maxima, jnp.max(scores, axis=-1))
    weights = jnp.where(visible, jnp.exp(scores - new_maxima[..., None]), 0.0)
    factor = jnp.exp(maxima - new_maxima)
    totals = totals * factor + jnp.sum(weights, axis=-1)
    accumulated = accumulated * factor[..., None] + jnp.einsum(
        "kgrn,nkd->kgrd",
        weights.astype(jnp.bfloat16),
        value_rows,
        preferred_element_type=jnp.float32,
    )
    return (new_maxima, totals, accumulated)


def attend(state_in, queries, key_rows, value_rows, allowed):
    key_count = key_rows.shape[0]
    block_size = key_block(key_count)
    if block_size == key_count:
        return attend_block(state_in, queries, key_rows, value_rows, allowed)

    def step_block(block_index, state_now):
        row_begin = block_index * block_size
        key_part = lax.dynamic_slice_in_dim(key_rows, row_begin, block_size, 0)
        value_part = lax.dynamic_slice_in_dim(value_rows, row_begin, block_size, 0)
        allowed_part = lax.dynamic_slice_in_dim(allowed, row_begin, block_size, 1)
        return attend_block(state_now, queries, key_part, value_part, allowed_part)

    return lax.fori_loop(0, key_count // block_size, step_block, state_in)


def keep_state(current):
    return current


def empty_state(row_count, kv_heads, group_size, head_size):
    maxima = jnp.full((kv_heads, group_size, row_count), lowest, jnp.float32)
    totals = jnp.zeros((kv_heads, group_size, row_count), jnp.float32)
    accumulated = jnp.zeros((kv_heads, group_size, row_count, head_size), jnp.float32)
    return (maxima, totals, accumulated)


def finish(state_in):
    maxima, totals, accumulated = state_in
    safe_totals = jnp.where(totals > 0.0, totals, 1.0)
    result = accumulated / safe_totals[..., None]
    kv_heads, group_size, row_count, head_size = result.shape
    return jnp.transpose(result, (2, 0, 1, 3)).reshape(row_count, kv_heads * group_size * head_size)


def causal_group(current, group, key_rows, value_rows, key_index, offset):
    queries, row_index = group
    allowed = key_index[None, :] <= row_index[:, None]

    def causal_compute(state_in):
        return attend(state_in, queries, key_rows, value_rows, allowed)

    return lax.cond(offset <= jnp.max(row_index), causal_compute, keep_state, current)


def frame_mask(frame_index, lower_frame, upper_frame):
    return jnp.logical_and(
        frame_index[None, :] >= lower_frame[:, None], frame_index[None, :] < upper_frame[:, None]
    )


def on_device_gathered(
    query_self,
    key_self,
    value_self,
    positions,
    query_cross,
    key_vision,
    value_vision,
    media_range,
    gate_scale,
):
    head_size = HD
    kv_heads = key_self.shape[1] // head_size
    group_size = query_self.shape[1] // key_self.shape[1]
    row_count = query_self.shape[0]
    vision_count = key_vision.shape[0]
    device = lax.axis_index("ctx")
    own_rows = device * row_count + jnp.arange(row_count, dtype=jnp.int32)
    rotated_query = rotate(
        query_self.astype(jnp.float32).reshape(row_count, kv_heads * group_size, head_size),
        positions,
    )
    rotated_query = rotated_query.astype(jnp.bfloat16).reshape(
        row_count, kv_heads, group_size, head_size
    )
    rotated_key = rotate(
        key_self.astype(jnp.float32).reshape(row_count, kv_heads, head_size), positions
    ).astype(jnp.bfloat16)
    self_values = value_self.reshape(row_count, kv_heads, head_size)
    vision_keys = key_vision.reshape(vision_count, kv_heads, head_size)
    vision_values = value_vision.reshape(vision_count, kv_heads, head_size)
    cross_queries = query_cross.reshape(row_count, kv_heads, group_size, head_size)
    lower_frame = jnp.repeat(media_range[:, 0], TBLOCK)
    upper_frame = jnp.repeat(media_range[:, 1], TBLOCK)
    has_frames = upper_frame > lower_frame
    query_groups = ((rotated_query, own_rows),)
    self_start = tuple(
        (empty_state(group[1].shape[0], kv_heads, group_size, head_size) for group in query_groups)
    )
    cross_start = empty_state(row_count, kv_heads, group_size, head_size)
    offset = jnp.int32(0)
    key_rows = lax.all_gather(rotated_key, "ctx", axis=0, tiled=True)
    value_rows = lax.all_gather(self_values, "ctx", axis=0, tiled=True)
    key_index = jnp.arange(key_rows.shape[0], dtype=jnp.int32)
    updated = []
    for current, group in zip(self_start, query_groups):
        updated.append(causal_group(current, group, key_rows, value_rows, key_index, offset))
    self_states = tuple(updated)
    key_rows = lax.all_gather(vision_keys, "ctx", axis=0, tiled=True)
    value_rows = lax.all_gather(vision_values, "ctx", axis=0, tiled=True)
    frame_index = jnp.arange(key_rows.shape[0], dtype=jnp.int32) // FRAME_LEN
    allowed = frame_mask(frame_index, lower_frame, upper_frame)
    touching = jnp.logical_and(lower_frame <= frame_index[-1], upper_frame > frame_index[0])
    needed = jnp.any(jnp.logical_and(has_frames, touching))

    def fold_compute(state_in):
        return attend(state_in, cross_queries, key_rows, value_rows, allowed)

    cross_state = lax.cond(needed, fold_compute, keep_state, cross_start)
    self_rows = finish(self_states[0]).astype(jnp.bfloat16)
    cross_rows = jnp.where(
        has_frames[:, None], jnp.tanh(gate_scale[0]) * finish(cross_state), 0.0
    ).astype(jnp.bfloat16)
    self_context, cross_context = (
        lax.all_to_all(self_rows, "head", split_axis=0, concat_axis=1, tiled=True),
        lax.all_to_all(cross_rows, "head", split_axis=0, concat_axis=1, tiled=True),
    )
    return (self_context, cross_context)


log2e = 1.4426950408889634
stat_rows = 16
unseen = -1e30
contract_last = (((1,), (1,)), ((), ()))


def whole(count):
    return [pl.BlockSpec(memory_space=pltpu.VMEM)] * count


def prepare_kernel(
    inner,
    range_ref,
    position_ref,
    frequency_ref,
    vision_key_ref,
    vision_value_ref,
    cross_ref,
    query_ref,
    key_ref,
    value_ref,
    near_ref,
    across_ref,
    beside_ref,
    own_ref,
    other_ref,
    own_self_ref,
    position_row,
    frequency_row,
    vision_rows,
    cross_rows,
    query_rows,
    key_rows,
    value_rows,
    packet_rows,
    self_rows,
    in_semaphores,
    out_semaphores,
):
    rows = query_rows.shape[0]
    heads = query_rows.shape[1] // inner // HD
    vision = vision_key_ref.shape[0]
    stacked = heads * rows
    place = lax.rem(lax.axis_index("ctx"), inner)
    sides = (place, 1 - place)

    def head_columns(head):
        return pl.ds(pl.multiple_of(head * HD, HD), HD)

    loads = []
    for source, target in (
        (position_ref, position_row),
        (frequency_ref, frequency_row),
        (cross_ref, cross_rows),
        (key_ref, key_rows),
        (value_ref, value_rows),
        (query_ref, query_rows),
    ):
        loads.append(pltpu.make_async_copy(source, target, in_semaphores.at[len(loads)]))
    for side in range(2):
        for slot, source in enumerate((vision_key_ref, vision_value_ref)):
            loads.append(
                pltpu.make_async_copy(
                    source.at[:, head_columns(sides[side])],
                    vision_rows.at[side, pl.ds(slot * vision, vision), :],
                    in_semaphores.at[len(loads)],
                )
            )
    for load in loads:
        load.start()

    stores = []

    def store(source, target):
        copy = pltpu.make_async_copy(source, target, out_semaphores.at[len(stores)])
        copy.start()
        stores.append(copy)

    def stack(target, head, block):
        for step in range(rows // TBLOCK):
            row = (step * heads + head) * TBLOCK
            target[row : row + TBLOCK, :] = block[step * TBLOCK : (step + 1) * TBLOCK]

    lane = lax.broadcasted_iota(jnp.int32, (TBLOCK, HD), 1)
    ranges = jnp.zeros((TBLOCK, HD), jnp.int32)
    for item in range(2 * rows // TBLOCK):
        ranges = jnp.where(lane == item, range_ref[item % 2, item // 2], ranges)
    ranges = ranges.astype(jnp.float32).astype(jnp.bfloat16)
    for load in loads[:2]:
        load.wait()
    place_of_row = jnp.broadcast_to(position_row[...].astype(jnp.float32), (HD, rows)).T
    frequency = jnp.concatenate([frequency_row[...]] * 2, axis=1)
    angles = place_of_row * frequency
    cosine = jnp.cos(angles)
    column = lax.broadcasted_iota(jnp.int32, angles.shape, 1)
    sine = jnp.sin(angles) * jnp.where(column < HD // 2, -1.0, 1.0)

    def turned(block):
        block = block.astype(jnp.float32)
        return (block * cosine + pltpu.roll(block, HD // 2, 1) * sine).astype(jnp.bfloat16)

    for load in loads[2:5]:
        load.wait()
    for side, target in ((1, other_ref), (0, own_ref)):
        packet = packet_rows.at[side]
        for head in range(heads):
            stack(packet, head, cross_rows[:, head_columns(sides[side] * heads + head)])
        packet[stacked : stacked + rows, :] = turned(key_rows[:, head_columns(sides[side])])
        packet[stacked + rows : stacked + 2 * rows, :] = value_rows[:, head_columns(sides[side])]
        packet[stacked + 2 * rows :, :] = ranges
        store(packet, target)
    key_value = pl.ds(stacked, 2 * rows)
    store(packet_rows.at[0, key_value, :], near_ref.at[pl.ds(2 * vision, 2 * rows), :])
    store(packet_rows.at[1, key_value, :], across_ref.at[pl.ds(2 * vision, 2 * rows), :])
    for load in loads[6:8]:
        load.wait()
    store(vision_rows.at[0], near_ref.at[pl.ds(0, 2 * vision), :])
    for load in loads[8:]:
        load.wait()
    store(vision_rows.at[1], across_ref.at[pl.ds(0, 2 * vision), :])
    store(vision_rows.at[1], beside_ref.at[pl.ds(0, 2 * vision), :])
    loads[5].wait()
    for side, target in ((1, beside_ref.at[pl.ds(2 * vision, stacked), :]), (0, own_self_ref)):
        for head in range(heads):
            stack(
                self_rows.at[side],
                head,
                turned(query_rows[:, head_columns(sides[side] * heads + head)]),
            )
        store(self_rows.at[side], target)
    for copy in stores:
        copy.wait()


def prepare(ranges, positions, frequency, vision_keys, vision_values, cross, query, key, value, inner):
    rows, columns = query.shape
    stacked = rows * (columns // inner // HD)
    vision = vision_keys.shape[0]
    packet = stacked + 2 * rows + TBLOCK
    counts = [2 * vision + 2 * rows] * 2 + [2 * vision + stacked] + [packet] * 2 + [stacked]
    return pl.pallas_call(
        functools.partial(prepare_kernel, inner),
        out_shape=[jax.ShapeDtypeStruct((count, HD), jnp.bfloat16) for count in counts],
        in_specs=[pl.BlockSpec(memory_space=pltpu.SMEM)]
        + [pl.BlockSpec(memory_space=pl.ANY)] * 8,
        out_specs=[pl.BlockSpec(memory_space=pl.ANY)] * 6,
        scratch_shapes=[
            pltpu.VMEM((1, rows), jnp.int32),
            pltpu.VMEM((1, HD // 2), jnp.float32),
            pltpu.VMEM((2, 2 * vision, HD), jnp.bfloat16),
            pltpu.VMEM(cross.shape, jnp.bfloat16),
            pltpu.VMEM(query.shape, jnp.bfloat16),
            pltpu.VMEM(key.shape, jnp.bfloat16),
            pltpu.VMEM(value.shape, jnp.bfloat16),
            pltpu.VMEM((2, packet, HD), jnp.bfloat16),
            pltpu.VMEM((2, stacked, HD), jnp.bfloat16),
            pltpu.SemaphoreType.DMA((10,)),
            pltpu.SemaphoreType.DMA((9,)),
        ],
        compiler_params=pltpu.CompilerParams(vmem_limit_bytes=60 * 2**20),
        name="prepare_packets",
    )(
        jnp.transpose(ranges),
        positions.reshape(1, rows),
        frequency.reshape(1, HD // 2),
        vision_keys,
        vision_values,
        cross,
        query,
        key,
        value,
    )


def fold_keys(keys, values_turned, jobs):
    scale = HD**-0.5 * log2e
    spans = []
    for job in jobs:
        width = min(256, job[0].shape[0])
        for begin in range(0, job[0].shape[0], width):
            spans.append((job, slice(begin, begin + width)))
    scores = [
        lax.dot_general(
            keys, stacked_ref[span, :], contract_last, preferred_element_type=jnp.float32
        )
        for (stacked_ref, _, _, _), span in spans
    ]
    for ((_, peak_ref, total_ref, visible), span), score in zip(spans, scores):
        peak = peak_ref[0:1, span]
        seen = visible[:, span]
        if seen.shape[0] == 1:
            highest = jnp.max(score, axis=0, keepdims=True) * scale
            new_peak = jnp.where(seen, jnp.maximum(peak, highest), peak)
            weights = jnp.exp2(score * scale - jnp.where(seen, new_peak, -unseen))
        else:
            score = jnp.where(seen, score * scale, unseen)
            new_peak = jnp.maximum(peak, jnp.max(score, axis=0, keepdims=True))
            weights = jnp.where(seen, jnp.exp2(score - new_peak), 0.0)
        total_ref[:, span] = total_ref[:, span] * jnp.exp2(peak - new_peak) + jnp.dot(
            values_turned, weights.astype(jnp.bfloat16), preferred_element_type=jnp.float32
        )
        peak_ref[0:1, span] = new_peak


def clear(peak_ref, total_ref):
    peak_ref[...] = jnp.full(peak_ref.shape, unseen, jnp.float32)
    total_ref[...] = jnp.zeros(total_ref.shape, jnp.float32)


def finish_columns(peak_ref, total_ref):
    sums = total_ref[HD : HD + 1, :]
    some = sums > 0.0
    safe = jnp.where(some, sums, 1.0)
    log_sum = jnp.where(some, peak_ref[0:1, :] + jnp.log2(safe), unseen)
    return total_ref[:HD, :] / safe, log_sum


def turn_values(value, target_ref):
    target_ref[:HD, :] = value.T
    target_ref[HD:, :] = jnp.ones((stat_rows, target_ref.shape[1]), jnp.bfloat16)


def frame_numbers(inner):
    device = lax.axis_index("ctx")
    plane, place = device // inner, lax.rem(device, inner)
    near = plane + 1 - 2 * lax.rem(plane, 2)
    return (
        plane * inner + place,
        plane * inner + 1 - place,
        near * inner + place,
        near * inner + 1 - place,
    )


def cross_kernel(inner, heads, columns, units, chosen, resumed, finish, table_ref, *refs):
    refs = list(refs)
    query_refs = {number: refs.pop(0) for number, frames in units if frames}
    frame_refs = [refs.pop(0) for _ in chosen]
    state_refs = [refs.pop(0) for _ in range(2)] if resumed else None
    out_refs, (turned_ref, peaks_ref, totals_ref) = refs[:-3], refs[-3:]
    if finish == "state":
        peaks_ref, totals_ref = out_refs
    lanes = heads * TBLOCK
    blocks = columns // lanes
    frames = frame_numbers(inner)
    vision = turned_ref.shape[2]
    for turn, (number, _) in enumerate(units):
        if resumed:
            peaks_ref[turn] = state_refs[0][number]
            totals_ref[turn] = state_refs[1][number]
        else:
            clear(peaks_ref.at[turn], totals_ref.at[turn])

    def job(turn, number, flags):
        visible = jnp.concatenate([jnp.full((1, lanes), flag, jnp.int32) for flag in flags], axis=1)
        queries = query_refs[number].at[:columns, :]
        return queries, peaks_ref.at[turn], totals_ref.at[turn], visible > 0

    for slot, index in enumerate(chosen):
        turn_values(frame_refs[slot][vision : 2 * vision, :], turned_ref.at[slot])
        members = []
        for turn, (number, indices) in enumerate(units):
            if index not in indices:
                continue
            flags = []
            for block in range(blocks):
                at = 2 * (number * blocks + block)
                inside = jnp.logical_and(
                    table_ref[at] <= frames[index], frames[index] < table_ref[at + 1]
                )
                flags.append(inside.astype(jnp.int32))
            members.append((turn, number, flags, functools.reduce(jnp.maximum, flags)))

        def fold(taken):
            fold_keys(
                frame_refs[slot][:vision, :],
                turned_ref[slot],
                [job(turn, number, flags) for turn, number, flags, _ in taken],
            )

        for begin in range(0, len(members), 2):
            pair = members[begin : begin + 2]
            if len(pair) == 2:
                count = pair[0][3] + pair[1][3]
                pl.when(count == 2)(functools.partial(fold, pair))
                for member in pair:
                    alone = jnp.logical_and(count == 1, member[3] == 1)
                    pl.when(alone)(functools.partial(fold, [member]))
            else:
                pl.when(pair[0][3] == 1)(functools.partial(fold, pair))

    if finish == "state":
        return
    stats = []
    for turn in range(len(units)):
        mixed, log_sum = finish_columns(peaks_ref.at[turn], totals_ref.at[turn])
        for block in range(blocks):
            span = slice(block * lanes, (block + 1) * lanes)
            stats.append(log_sum[:, span])
            row = (turn * blocks + block) * HD
            out_refs[0][row : row + HD, :] = mixed[:, span].astype(out_refs[0].dtype)
    stat = jnp.concatenate(stats, axis=0)
    if finish == "packed":
        high = stat.astype(jnp.bfloat16)
        rest = stat - high.astype(jnp.float32)
        middle = rest.astype(jnp.bfloat16)
        low = rest - middle.astype(jnp.float32)
        rows = [high.astype(jnp.float32), middle.astype(jnp.float32), low, jnp.zeros_like(stat)]
        out_refs[0][len(stats) * HD :, :] = jnp.concatenate(rows, axis=0).astype(jnp.bfloat16)
    else:
        out_refs[1][...] = stat


def cross_part(table, queries, frames, units, state, finish, rows, inner, heads):
    lanes = heads * TBLOCK
    columns = rows * heads
    vision = FRAME_LEN
    count = len(units) * (rows // TBLOCK)
    chosen = tuple(sorted({index for _, indices in units for index in indices}))
    if finish == "state":
        out_shape = (
            jax.ShapeDtypeStruct((len(units), 8, columns), jnp.float32),
            jax.ShapeDtypeStruct((len(units), HD + stat_rows, columns), jnp.float32),
        )
    elif finish == "packed":
        out_shape = (jax.ShapeDtypeStruct((count * HD + 4 * count, lanes), jnp.bfloat16),)
    else:
        out_shape = (
            jax.ShapeDtypeStruct((count * HD, lanes), jnp.float32),
            jax.ShapeDtypeStruct((count, lanes), jnp.float32),
        )
    arguments = [queries[number] for number, indices in units if indices]
    arguments += [*(frames[index] for index in chosen), *state]
    return pl.pallas_call(
        functools.partial(
            cross_kernel, inner, heads, columns, units, chosen, len(state) > 0, finish
        ),
        out_shape=out_shape,
        in_specs=[pl.BlockSpec(memory_space=pltpu.SMEM)] + whole(len(arguments)),
        out_specs=whole(len(out_shape)),
        scratch_shapes=[
            pltpu.VMEM((len(chosen), HD + stat_rows, vision), jnp.bfloat16),
            pltpu.VMEM((len(units), 8, columns), jnp.float32),
            pltpu.VMEM((len(units), HD + stat_rows, columns), jnp.float32),
        ],
        compiler_params=pltpu.CompilerParams(vmem_limit_bytes=28 * 2**20),
        name="cross_" + finish,
    )(table, *arguments)


def self_kernel(inner, heads, rows, own_ref, beside_ref, *refs):
    key_value_refs, out_ref = refs[:7], refs[7]
    key_ref, value_ref, turned_ref, peak_ref, total_ref = refs[8:]
    device = lax.axis_index("ctx")
    plane, place = device // inner, lax.rem(device, inner)
    lanes = heads * TBLOCK
    columns = rows * heads
    vision = beside_ref.shape[0] - columns
    tails = [(ref, ref.shape[0] - TBLOCK - 2 * rows) for ref in key_value_refs[:2]]
    tails += [(ref, ref.shape[0] - 2 * rows) for ref in key_value_refs[2:4]]
    tails += [(ref, ref.shape[0] - TBLOCK - 2 * rows) for ref in key_value_refs[4:6]]
    tails += [(key_value_refs[6], 0), (key_value_refs[6], 2 * rows)]
    for slot, (ref, begin) in enumerate(tails):
        span = slice(slot * rows, (slot + 1) * rows)
        key_ref[span, :] = ref[begin : begin + rows, :]
        value_ref[span, :] = ref[begin + rows : begin + 2 * rows, :]
    turn_values(value_ref[...], turned_ref)
    planes = (plane, plane + 1 - 2 * lax.rem(plane, 2), lax.rem(plane + 2, 4), 3 - plane)
    starts = []
    for source in planes:
        starts.append((source * inner + place) * rows)
        starts.append((source * inner + 1 - place) * rows)
    down = lax.broadcasted_iota(jnp.int32, (rows, columns), 0)
    key_index = jnp.concatenate([down + start for start in starts], axis=0)
    across = lax.broadcasted_iota(jnp.int32, key_index.shape, 1)
    token = (across // lanes) * TBLOCK + lax.rem(across, TBLOCK)
    queries = (own_ref, beside_ref.at[pl.ds(vision, columns), :])
    for slot, query_ref in enumerate(queries):
        side = place if slot == 0 else 1 - place
        clear(peak_ref, total_ref)
        visible = key_index <= token + (plane * inner + side) * rows
        fold_keys(key_ref[...], turned_ref[...], [(query_ref, peak_ref, total_ref, visible)])
        mixed, _ = finish_columns(peak_ref, total_ref)
        for block in range(rows // TBLOCK):
            part = mixed[:, block * lanes : (block + 1) * lanes].T.astype(jnp.bfloat16)
            for head in range(heads):
                out_ref[block * inner + side, :, head * HD : (head + 1) * HD] = part[
                    head * TBLOCK : (head + 1) * TBLOCK
                ]


def self_part(own, beside, key_values, rows, inner, heads):
    return pl.pallas_call(
        functools.partial(self_kernel, inner, heads, rows),
        out_shape=jax.ShapeDtypeStruct((inner * rows // TBLOCK, TBLOCK, heads * HD), jnp.bfloat16),
        in_specs=whole(2 + len(key_values)),
        out_specs=whole(1)[0],
        scratch_shapes=[
            pltpu.VMEM((8 * rows, HD), jnp.bfloat16),
            pltpu.VMEM((8 * rows, HD), jnp.bfloat16),
            pltpu.VMEM((HD + stat_rows, 8 * rows), jnp.bfloat16),
            pltpu.VMEM((8, rows * heads), jnp.float32),
            pltpu.VMEM((HD + stat_rows, rows * heads), jnp.float32),
        ],
        compiler_params=pltpu.CompilerParams(vmem_limit_bytes=24 * 2**20),
        name="self_attention",
    )(own, beside, *key_values)


def combine_kernel(inner, heads, gate_ref, mixed_ref, stat_ref, returned_ref, out_ref):
    count = stat_ref.shape[0]
    side = count // inner
    place = lax.rem(lax.axis_index("ctx"), inner)
    gate = jnp.tanh(jnp.full((1, heads * TBLOCK), gate_ref[0], jnp.float32))
    stats = returned_ref[count * HD :, :].astype(jnp.float32)
    far_stat = stats[:count] + stats[count : 2 * count] + stats[2 * count : 3 * count]
    own_stat = stat_ref[...]
    peak = jnp.maximum(own_stat, far_stat)
    own_weight = jnp.exp2(own_stat - peak)
    far_weight = jnp.exp2(far_stat - peak)
    ratio = gate / (own_weight + far_weight)
    own_weight, far_weight = own_weight * ratio, far_weight * ratio
    for block in range(count):
        target = (block % side) * inner + (place if block < side else 1 - place)
        span = slice(block * HD, (block + 1) * HD)
        mixed = mixed_ref[span, :] * own_weight[block : block + 1] + returned_ref[span, :].astype(
            jnp.float32
        ) * far_weight[block : block + 1]
        part = mixed.T.astype(jnp.bfloat16)
        for head in range(heads):
            out_ref[target, :, head * HD : (head + 1) * HD] = part[
                head * TBLOCK : (head + 1) * TBLOCK
            ]


def combine(gate_scale, mixed, stat, returned, inner, heads):
    return pl.pallas_call(
        functools.partial(combine_kernel, inner, heads),
        out_shape=jax.ShapeDtypeStruct((stat.shape[0], TBLOCK, heads * HD), jnp.bfloat16),
        in_specs=[pl.BlockSpec(memory_space=pltpu.SMEM)] + whole(3),
        out_specs=whole(1)[0],
        compiler_params=pltpu.CompilerParams(vmem_limit_bytes=16 * 2**20),
        name="combine_planes",
    )(gate_scale, mixed, stat, returned)


def spread_kernel(in_ref, out_ref):
    group = in_ref.shape[2]
    for head in range(in_ref.shape[0]):
        out_ref[:, head * group : (head + 1) * group] = in_ref[head]


def spread(inward):
    count, rows, columns = inward.shape
    return pl.pallas_call(
        spread_kernel,
        out_shape=jax.ShapeDtypeStruct((rows, count * columns), inward.dtype),
        in_specs=whole(1),
        out_specs=whole(1)[0],
        compiler_params=pltpu.CompilerParams(vmem_limit_bytes=16 * 2**20),
        name="spread_heads",
    )(inward)


def on_device_split(
    axes,
    query_self,
    key_self,
    value_self,
    positions,
    query_cross,
    key_vision,
    value_vision,
    media_range,
    gate_scale,
):
    inner = key_self.shape[1] // HD
    heads = query_self.shape[1] // key_self.shape[1]
    rows = query_self.shape[0]
    group = heads * HD
    columns = axes["head"]
    devices = axes["ctx"]
    plane_count = devices // inner

    def place_of(device):
        return device // inner, device % inner

    def send(values, turn, flip, upward=0):
        pairs = []
        for device in range(devices):
            plane, place = place_of(device)
            target = plane ^ turn
            if upward == 0 or target ^ upward < target:
                pairs.append((device, target * inner + (place ^ flip)))
        return lax.ppermute(values, "ctx", pairs)

    exponents = np.arange(HD // 2) * (2.0 / HD)
    frequency = jnp.asarray(np.power(rope_base, -exponents), jnp.float32)
    near_out, across_out, beside_out, own, other, own_self = prepare(
        media_range,
        positions,
        frequency,
        key_vision,
        value_vision,
        query_cross,
        query_self,
        key_self,
        value_self,
        inner,
    )
    partner = send(other, 0, 1)
    far = send(own, 2, 0)
    near = send(near_out, 1, 0)
    beside = send(beside_out, 0, 1)
    across_out, partner = lax.optimization_barrier((across_out, partner))
    far_across = send(partner, 2, 0)
    across = send(across_out, 1, 1)
    tail = slice(rows * heads, rows * heads + 2 * rows)
    last = send(jnp.concatenate([own[tail], partner[tail]], axis=0), 3, 0, upward=3)

    queries = (own, partner, far, far_across)
    table = [values[-TBLOCK, : 2 * (rows // TBLOCK)] for values in queries]
    first_table = jnp.concatenate(table[:2]).astype(jnp.int32)
    table = jnp.concatenate(table).astype(jnp.int32)
    frames = (near_out, beside, near, across)
    sizes = (rows, inner, heads)
    units = ((0, (0, 2)), (1, (0, 2)), (2, ()), (3, ()))
    state = cross_part(first_table, queries, frames, units, (), "state", *sizes)
    units = ((0, ()), (1, ()), (2, (0, 2)), (3, (0, 2)))
    state = cross_part(table, queries, frames, units, state, "state", *sizes)
    units = ((0, (1,)), (1, (1,)), (2, (1,)), (3, (1,)))
    state = cross_part(table, queries, frames, units, state, "state", *sizes)
    state, last = lax.optimization_barrier((state, last))
    units = ((2, (3,)), (3, (3,)))
    (outgoing,) = cross_part(table, queries, frames, units, state, "packed", *sizes)
    returned = send(outgoing, 2, 0)
    outgoing, table, own_self = lax.optimization_barrier((outgoing, table, own_self))
    units = ((0, (3,)), (1, (3,)))
    mixed, stat = cross_part(table, queries, frames, units, state, "own", *sizes)
    self_rows = self_part(
        own_self, beside, (own, partner, near, across, far, far_across, last), *sizes
    )
    planes = [
        [
            (plane * inner + place) * columns + column
            for column in range(columns)
            for place in range(inner)
        ]
        for plane in range(plane_count)
    ]

    def exchange(outward):
        inward = lax.all_to_all(
            outward.reshape(-1, outward.shape[2]),
            ("ctx", "head"),
            0,
            0,
            axis_index_groups=planes,
            tiled=True,
        )
        return spread(inward.reshape(outward.shape))

    self_context = exchange(self_rows)
    cross_context = exchange(combine(gate_scale, mixed, stat, returned, inner, heads))
    return self_context, cross_context


def on_device(axes, *arguments):
    query_self, key_self, _, _, _, key_vision, _, media_range, _ = arguments
    inner = key_self.shape[1] // HD
    heads = query_self.shape[1] // key_self.shape[1]
    rows = query_self.shape[0]
    suited = (
        inner == 2
        and axes["ctx"] == 4 * inner
        and heads * TBLOCK == HD
        and key_vision.shape[0] == FRAME_LEN
        and rows == axes["head"] * TBLOCK
        and media_range.shape[0] * TBLOCK == rows
    )
    if suited:
        return on_device_split(axes, *arguments)
    return on_device_gathered(*arguments)


def solution(mesh):
    placed = (
        P("ctx", "head"),
        P("ctx", "head"),
        P("ctx", "head"),
        P("ctx"),
        P("ctx", "head"),
        P("ctx", "head"),
        P("ctx", "head"),
        P("ctx", None),
        P(),
    )
    return jax.shard_map(
        functools.partial(on_device, dict(mesh.shape)),
        mesh=mesh,
        in_specs=placed,
        out_specs=(P(("ctx", "head"), None), P(("ctx", "head"), None)),
        check_vma=False,
    )
```

```python
import functools

import jax
import jax.numpy as jnp
import numpy as np
from jax import lax
from jax.experimental import pallas as pl
from jax.experimental.pallas import tpu as pltpu
from jax.sharding import PartitionSpec as P

HD = 128
TBLOCK = 16
FRAME_LEN = 896


rope_base = 500000.0
lowest = -1e30


def rotate(values, positions):
    half_width = values.shape[-1] // 2
    exponents = jnp.arange(half_width, dtype=jnp.float32) * (2.0 / values.shape[-1])
    frequency = jnp.power(rope_base, -exponents)
    angles = positions.astype(jnp.float32)[:, None] * frequency[None, :]
    cosine = jnp.cos(angles)[:, None, :]
    sine_part = jnp.sin(angles)[:, None, :]
    first_half = values[..., :half_width]
    second_half = values[..., half_width:]
    return jnp.concatenate(
        [
            first_half * cosine - second_half * sine_part,
            second_half * cosine + first_half * sine_part,
        ],
        axis=-1,
    )


def key_block(key_count):
    block_size = min(key_count, 1024)
    while key_count % block_size != 0:
        block_size = block_size - 1
    return block_size


def attend_block(state_in, queries, key_rows, value_rows, allowed):
    maxima, totals, accumulated = state_in
    scale_factor = queries.shape[-1] ** (-0.5)
    scores = (
        jnp.einsum("rkgd,nkd->kgrn", queries, key_rows, preferred_element_type=jnp.float32)
        * scale_factor
    )
    visible = allowed[None, None, :, :]
    scores = jnp.where(visible, scores, lowest)
    new_maxima = jnp.maximum(maxima, jnp.max(scores, axis=-1))
    weights = jnp.where(visible, jnp.exp(scores - new_maxima[..., None]), 0.0)
    factor = jnp.exp(maxima - new_maxima)
    totals = totals * factor + jnp.sum(weights, axis=-1)
    accumulated = accumulated * factor[..., None] + jnp.einsum(
        "kgrn,nkd->kgrd",
        weights.astype(jnp.bfloat16),
        value_rows,
        preferred_element_type=jnp.float32,
    )
    return (new_maxima, totals, accumulated)


def attend(state_in, queries, key_rows, value_rows, allowed):
    key_count = key_rows.shape[0]
    block_size = key_block(key_count)
    if block_size == key_count:
        return attend_block(state_in, queries, key_rows, value_rows, allowed)

    def step_block(block_index, state_now):
        row_begin = block_index * block_size
        key_part = lax.dynamic_slice_in_dim(key_rows, row_begin, block_size, 0)
        value_part = lax.dynamic_slice_in_dim(value_rows, row_begin, block_size, 0)
        allowed_part = lax.dynamic_slice_in_dim(allowed, row_begin, block_size, 1)
        return attend_block(state_now, queries, key_part, value_part, allowed_part)

    return lax.fori_loop(0, key_count // block_size, step_block, state_in)


def keep_state(current):
    return current


def empty_state(row_count, kv_heads, group_size, head_size):
    maxima = jnp.full((kv_heads, group_size, row_count), lowest, jnp.float32)
    totals = jnp.zeros((kv_heads, group_size, row_count), jnp.float32)
    accumulated = jnp.zeros((kv_heads, group_size, row_count, head_size), jnp.float32)
    return (maxima, totals, accumulated)


def finish(state_in):
    maxima, totals, accumulated = state_in
    safe_totals = jnp.where(totals > 0.0, totals, 1.0)
    result = accumulated / safe_totals[..., None]
    kv_heads, group_size, row_count, head_size = result.shape
    return jnp.transpose(result, (2, 0, 1, 3)).reshape(row_count, kv_heads * group_size * head_size)


def causal_group(current, group, key_rows, value_rows, key_index, offset):
    queries, row_index = group
    allowed = key_index[None, :] <= row_index[:, None]

    def causal_compute(state_in):
        return attend(state_in, queries, key_rows, value_rows, allowed)

    return lax.cond(offset <= jnp.max(row_index), causal_compute, keep_state, current)


def frame_mask(frame_index, lower_frame, upper_frame):
    return jnp.logical_and(
        frame_index[None, :] >= lower_frame[:, None], frame_index[None, :] < upper_frame[:, None]
    )


def on_device_gathered(
    query_self,
    key_self,
    value_self,
    positions,
    query_cross,
    key_vision,
    value_vision,
    media_range,
    gate_scale,
):
    head_size = HD
    kv_heads = key_self.shape[1] // head_size
    group_size = query_self.shape[1] // key_self.shape[1]
    row_count = query_self.shape[0]
    vision_count = key_vision.shape[0]
    device = lax.axis_index("ctx")
    own_rows = device * row_count + jnp.arange(row_count, dtype=jnp.int32)
    rotated_query = rotate(
        query_self.astype(jnp.float32).reshape(row_count, kv_heads * group_size, head_size),
        positions,
    )
    rotated_query = rotated_query.astype(jnp.bfloat16).reshape(
        row_count, kv_heads, group_size, head_size
    )
    rotated_key = rotate(
        key_self.astype(jnp.float32).reshape(row_count, kv_heads, head_size), positions
    ).astype(jnp.bfloat16)
    self_values = value_self.reshape(row_count, kv_heads, head_size)
    vision_keys = key_vision.reshape(vision_count, kv_heads, head_size)
    vision_values = value_vision.reshape(vision_count, kv_heads, head_size)
    cross_queries = query_cross.reshape(row_count, kv_heads, group_size, head_size)
    lower_frame = jnp.repeat(media_range[:, 0], TBLOCK)
    upper_frame = jnp.repeat(media_range[:, 1], TBLOCK)
    has_frames = upper_frame > lower_frame
    query_groups = ((rotated_query, own_rows),)
    self_start = tuple(
        (empty_state(group[1].shape[0], kv_heads, group_size, head_size) for group in query_groups)
    )
    cross_start = empty_state(row_count, kv_heads, group_size, head_size)
    offset = jnp.int32(0)
    key_rows = lax.all_gather(rotated_key, "ctx", axis=0, tiled=True)
    value_rows = lax.all_gather(self_values, "ctx", axis=0, tiled=True)
    key_index = jnp.arange(key_rows.shape[0], dtype=jnp.int32)
    updated = []
    for current, group in zip(self_start, query_groups):
        updated.append(causal_group(current, group, key_rows, value_rows, key_index, offset))
    self_states = tuple(updated)
    key_rows = lax.all_gather(vision_keys, "ctx", axis=0, tiled=True)
    value_rows = lax.all_gather(vision_values, "ctx", axis=0, tiled=True)
    frame_index = jnp.arange(key_rows.shape[0], dtype=jnp.int32) // FRAME_LEN
    allowed = frame_mask(frame_index, lower_frame, upper_frame)
    touching = jnp.logical_and(lower_frame <= frame_index[-1], upper_frame > frame_index[0])
    needed = jnp.any(jnp.logical_and(has_frames, touching))

    def fold_compute(state_in):
        return attend(state_in, cross_queries, key_rows, value_rows, allowed)

    cross_state = lax.cond(needed, fold_compute, keep_state, cross_start)
    self_rows = finish(self_states[0]).astype(jnp.bfloat16)
    cross_rows = jnp.where(
        has_frames[:, None], jnp.tanh(gate_scale[0]) * finish(cross_state), 0.0
    ).astype(jnp.bfloat16)
    self_context, cross_context = (
        lax.all_to_all(self_rows, "head", split_axis=0, concat_axis=1, tiled=True),
        lax.all_to_all(cross_rows, "head", split_axis=0, concat_axis=1, tiled=True),
    )
    return (self_context, cross_context)


log2e = 1.4426950408889634
stat_rows = 16
unseen = -1e30
contract_last = (((1,), (1,)), ((), ()))


def whole(count):
    return [pl.BlockSpec(memory_space=pltpu.VMEM)] * count


def prepare_kernel(
    inner,
    range_ref,
    position_ref,
    frequency_ref,
    vision_key_ref,
    vision_value_ref,
    cross_ref,
    query_ref,
    key_ref,
    value_ref,
    near_ref,
    across_ref,
    beside_ref,
    own_ref,
    other_ref,
    own_self_ref,
    position_row,
    frequency_row,
    vision_rows,
    cross_rows,
    query_rows,
    key_rows,
    value_rows,
    packet_rows,
    self_rows,
    in_semaphores,
    out_semaphores,
):
    rows = query_rows.shape[0]
    heads = query_rows.shape[1] // inner // HD
    vision = vision_key_ref.shape[0]
    stacked = heads * rows
    place = lax.rem(lax.axis_index("ctx"), inner)
    sides = (place, 1 - place)

    def head_columns(head):
        return pl.ds(pl.multiple_of(head * HD, HD), HD)

    loads = []
    for source, target in (
        (position_ref, position_row),
        (frequency_ref, frequency_row),
        (cross_ref, cross_rows),
        (key_ref, key_rows),
        (value_ref, value_rows),
        (query_ref, query_rows),
    ):
        loads.append(pltpu.make_async_copy(source, target, in_semaphores.at[len(loads)]))
    for side in range(2):
        for slot, source in enumerate((vision_key_ref, vision_value_ref)):
            loads.append(
                pltpu.make_async_copy(
                    source.at[:, head_columns(sides[side])],
                    vision_rows.at[side, pl.ds(slot * vision, vision), :],
                    in_semaphores.at[len(loads)],
                )
            )
    for load in loads:
        load.start()

    stores = []

    def store(source, target):
        copy = pltpu.make_async_copy(source, target, out_semaphores.at[len(stores)])
        copy.start()
        stores.append(copy)

    def stack(target, head, block):
        for step in range(rows // TBLOCK):
            row = (step * heads + head) * TBLOCK
            target[row : row + TBLOCK, :] = block[step * TBLOCK : (step + 1) * TBLOCK]

    lane = lax.broadcasted_iota(jnp.int32, (TBLOCK, HD), 1)
    ranges = jnp.zeros((TBLOCK, HD), jnp.int32)
    for item in range(2 * rows // TBLOCK):
        ranges = jnp.where(lane == item, range_ref[item % 2, item // 2], ranges)
    ranges = ranges.astype(jnp.float32).astype(jnp.bfloat16)
    for load in loads[:2]:
        load.wait()
    place_of_row = jnp.broadcast_to(position_row[...].astype(jnp.float32), (HD, rows)).T
    frequency = jnp.concatenate([frequency_row[...]] * 2, axis=1)
    angles = place_of_row * frequency
    cosine = jnp.cos(angles)
    column = lax.broadcasted_iota(jnp.int32, angles.shape, 1)
    sine = jnp.sin(angles) * jnp.where(column < HD // 2, -1.0, 1.0)

    def turned(block):
        block = block.astype(jnp.float32)
        return (block * cosine + pltpu.roll(block, HD // 2, 1) * sine).astype(jnp.bfloat16)

    for load in loads[2:5]:
        load.wait()
    for side, target in ((1, other_ref), (0, own_ref)):
        packet = packet_rows.at[side]
        for head in range(heads):
            stack(packet, head, cross_rows[:, head_columns(sides[side] * heads + head)])
        packet[stacked : stacked + rows, :] = turned(key_rows[:, head_columns(sides[side])])
        packet[stacked + rows : stacked + 2 * rows, :] = value_rows[:, head_columns(sides[side])]
        packet[stacked + 2 * rows :, :] = ranges
        store(packet, target)
    key_value = pl.ds(stacked, 2 * rows)
    store(packet_rows.at[0, key_value, :], near_ref.at[pl.ds(2 * vision, 2 * rows), :])
    store(packet_rows.at[1, key_value, :], across_ref.at[pl.ds(2 * vision, 2 * rows), :])
    for load in loads[6:8]:
        load.wait()
    store(vision_rows.at[0], near_ref.at[pl.ds(0, 2 * vision), :])
    for load in loads[8:]:
        load.wait()
    store(vision_rows.at[1], across_ref.at[pl.ds(0, 2 * vision), :])
    store(vision_rows.at[1], beside_ref.at[pl.ds(0, 2 * vision), :])
    loads[5].wait()
    for side, target in ((1, beside_ref.at[pl.ds(2 * vision, stacked), :]), (0, own_self_ref)):
        for head in range(heads):
            stack(
                self_rows.at[side],
                head,
                turned(query_rows[:, head_columns(sides[side] * heads + head)]),
            )
        store(self_rows.at[side], target)
    for copy in stores:
        copy.wait()


def prepare(ranges, positions, frequency, vision_keys, vision_values, cross, query, key, value, inner):
    rows, columns = query.shape
    stacked = rows * (columns // inner // HD)
    vision = vision_keys.shape[0]
    packet = stacked + 2 * rows + TBLOCK
    counts = [2 * vision + 2 * rows] * 2 + [2 * vision + stacked] + [packet] * 2 + [stacked]
    return pl.pallas_call(
        functools.partial(prepare_kernel, inner),
        out_shape=[jax.ShapeDtypeStruct((count, HD), jnp.bfloat16) for count in counts],
        in_specs=[pl.BlockSpec(memory_space=pltpu.SMEM)]
        + [pl.BlockSpec(memory_space=pl.ANY)] * 8,
        out_specs=[pl.BlockSpec(memory_space=pl.ANY)] * 6,
        scratch_shapes=[
            pltpu.VMEM((1, rows), jnp.int32),
            pltpu.VMEM((1, HD // 2), jnp.float32),
            pltpu.VMEM((2, 2 * vision, HD), jnp.bfloat16),
            pltpu.VMEM(cross.shape, jnp.bfloat16),
            pltpu.VMEM(query.shape, jnp.bfloat16),
            pltpu.VMEM(key.shape, jnp.bfloat16),
            pltpu.VMEM(value.shape, jnp.bfloat16),
            pltpu.VMEM((2, packet, HD), jnp.bfloat16),
            pltpu.VMEM((2, stacked, HD), jnp.bfloat16),
            pltpu.SemaphoreType.DMA((10,)),
            pltpu.SemaphoreType.DMA((9,)),
        ],
        compiler_params=pltpu.CompilerParams(vmem_limit_bytes=60 * 2**20),
        name="prepare_packets",
    )(
        jnp.transpose(ranges),
        positions.reshape(1, rows),
        frequency.reshape(1, HD // 2),
        vision_keys,
        vision_values,
        cross,
        query,
        key,
        value,
    )


def fold_keys(keys, values_turned, jobs):
    scale = HD**-0.5 * log2e
    spans = []
    for job in jobs:
        width = min(256, job[0].shape[0])
        for begin in range(0, job[0].shape[0], width):
            spans.append((job, slice(begin, begin + width)))
    scores = [
        lax.dot_general(
            keys, stacked_ref[span, :], contract_last, preferred_element_type=jnp.float32
        )
        for (stacked_ref, _, _, _), span in spans
    ]
    for ((_, peak_ref, total_ref, visible), span), score in zip(spans, scores):
        peak = peak_ref[0:1, span]
        seen = visible[:, span]
        if seen.shape[0] == 1:
            highest = jnp.max(score, axis=0, keepdims=True) * scale
            new_peak = jnp.where(seen, jnp.maximum(peak, highest), peak)
            weights = jnp.exp2(score * scale - jnp.where(seen, new_peak, -unseen))
        else:
            score = jnp.where(seen, score * scale, unseen)
            new_peak = jnp.maximum(peak, jnp.max(score, axis=0, keepdims=True))
            weights = jnp.where(seen, jnp.exp2(score - new_peak), 0.0)
        total_ref[:, span] = total_ref[:, span] * jnp.exp2(peak - new_peak) + jnp.dot(
            values_turned, weights.astype(jnp.bfloat16), preferred_element_type=jnp.float32
        )
        peak_ref[0:1, span] = new_peak


def clear(peak_ref, total_ref):
    peak_ref[...] = jnp.full(peak_ref.shape, unseen, jnp.float32)
    total_ref[...] = jnp.zeros(total_ref.shape, jnp.float32)


def finish_columns(peak_ref, total_ref):
    sums = total_ref[HD : HD + 1, :]
    some = sums > 0.0
    safe = jnp.where(some, sums, 1.0)
    log_sum = jnp.where(some, peak_ref[0:1, :] + jnp.log2(safe), unseen)
    return total_ref[:HD, :] / safe, log_sum


def turn_values(value, target_ref):
    target_ref[:HD, :] = value.T
    target_ref[HD:, :] = jnp.ones((stat_rows, target_ref.shape[1]), jnp.bfloat16)


def frame_numbers(inner):
    device = lax.axis_index("ctx")
    plane, place = device // inner, lax.rem(device, inner)
    near = plane + 1 - 2 * lax.rem(plane, 2)
    return (
        plane * inner + place,
        plane * inner + 1 - place,
        near * inner + place,
        near * inner + 1 - place,
    )


def cross_kernel(inner, heads, columns, places, units, chosen, resumed, finish, table_ref, *refs):
    refs = list(refs)
    arrays = sorted({places[number][0] for number, frames in units if frames})
    arrays = {array: refs.pop(0) for array in arrays}
    query_refs = {}
    for number, frames in units:
        if frames:
            array, row = places[number]
            query_refs[number] = arrays[array].at[pl.ds(row, columns), :]
    frame_refs = [refs.pop(0) for _ in chosen]
    state_refs = [refs.pop(0) for _ in range(2)] if resumed else None
    out_refs, (turned_ref, peaks_ref, totals_ref) = refs[:-3], refs[-3:]
    if finish == "state":
        peaks_ref, totals_ref = out_refs
    lanes = heads * TBLOCK
    blocks = columns // lanes
    frames = frame_numbers(inner)
    vision = turned_ref.shape[2]
    for turn, (number, _) in enumerate(units):
        if resumed:
            peaks_ref[turn] = state_refs[0][number]
            totals_ref[turn] = state_refs[1][number]
        else:
            clear(peaks_ref.at[turn], totals_ref.at[turn])

    def job(turn, number, flags):
        visible = jnp.concatenate([jnp.full((1, lanes), flag, jnp.int32) for flag in flags], axis=1)
        return query_refs[number], peaks_ref.at[turn], totals_ref.at[turn], visible > 0

    for slot, index in enumerate(chosen):
        turn_values(frame_refs[slot][vision : 2 * vision, :], turned_ref.at[slot])
        members = []
        for turn, (number, indices) in enumerate(units):
            if index not in indices:
                continue
            flags = []
            for block in range(blocks):
                at = 2 * (number * blocks + block)
                inside = jnp.logical_and(
                    table_ref[at] <= frames[index], frames[index] < table_ref[at + 1]
                )
                flags.append(inside.astype(jnp.int32))
            members.append((turn, number, flags, functools.reduce(jnp.maximum, flags)))

        def fold(taken):
            fold_keys(
                frame_refs[slot][:vision, :],
                turned_ref[slot],
                [job(turn, number, flags) for turn, number, flags, _ in taken],
            )

        for begin in range(0, len(members), 2):
            pair = members[begin : begin + 2]
            if len(pair) == 2:
                count = pair[0][3] + pair[1][3]
                pl.when(count == 2)(functools.partial(fold, pair))
                for member in pair:
                    alone = jnp.logical_and(count == 1, member[3] == 1)
                    pl.when(alone)(functools.partial(fold, [member]))
            else:
                pl.when(pair[0][3] == 1)(functools.partial(fold, pair))

    if finish == "state":
        return
    stats = []
    for turn in range(len(units)):
        mixed, log_sum = finish_columns(peaks_ref.at[turn], totals_ref.at[turn])
        for block in range(blocks):
            span = slice(block * lanes, (block + 1) * lanes)
            stats.append(log_sum[:, span])
            row = (turn * blocks + block) * HD
            out_refs[0][row : row + HD, :] = mixed[:, span].astype(out_refs[0].dtype)
    stat = jnp.concatenate(stats, axis=0)
    if finish == "packed":
        high = stat.astype(jnp.bfloat16)
        rest = stat - high.astype(jnp.float32)
        middle = rest.astype(jnp.bfloat16)
        low = rest - middle.astype(jnp.float32)
        rows = [high.astype(jnp.float32), middle.astype(jnp.float32), low, jnp.zeros_like(stat)]
        out_refs[0][len(stats) * HD :, :] = jnp.concatenate(rows, axis=0).astype(jnp.bfloat16)
    else:
        out_refs[1][...] = stat


def cross_part(table, queries, frames, units, state, finish, rows, inner, heads):
    lanes = heads * TBLOCK
    columns = rows * heads
    vision = FRAME_LEN
    count = len(units) * (rows // TBLOCK)
    chosen = tuple(sorted({index for _, indices in units for index in indices}))
    if finish == "state":
        out_shape = (
            jax.ShapeDtypeStruct((len(units), 8, columns), jnp.float32),
            jax.ShapeDtypeStruct((len(units), HD + stat_rows, columns), jnp.float32),
        )
    elif finish == "packed":
        out_shape = (jax.ShapeDtypeStruct((count * HD + 4 * count, lanes), jnp.bfloat16),)
    else:
        out_shape = (
            jax.ShapeDtypeStruct((count * HD, lanes), jnp.float32),
            jax.ShapeDtypeStruct((count, lanes), jnp.float32),
        )
    packet = columns + 2 * rows + TBLOCK
    places = ((0, 0), (1, 0), (2, 0), (2, packet))
    arrays = sorted({places[number][0] for number, indices in units if indices})
    arguments = [queries[array] for array in arrays]
    arguments += [*(frames[index] for index in chosen), *state]
    return pl.pallas_call(
        functools.partial(
            cross_kernel, inner, heads, columns, places, units, chosen, len(state) > 0, finish
        ),
        out_shape=out_shape,
        in_specs=[pl.BlockSpec(memory_space=pltpu.SMEM)] + whole(len(arguments)),
        out_specs=whole(len(out_shape)),
        scratch_shapes=[
            pltpu.VMEM((len(chosen), HD + stat_rows, vision), jnp.bfloat16),
            pltpu.VMEM((len(units), 8, columns), jnp.float32),
            pltpu.VMEM((len(units), HD + stat_rows, columns), jnp.float32),
        ],
        compiler_params=pltpu.CompilerParams(vmem_limit_bytes=28 * 2**20),
        name="cross_" + finish,
    )(table, *arguments)


def self_kernel(inner, heads, rows, own_ref, beside_ref, *refs):
    key_value_refs, out_ref = refs[:6], refs[6]
    key_ref, value_ref, turned_ref, peak_ref, total_ref = refs[7:]
    device = lax.axis_index("ctx")
    plane, place = device // inner, lax.rem(device, inner)
    lanes = heads * TBLOCK
    columns = rows * heads
    vision = beside_ref.shape[0] - columns
    own_kv, partner_kv, near_kv, across_kv, far_kv, last_kv = key_value_refs
    packet = own_kv.shape[0]
    vision_rows = near_kv.shape[0] - 2 * rows
    tails = [(own_kv, columns), (partner_kv, columns), (near_kv, vision_rows)]
    tails += [(across_kv, vision_rows), (far_kv, columns), (far_kv, packet + columns)]
    tails += [(last_kv, 0), (last_kv, 2 * rows)]
    for slot, (ref, begin) in enumerate(tails):
        span = slice(slot * rows, (slot + 1) * rows)
        key_ref[span, :] = ref[begin : begin + rows, :]
        value_ref[span, :] = ref[begin + rows : begin + 2 * rows, :]
    turn_values(value_ref[...], turned_ref)
    planes = (plane, plane + 1 - 2 * lax.rem(plane, 2), lax.rem(plane + 2, 4), 3 - plane)
    starts = []
    for source in planes:
        starts.append((source * inner + place) * rows)
        starts.append((source * inner + 1 - place) * rows)
    down = lax.broadcasted_iota(jnp.int32, (rows, columns), 0)
    key_index = jnp.concatenate([down + start for start in starts], axis=0)
    across = lax.broadcasted_iota(jnp.int32, key_index.shape, 1)
    token = (across // lanes) * TBLOCK + lax.rem(across, TBLOCK)
    queries = (own_ref, beside_ref.at[pl.ds(vision, columns), :])
    for slot, query_ref in enumerate(queries):
        side = place if slot == 0 else 1 - place
        clear(peak_ref, total_ref)
        visible = key_index <= token + (plane * inner + side) * rows
        fold_keys(key_ref[...], turned_ref[...], [(query_ref, peak_ref, total_ref, visible)])
        mixed, _ = finish_columns(peak_ref, total_ref)
        for block in range(rows // TBLOCK):
            part = mixed[:, block * lanes : (block + 1) * lanes].T.astype(jnp.bfloat16)
            for head in range(heads):
                out_ref[block * inner + side, :, head * HD : (head + 1) * HD] = part[
                    head * TBLOCK : (head + 1) * TBLOCK
                ]


def self_part(own, beside, key_values, rows, inner, heads):
    return pl.pallas_call(
        functools.partial(self_kernel, inner, heads, rows),
        out_shape=jax.ShapeDtypeStruct((inner * rows // TBLOCK, TBLOCK, heads * HD), jnp.bfloat16),
        in_specs=whole(2 + len(key_values)),
        out_specs=whole(1)[0],
        scratch_shapes=[
            pltpu.VMEM((8 * rows, HD), jnp.bfloat16),
            pltpu.VMEM((8 * rows, HD), jnp.bfloat16),
            pltpu.VMEM((HD + stat_rows, 8 * rows), jnp.bfloat16),
            pltpu.VMEM((8, rows * heads), jnp.float32),
            pltpu.VMEM((HD + stat_rows, rows * heads), jnp.float32),
        ],
        compiler_params=pltpu.CompilerParams(vmem_limit_bytes=24 * 2**20),
        name="self_attention",
    )(own, beside, *key_values)


def combine_kernel(inner, heads, gate_ref, mixed_ref, stat_ref, returned_ref, out_ref):
    count = stat_ref.shape[0]
    side = count // inner
    place = lax.rem(lax.axis_index("ctx"), inner)
    gate = jnp.tanh(jnp.full((1, heads * TBLOCK), gate_ref[0], jnp.float32))
    stats = returned_ref[count * HD :, :].astype(jnp.float32)
    far_stat = stats[:count] + stats[count : 2 * count] + stats[2 * count : 3 * count]
    own_stat = stat_ref[...]
    peak = jnp.maximum(own_stat, far_stat)
    own_weight = jnp.exp2(own_stat - peak)
    far_weight = jnp.exp2(far_stat - peak)
    ratio = gate / (own_weight + far_weight)
    own_weight, far_weight = own_weight * ratio, far_weight * ratio
    for block in range(count):
        target = (block % side) * inner + (place if block < side else 1 - place)
        span = slice(block * HD, (block + 1) * HD)
        mixed = mixed_ref[span, :] * own_weight[block : block + 1] + returned_ref[span, :].astype(
            jnp.float32
        ) * far_weight[block : block + 1]
        part = mixed.T.astype(jnp.bfloat16)
        for head in range(heads):
            out_ref[target, :, head * HD : (head + 1) * HD] = part[
                head * TBLOCK : (head + 1) * TBLOCK
            ]


def combine(gate_scale, mixed, stat, returned, inner, heads):
    return pl.pallas_call(
        functools.partial(combine_kernel, inner, heads),
        out_shape=jax.ShapeDtypeStruct((stat.shape[0], TBLOCK, heads * HD), jnp.bfloat16),
        in_specs=[pl.BlockSpec(memory_space=pltpu.SMEM)] + whole(3),
        out_specs=whole(1)[0],
        compiler_params=pltpu.CompilerParams(vmem_limit_bytes=16 * 2**20),
        name="combine_planes",
    )(gate_scale, mixed, stat, returned)


def spread_kernel(in_ref, out_ref):
    group = in_ref.shape[2]
    for head in range(in_ref.shape[0]):
        out_ref[:, head * group : (head + 1) * group] = in_ref[head]


def spread(inward):
    count, rows, columns = inward.shape
    return pl.pallas_call(
        spread_kernel,
        out_shape=jax.ShapeDtypeStruct((rows, count * columns), inward.dtype),
        in_specs=whole(1),
        out_specs=whole(1)[0],
        compiler_params=pltpu.CompilerParams(vmem_limit_bytes=16 * 2**20),
        name="spread_heads",
    )(inward)


def on_device_split(
    axes,
    query_self,
    key_self,
    value_self,
    positions,
    query_cross,
    key_vision,
    value_vision,
    media_range,
    gate_scale,
):
    inner = key_self.shape[1] // HD
    heads = query_self.shape[1] // key_self.shape[1]
    rows = query_self.shape[0]
    group = heads * HD
    columns = axes["head"]
    devices = axes["ctx"]
    plane_count = devices // inner

    def place_of(device):
        return device // inner, device % inner

    def send(values, turn, flip, upward=0):
        pairs = []
        for device in range(devices):
            plane, place = place_of(device)
            target = plane ^ turn
            if upward == 0 or target ^ upward < target:
                pairs.append((device, target * inner + (place ^ flip)))
        return lax.ppermute(values, "ctx", pairs)

    exponents = np.arange(HD // 2) * (2.0 / HD)
    frequency = jnp.asarray(np.power(rope_base, -exponents), jnp.float32)
    near_out, across_out, beside_out, own, other, own_self = prepare(
        media_range,
        positions,
        frequency,
        key_vision,
        value_vision,
        query_cross,
        query_self,
        key_self,
        value_self,
        inner,
    )
    partner = send(other, 0, 1)
    near = send(near_out, 1, 0)
    beside = send(beside_out, 0, 1)
    across_out, partner = lax.optimization_barrier((across_out, partner))
    packets = jnp.concatenate([own, partner], axis=0)
    far = send(packets, 2, 0)
    across = send(across_out, 1, 1)
    tail = slice(rows * heads, rows * heads + 2 * rows)
    last = send(jnp.concatenate([own[tail], partner[tail]], axis=0), 3, 0, upward=3)

    queries = (own, partner, far)
    count = own.shape[0]
    table = [values[count - TBLOCK, : 2 * (rows // TBLOCK)] for values in queries]
    table.append(far[2 * count - TBLOCK, : 2 * (rows // TBLOCK)])
    first_table = jnp.concatenate(table[:2]).astype(jnp.int32)
    table = jnp.concatenate(table).astype(jnp.int32)
    frames = (near_out, beside, near, across)
    sizes = (rows, inner, heads)
    units = ((0, (0, 2)), (1, (0, 2)), (2, ()), (3, ()))
    state = cross_part(first_table, queries, frames, units, (), "state", *sizes)
    units = ((0, ()), (1, ()), (2, (0, 2)), (3, (0, 2)))
    state = cross_part(table, queries, frames, units, state, "state", *sizes)
    units = ((0, (1,)), (1, (1,)), (2, (1,)), (3, (1,)))
    state = cross_part(table, queries, frames, units, state, "state", *sizes)
    state, last = lax.optimization_barrier((state, last))
    units = ((2, (3,)), (3, (3,)))
    (outgoing,) = cross_part(table, queries, frames, units, state, "packed", *sizes)
    returned = send(outgoing, 2, 0)
    outgoing, table, own_self = lax.optimization_barrier((outgoing, table, own_self))
    units = ((0, (3,)), (1, (3,)))
    mixed, stat = cross_part(table, queries, frames, units, state, "own", *sizes)
    self_rows = self_part(
        own_self, beside, (own, partner, near, across, far, last), *sizes
    )
    planes = [
        [
            (plane * inner + place) * columns + column
            for column in range(columns)
            for place in range(inner)
        ]
        for plane in range(plane_count)
    ]

    def exchange(outward):
        inward = lax.all_to_all(
            outward.reshape(-1, outward.shape[2]),
            ("ctx", "head"),
            0,
            0,
            axis_index_groups=planes,
            tiled=True,
        )
        return spread(inward.reshape(outward.shape))

    self_context = exchange(self_rows)
    cross_context = exchange(combine(gate_scale, mixed, stat, returned, inner, heads))
    return self_context, cross_context


def on_device(axes, *arguments):
    query_self, key_self, _, _, _, key_vision, _, media_range, _ = arguments
    inner = key_self.shape[1] // HD
    heads = query_self.shape[1] // key_self.shape[1]
    rows = query_self.shape[0]
    suited = (
        inner == 2
        and axes["ctx"] == 4 * inner
        and heads * TBLOCK == HD
        and key_vision.shape[0] == FRAME_LEN
        and rows == axes["head"] * TBLOCK
        and media_range.shape[0] * TBLOCK == rows
    )
    if suited:
        return on_device_split(axes, *arguments)
    return on_device_gathered(*arguments)


def solution(mesh):
    placed = (
        P("ctx", "head"),
        P("ctx", "head"),
        P("ctx", "head"),
        P("ctx"),
        P("ctx", "head"),
        P("ctx", "head"),
        P("ctx", "head"),
        P("ctx", None),
        P(),
    )
    return jax.shard_map(
        functools.partial(on_device, dict(mesh.shape)),
        mesh=mesh,
        in_specs=placed,
        out_specs=(P(("ctx", "head"), None), P(("ctx", "head"), None)),
        check_vma=False,
    )
```

```python
import functools

import jax
import jax.numpy as jnp
import numpy as np
from jax import lax
from jax.experimental import pallas as pl
from jax.experimental.pallas import tpu as pltpu
from jax.sharding import PartitionSpec as P

HD = 128
TBLOCK = 16
FRAME_LEN = 896


rope_base = 500000.0
lowest = -1e30


def rotate(values, positions):
    half_width = values.shape[-1] // 2
    exponents = jnp.arange(half_width, dtype=jnp.float32) * (2.0 / values.shape[-1])
    frequency = jnp.power(rope_base, -exponents)
    angles = positions.astype(jnp.float32)[:, None] * frequency[None, :]
    cosine = jnp.cos(angles)[:, None, :]
    sine_part = jnp.sin(angles)[:, None, :]
    first_half = values[..., :half_width]
    second_half = values[..., half_width:]
    return jnp.concatenate(
        [
            first_half * cosine - second_half * sine_part,
            second_half * cosine + first_half * sine_part,
        ],
        axis=-1,
    )


def key_block(key_count):
    block_size = min(key_count, 1024)
    while key_count % block_size != 0:
        block_size = block_size - 1
    return block_size


def attend_block(state_in, queries, key_rows, value_rows, allowed):
    maxima, totals, accumulated = state_in
    scale_factor = queries.shape[-1] ** (-0.5)
    scores = (
        jnp.einsum("rkgd,nkd->kgrn", queries, key_rows, preferred_element_type=jnp.float32)
        * scale_factor
    )
    visible = allowed[None, None, :, :]
    scores = jnp.where(visible, scores, lowest)
    new_maxima = jnp.maximum(maxima, jnp.max(scores, axis=-1))
    weights = jnp.where(visible, jnp.exp(scores - new_maxima[..., None]), 0.0)
    factor = jnp.exp(maxima - new_maxima)
    totals = totals * factor + jnp.sum(weights, axis=-1)
    accumulated = accumulated * factor[..., None] + jnp.einsum(
        "kgrn,nkd->kgrd",
        weights.astype(jnp.bfloat16),
        value_rows,
        preferred_element_type=jnp.float32,
    )
    return (new_maxima, totals, accumulated)


def attend(state_in, queries, key_rows, value_rows, allowed):
    key_count = key_rows.shape[0]
    block_size = key_block(key_count)
    if block_size == key_count:
        return attend_block(state_in, queries, key_rows, value_rows, allowed)

    def step_block(block_index, state_now):
        row_begin = block_index * block_size
        key_part = lax.dynamic_slice_in_dim(key_rows, row_begin, block_size, 0)
        value_part = lax.dynamic_slice_in_dim(value_rows, row_begin, block_size, 0)
        allowed_part = lax.dynamic_slice_in_dim(allowed, row_begin, block_size, 1)
        return attend_block(state_now, queries, key_part, value_part, allowed_part)

    return lax.fori_loop(0, key_count // block_size, step_block, state_in)


def keep_state(current):
    return current


def empty_state(row_count, kv_heads, group_size, head_size):
    maxima = jnp.full((kv_heads, group_size, row_count), lowest, jnp.float32)
    totals = jnp.zeros((kv_heads, group_size, row_count), jnp.float32)
    accumulated = jnp.zeros((kv_heads, group_size, row_count, head_size), jnp.float32)
    return (maxima, totals, accumulated)


def finish(state_in):
    maxima, totals, accumulated = state_in
    safe_totals = jnp.where(totals > 0.0, totals, 1.0)
    result = accumulated / safe_totals[..., None]
    kv_heads, group_size, row_count, head_size = result.shape
    return jnp.transpose(result, (2, 0, 1, 3)).reshape(row_count, kv_heads * group_size * head_size)


def causal_group(current, group, key_rows, value_rows, key_index, offset):
    queries, row_index = group
    allowed = key_index[None, :] <= row_index[:, None]

    def causal_compute(state_in):
        return attend(state_in, queries, key_rows, value_rows, allowed)

    return lax.cond(offset <= jnp.max(row_index), causal_compute, keep_state, current)


def frame_mask(frame_index, lower_frame, upper_frame):
    return jnp.logical_and(
        frame_index[None, :] >= lower_frame[:, None], frame_index[None, :] < upper_frame[:, None]
    )


def on_device_gathered(
    query_self,
    key_self,
    value_self,
    positions,
    query_cross,
    key_vision,
    value_vision,
    media_range,
    gate_scale,
):
    head_size = HD
    kv_heads = key_self.shape[1] // head_size
    group_size = query_self.shape[1] // key_self.shape[1]
    row_count = query_self.shape[0]
    vision_count = key_vision.shape[0]
    device = lax.axis_index("ctx")
    own_rows = device * row_count + jnp.arange(row_count, dtype=jnp.int32)
    rotated_query = rotate(
        query_self.astype(jnp.float32).reshape(row_count, kv_heads * group_size, head_size),
        positions,
    )
    rotated_query = rotated_query.astype(jnp.bfloat16).reshape(
        row_count, kv_heads, group_size, head_size
    )
    rotated_key = rotate(
        key_self.astype(jnp.float32).reshape(row_count, kv_heads, head_size), positions
    ).astype(jnp.bfloat16)
    self_values = value_self.reshape(row_count, kv_heads, head_size)
    vision_keys = key_vision.reshape(vision_count, kv_heads, head_size)
    vision_values = value_vision.reshape(vision_count, kv_heads, head_size)
    cross_queries = query_cross.reshape(row_count, kv_heads, group_size, head_size)
    lower_frame = jnp.repeat(media_range[:, 0], TBLOCK)
    upper_frame = jnp.repeat(media_range[:, 1], TBLOCK)
    has_frames = upper_frame > lower_frame
    query_groups = ((rotated_query, own_rows),)
    self_start = tuple(
        (empty_state(group[1].shape[0], kv_heads, group_size, head_size) for group in query_groups)
    )
    cross_start = empty_state(row_count, kv_heads, group_size, head_size)
    offset = jnp.int32(0)
    key_rows = lax.all_gather(rotated_key, "ctx", axis=0, tiled=True)
    value_rows = lax.all_gather(self_values, "ctx", axis=0, tiled=True)
    key_index = jnp.arange(key_rows.shape[0], dtype=jnp.int32)
    updated = []
    for current, group in zip(self_start, query_groups):
        updated.append(causal_group(current, group, key_rows, value_rows, key_index, offset))
    self_states = tuple(updated)
    key_rows = lax.all_gather(vision_keys, "ctx", axis=0, tiled=True)
    value_rows = lax.all_gather(vision_values, "ctx", axis=0, tiled=True)
    frame_index = jnp.arange(key_rows.shape[0], dtype=jnp.int32) // FRAME_LEN
    allowed = frame_mask(frame_index, lower_frame, upper_frame)
    touching = jnp.logical_and(lower_frame <= frame_index[-1], upper_frame > frame_index[0])
    needed = jnp.any(jnp.logical_and(has_frames, touching))

    def fold_compute(state_in):
        return attend(state_in, cross_queries, key_rows, value_rows, allowed)

    cross_state = lax.cond(needed, fold_compute, keep_state, cross_start)
    self_rows = finish(self_states[0]).astype(jnp.bfloat16)
    cross_rows = jnp.where(
        has_frames[:, None], jnp.tanh(gate_scale[0]) * finish(cross_state), 0.0
    ).astype(jnp.bfloat16)
    self_context, cross_context = (
        lax.all_to_all(self_rows, "head", split_axis=0, concat_axis=1, tiled=True),
        lax.all_to_all(cross_rows, "head", split_axis=0, concat_axis=1, tiled=True),
    )
    return (self_context, cross_context)


log2e = 1.4426950408889634
stat_rows = 16
score_limit = 100.0
unseen = -1e30
contract_last = (((1,), (1,)), ((), ()))


def whole(count):
    return [pl.BlockSpec(memory_space=pltpu.VMEM)] * count


def largest_square(values):
    sums = lax.dot_general(
        jnp.ones((8, values.shape[1]), jnp.bfloat16),
        values * values,
        contract_last,
        preferred_element_type=jnp.float32,
    )
    return jnp.max(jnp.max(sums, axis=0, keepdims=True), axis=1, keepdims=True)


def prepare_kernel(
    inner,
    first,
    range_ref,
    position_ref,
    frequency_ref,
    vision_key_ref,
    vision_value_ref,
    cross_ref,
    query_ref,
    key_ref,
    value_ref,
    *refs,
):
    if first:
        vision_out, packet_out = refs[:2]
    else:
        vision_out, packet_out, self_out, across_out = refs[:4]
    position_row, frequency_row, vision_rows, cross_rows, query_rows, key_rows = refs[-12:-6]
    value_rows, packet_rows, self_rows, pair_rows, in_semaphores, out_semaphores = refs[-6:]
    rows, group = cross_rows.shape
    heads = group // HD
    vision = vision_key_ref.shape[0]
    stacked = heads * rows
    place = lax.rem(lax.axis_index("ctx"), inner)
    sides = (place, 1 - place)
    vision_side, packet_side = (sides[0], sides[1]) if first else (sides[1], sides[0])

    def head_columns(head):
        return pl.ds(pl.multiple_of(head * HD, HD), HD)

    def load(source, target):
        copy = pltpu.make_async_copy(source, target, in_semaphores.at[len(loads)])
        copy.start()
        loads.append(copy)

    def store(source, target):
        copy = pltpu.make_async_copy(source, target, out_semaphores.at[len(stores)])
        copy.start()
        stores.append(copy)

    loads, stores = [], []
    load(position_ref, position_row)
    load(frequency_ref, frequency_row)
    load(cross_ref.at[:, pl.ds(pl.multiple_of(packet_side * group, group), group)], cross_rows)
    load(key_ref, key_rows)
    load(value_ref, value_rows)
    for slot, source in enumerate((vision_key_ref, vision_value_ref)):
        load(
            source.at[:, head_columns(vision_side)], vision_rows.at[pl.ds(slot * vision, vision), :]
        )
    if not first:
        load(query_ref, query_rows)

    def stack(target, head, block):
        for step in range(rows // TBLOCK):
            row = (step * heads + head) * TBLOCK
            target[row : row + TBLOCK, :] = block[step * TBLOCK : (step + 1) * TBLOCK]

    lane = lax.broadcasted_iota(jnp.int32, (TBLOCK, HD), 1)
    ranges = jnp.zeros((TBLOCK, HD), jnp.int32)
    for item in range(2 * rows // TBLOCK):
        ranges = jnp.where(lane == item, range_ref[item % 2, item // 2], ranges)
    ranges = ranges.astype(jnp.float32)
    for copy in loads[:2]:
        copy.wait()
    place_of_row = jnp.broadcast_to(position_row[...].astype(jnp.float32), (HD, rows)).T
    frequency = jnp.concatenate([frequency_row[...]] * 2, axis=1)
    angles = place_of_row * frequency
    cosine = jnp.cos(angles)
    column = lax.broadcasted_iota(jnp.int32, angles.shape, 1)
    sine = jnp.sin(angles) * jnp.where(column < HD // 2, -1.0, 1.0)

    def turned(block):
        block = block.astype(jnp.float32)
        return (block * cosine + pltpu.roll(block, HD // 2, 1) * sine).astype(jnp.bfloat16)

    for copy in loads[2:5]:
        copy.wait()
    for head in range(heads):
        stack(packet_rows, head, cross_rows[:, head * HD : (head + 1) * HD])
    packet_rows[stacked : stacked + rows, :] = turned(key_rows[:, head_columns(packet_side)])
    packet_rows[stacked + rows : stacked + 2 * rows, :] = value_rows[:, head_columns(packet_side)]
    largest = largest_square(packet_rows[:stacked, :]) * 1.02 + 2.0
    ranges = jnp.where(lane == 2 * rows // TBLOCK, largest, ranges).astype(jnp.bfloat16)
    packet_rows[stacked + 2 * rows :, :] = ranges
    store(packet_rows, packet_out)
    with_self = vision_out if first else across_out
    pair_rows[:rows, :] = turned(key_rows[:, head_columns(vision_side)])
    pair_rows[rows:, :] = value_rows[:, head_columns(vision_side)]
    store(pair_rows, with_self.at[pl.ds(2 * vision, 2 * rows), :])
    for slot, copy in enumerate(loads[5:7]):
        span = pl.ds(slot * vision, vision)
        copy.wait()
        store(vision_rows.at[span, :], vision_out.at[span, :])
        if not first:
            store(vision_rows.at[span, :], across_out.at[span, :])
    if not first:
        loads[7].wait()
        tails = (vision_out.at[pl.ds(2 * vision, stacked), :], self_out)
        for side, target in zip((1, 0), tails):
            part = self_rows.at[pl.ds(side * stacked, stacked), :]
            for head in range(heads):
                stack(part, head, turned(query_rows[:, head_columns(sides[side] * heads + head)]))
            store(part, target)
    for copy in stores:
        copy.wait()


def prepare(ranges, positions, frequency, vision_keys, vision_values, cross, query, key, value, inner, first):
    rows, columns = query.shape
    group = columns // inner
    stacked = rows * (group // HD)
    vision = vision_keys.shape[0]
    packet = stacked + 2 * rows + TBLOCK
    counts = [2 * vision + 2 * rows, packet]
    if not first:
        counts = [2 * vision + stacked, packet, stacked, 2 * vision + 2 * rows]
    return pl.pallas_call(
        functools.partial(prepare_kernel, inner, first),
        out_shape=[jax.ShapeDtypeStruct((count, HD), jnp.bfloat16) for count in counts],
        in_specs=[pl.BlockSpec(memory_space=pltpu.SMEM)]
        + [pl.BlockSpec(memory_space=pl.ANY)] * 8,
        out_specs=[pl.BlockSpec(memory_space=pl.ANY)] * len(counts),
        scratch_shapes=[
            pltpu.VMEM((1, rows), jnp.int32),
            pltpu.VMEM((1, HD // 2), jnp.float32),
            pltpu.VMEM((2 * vision, HD), jnp.bfloat16),
            pltpu.VMEM((rows, group), jnp.bfloat16),
            pltpu.VMEM(query.shape, jnp.bfloat16),
            pltpu.VMEM(key.shape, jnp.bfloat16),
            pltpu.VMEM(value.shape, jnp.bfloat16),
            pltpu.VMEM((packet, HD), jnp.bfloat16),
            pltpu.VMEM((2 * stacked, HD), jnp.bfloat16),
            pltpu.VMEM((2 * rows, HD), jnp.bfloat16),
            pltpu.SemaphoreType.DMA((8,)),
            pltpu.SemaphoreType.DMA((8,)),
        ],
        compiler_params=pltpu.CompilerParams(vmem_limit_bytes=60 * 2**20),
        name="prepare_first" if first else "prepare_second",
    )(
        jnp.transpose(ranges),
        positions.reshape(1, rows),
        frequency.reshape(1, HD // 2),
        vision_keys,
        vision_values,
        cross,
        query,
        key,
        value,
    )


def fold_keys(keys, values_turned, jobs, bounded=False):
    scale = HD**-0.5 * log2e
    spans = []
    for job in jobs:
        width = min(256, job[0].shape[0])
        for begin in range(0, job[0].shape[0], width):
            spans.append((job, slice(begin, begin + width)))
    scores = [
        lax.dot_general(
            keys, stacked_ref[span, :], contract_last, preferred_element_type=jnp.float32
        )
        for (stacked_ref, _, _, _), span in spans
    ]
    for ((_, peak_ref, total_ref, visible), span), score in zip(spans, scores):
        peak = peak_ref[0:1, span]
        seen = visible[:, span]
        if seen.shape[0] == 1:
            highest = 0.0 if bounded else jnp.max(score, axis=0, keepdims=True) * scale
            new_peak = jnp.where(seen, jnp.maximum(peak, highest), peak)
            weights = jnp.exp2(score * scale - jnp.where(seen, new_peak, -unseen))
        else:
            score = jnp.where(seen, score * scale, unseen)
            new_peak = jnp.maximum(peak, jnp.max(score, axis=0, keepdims=True))
            weights = jnp.where(seen, jnp.exp2(score - new_peak), 0.0)
        total_ref[:, span] = total_ref[:, span] * jnp.exp2(peak - new_peak) + jnp.dot(
            values_turned, weights.astype(jnp.bfloat16), preferred_element_type=jnp.float32
        )
        peak_ref[0:1, span] = new_peak


def clear(peak_ref, total_ref):
    peak_ref[...] = jnp.full(peak_ref.shape, unseen, jnp.float32)
    total_ref[...] = jnp.zeros(total_ref.shape, jnp.float32)


def finish_columns(peak_ref, total_ref):
    sums = total_ref[HD : HD + 1, :]
    some = sums > 0.0
    safe = jnp.where(some, sums, 1.0)
    log_sum = jnp.where(some, peak_ref[0:1, :] + jnp.log2(safe), unseen)
    return total_ref[:HD, :] / safe, log_sum


def turn_values(value, target_ref):
    target_ref[:HD, :] = value.T
    target_ref[HD:, :] = jnp.ones((stat_rows, target_ref.shape[1]), jnp.bfloat16)


def frame_numbers(inner):
    device = lax.axis_index("ctx")
    plane, place = device // inner, lax.rem(device, inner)
    near = plane + 1 - 2 * lax.rem(plane, 2)
    return (
        plane * inner + place,
        plane * inner + 1 - place,
        near * inner + place,
        near * inner + 1 - place,
    )


def cross_kernel(inner, heads, columns, places, units, chosen, resumed, finish, table_ref, *refs):
    refs = list(refs)
    arrays = sorted({places[number][0] for number, frames in units if frames})
    arrays = {array: refs.pop(0) for array in arrays}
    query_refs = {}
    for number, frames in units:
        if frames:
            array, row = places[number]
            query_refs[number] = arrays[array].at[pl.ds(row, columns), :]
    frame_refs = [refs.pop(0) for _ in chosen]
    state_refs = [refs.pop(0) for _ in range(2)] if resumed else None
    out_refs, (turned_ref, peaks_ref, totals_ref) = refs[:-3], refs[-3:]
    if finish == "state":
        peaks_ref, totals_ref = out_refs
    lanes = heads * TBLOCK
    blocks = columns // lanes
    frames = frame_numbers(inner)
    vision = turned_ref.shape[2]
    for turn, (number, _) in enumerate(units):
        if resumed:
            peaks_ref[turn] = state_refs[0][number]
            totals_ref[turn] = state_refs[1][number]
        else:
            clear(peaks_ref.at[turn], totals_ref.at[turn])

    def job(turn, number, flags):
        visible = jnp.concatenate([jnp.full((1, lanes), flag, jnp.int32) for flag in flags], axis=1)
        return query_refs[number], peaks_ref.at[turn], totals_ref.at[turn], visible > 0

    for slot, index in enumerate(chosen):
        turn_values(frame_refs[slot][vision : 2 * vision, :], turned_ref.at[slot])
        keys = frame_refs[slot][:vision, :]
        limit = largest_square(keys)[0, 0] * (1.05 * (HD**-0.5 * log2e / score_limit) ** 2)
        members = []
        for turn, (number, indices) in enumerate(units):
            if index not in indices:
                continue
            flags = []
            for block in range(blocks):
                at = number * (2 * blocks + 1) + 2 * block
                inside = jnp.logical_and(
                    table_ref[at] <= frames[index], frames[index] < table_ref[at + 1]
                )
                flags.append(inside.astype(jnp.int32))
            needed = functools.reduce(jnp.maximum, flags)
            square = table_ref[number * (2 * blocks + 1) + 2 * blocks].astype(jnp.float32)
            bounded = (square * limit < 1.0).astype(jnp.int32)
            members.append((turn, number, flags, needed * bounded, needed * (1 - bounded)))

        def fold(taken, bounded):
            jobs = [job(turn, number, flags) for turn, number, flags, _, _ in taken]
            fold_keys(frame_refs[slot][:vision, :], turned_ref[slot], jobs, bounded)

        for begin in range(0, len(members), 2):
            pair = members[begin : begin + 2]
            count = sum(member[3] for member in pair)
            if len(pair) == 2:
                pl.when(count == 2)(functools.partial(fold, pair, True))
            for member in pair:
                alone = jnp.logical_and(count == 1, member[3] == 1)
                pl.when(alone)(functools.partial(fold, [member], True))
                pl.when(member[4] == 1)(functools.partial(fold, [member], False))

    if finish == "state":
        return
    stats = []
    for turn in range(len(units)):
        mixed, log_sum = finish_columns(peaks_ref.at[turn], totals_ref.at[turn])
        for block in range(blocks):
            span = slice(block * lanes, (block + 1) * lanes)
            stats.append(log_sum[:, span])
            row = (turn * blocks + block) * HD
            out_refs[0][row : row + HD, :] = mixed[:, span].astype(out_refs[0].dtype)
    stat = jnp.concatenate(stats, axis=0)
    if finish == "packed":
        high = stat.astype(jnp.bfloat16)
        rest = stat - high.astype(jnp.float32)
        middle = rest.astype(jnp.bfloat16)
        low = rest - middle.astype(jnp.float32)
        rows = [high.astype(jnp.float32), middle.astype(jnp.float32), low, jnp.zeros_like(stat)]
        out_refs[0][len(stats) * HD :, :] = jnp.concatenate(rows, axis=0).astype(jnp.bfloat16)
    else:
        out_refs[1][...] = stat


def cross_part(table, queries, frames, units, state, finish, rows, inner, heads):
    lanes = heads * TBLOCK
    columns = rows * heads
    vision = FRAME_LEN
    count = len(units) * (rows // TBLOCK)
    chosen = tuple(sorted({index for _, indices in units for index in indices}))
    if finish == "state":
        out_shape = (
            jax.ShapeDtypeStruct((len(units), 8, columns), jnp.float32),
            jax.ShapeDtypeStruct((len(units), HD + stat_rows, columns), jnp.float32),
        )
    elif finish == "packed":
        out_shape = (jax.ShapeDtypeStruct((count * HD + 4 * count, lanes), jnp.bfloat16),)
    else:
        out_shape = (
            jax.ShapeDtypeStruct((count * HD, lanes), jnp.float32),
            jax.ShapeDtypeStruct((count, lanes), jnp.float32),
        )
    packet = columns + 2 * rows + TBLOCK
    places = ((0, 0), (1, 0), (2, 0), (2, packet))
    arrays = sorted({places[number][0] for number, indices in units if indices})
    arguments = [queries[array] for array in arrays]
    arguments += [*(frames[index] for index in chosen), *state]
    return pl.pallas_call(
        functools.partial(
            cross_kernel, inner, heads, columns, places, units, chosen, len(state) > 0, finish
        ),
        out_shape=out_shape,
        in_specs=[pl.BlockSpec(memory_space=pltpu.SMEM)] + whole(len(arguments)),
        out_specs=whole(len(out_shape)),
        scratch_shapes=[
            pltpu.VMEM((len(chosen), HD + stat_rows, vision), jnp.bfloat16),
            pltpu.VMEM((len(units), 8, columns), jnp.float32),
            pltpu.VMEM((len(units), HD + stat_rows, columns), jnp.float32),
        ],
        compiler_params=pltpu.CompilerParams(vmem_limit_bytes=28 * 2**20),
        name="cross_" + finish,
    )(table, *arguments)


def self_kernel(inner, heads, rows, own_ref, beside_ref, *refs):
    key_value_refs, out_ref = refs[:6], refs[6]
    key_ref, value_ref, turned_ref, peak_ref, total_ref = refs[7:]
    device = lax.axis_index("ctx")
    plane, place = device // inner, lax.rem(device, inner)
    lanes = heads * TBLOCK
    columns = rows * heads
    vision = beside_ref.shape[0] - columns
    own_kv, partner_kv, near_kv, across_kv, far_kv, last_kv = key_value_refs
    packet = own_kv.shape[0]
    vision_rows = near_kv.shape[0] - 2 * rows
    tails = [(own_kv, columns), (partner_kv, columns), (near_kv, vision_rows)]
    tails += [(across_kv, vision_rows), (far_kv, columns), (far_kv, packet + columns)]
    tails += [(last_kv, 0), (last_kv, 2 * rows)]
    for slot, (ref, begin) in enumerate(tails):
        span = slice(slot * rows, (slot + 1) * rows)
        key_ref[span, :] = ref[begin : begin + rows, :]
        value_ref[span, :] = ref[begin + rows : begin + 2 * rows, :]
    turn_values(value_ref[...], turned_ref)
    planes = (plane, plane + 1 - 2 * lax.rem(plane, 2), lax.rem(plane + 2, 4), 3 - plane)
    starts = []
    for source in planes:
        starts.append((source * inner + place) * rows)
        starts.append((source * inner + 1 - place) * rows)
    down = lax.broadcasted_iota(jnp.int32, (rows, columns), 0)
    key_index = jnp.concatenate([down + start for start in starts], axis=0)
    across = lax.broadcasted_iota(jnp.int32, key_index.shape, 1)
    token = (across // lanes) * TBLOCK + lax.rem(across, TBLOCK)
    queries = (own_ref, beside_ref.at[pl.ds(vision, columns), :])
    for slot, query_ref in enumerate(queries):
        side = place if slot == 0 else 1 - place
        clear(peak_ref, total_ref)
        visible = key_index <= token + (plane * inner + side) * rows
        fold_keys(key_ref[...], turned_ref[...], [(query_ref, peak_ref, total_ref, visible)])
        mixed, _ = finish_columns(peak_ref, total_ref)
        for block in range(rows // TBLOCK):
            part = mixed[:, block * lanes : (block + 1) * lanes].T.astype(jnp.bfloat16)
            for head in range(heads):
                out_ref[block * inner + side, :, head * HD : (head + 1) * HD] = part[
                    head * TBLOCK : (head + 1) * TBLOCK
                ]


def self_part(own, beside, key_values, rows, inner, heads):
    return pl.pallas_call(
        functools.partial(self_kernel, inner, heads, rows),
        out_shape=jax.ShapeDtypeStruct((inner * rows // TBLOCK, TBLOCK, heads * HD), jnp.bfloat16),
        in_specs=whole(2 + len(key_values)),
        out_specs=whole(1)[0],
        scratch_shapes=[
            pltpu.VMEM((8 * rows, HD), jnp.bfloat16),
            pltpu.VMEM((8 * rows, HD), jnp.bfloat16),
            pltpu.VMEM((HD + stat_rows, 8 * rows), jnp.bfloat16),
            pltpu.VMEM((8, rows * heads), jnp.float32),
            pltpu.VMEM((HD + stat_rows, rows * heads), jnp.float32),
        ],
        compiler_params=pltpu.CompilerParams(vmem_limit_bytes=24 * 2**20),
        name="self_attention",
    )(own, beside, *key_values)


def combine_kernel(inner, heads, gate_ref, mixed_ref, stat_ref, returned_ref, out_ref):
    count = stat_ref.shape[0]
    side = count // inner
    place = lax.rem(lax.axis_index("ctx"), inner)
    gate = jnp.tanh(jnp.full((1, heads * TBLOCK), gate_ref[0], jnp.float32))
    stats = returned_ref[count * HD :, :].astype(jnp.float32)
    far_stat = stats[:count] + stats[count : 2 * count] + stats[2 * count : 3 * count]
    own_stat = stat_ref[...]
    peak = jnp.maximum(own_stat, far_stat)
    own_weight = jnp.exp2(own_stat - peak)
    far_weight = jnp.exp2(far_stat - peak)
    ratio = gate / (own_weight + far_weight)
    own_weight, far_weight = own_weight * ratio, far_weight * ratio
    for block in range(count):
        target = (block % side) * inner + (place if block < side else 1 - place)
        span = slice(block * HD, (block + 1) * HD)
        mixed = mixed_ref[span, :] * own_weight[block : block + 1] + returned_ref[span, :].astype(
            jnp.float32
        ) * far_weight[block : block + 1]
        part = mixed.T.astype(jnp.bfloat16)
        for head in range(heads):
            out_ref[target, :, head * HD : (head + 1) * HD] = part[
                head * TBLOCK : (head + 1) * TBLOCK
            ]


def combine(gate_scale, mixed, stat, returned, inner, heads):
    return pl.pallas_call(
        functools.partial(combine_kernel, inner, heads),
        out_shape=jax.ShapeDtypeStruct((stat.shape[0], TBLOCK, heads * HD), jnp.bfloat16),
        in_specs=[pl.BlockSpec(memory_space=pltpu.SMEM)] + whole(3),
        out_specs=whole(1)[0],
        compiler_params=pltpu.CompilerParams(vmem_limit_bytes=16 * 2**20),
        name="combine_planes",
    )(gate_scale, mixed, stat, returned)


def spread_kernel(in_ref, out_ref):
    group = in_ref.shape[2]
    for head in range(in_ref.shape[0]):
        out_ref[:, head * group : (head + 1) * group] = in_ref[head]


def spread(inward):
    count, rows, columns = inward.shape
    return pl.pallas_call(
        spread_kernel,
        out_shape=jax.ShapeDtypeStruct((rows, count * columns), inward.dtype),
        in_specs=whole(1),
        out_specs=whole(1)[0],
        compiler_params=pltpu.CompilerParams(vmem_limit_bytes=16 * 2**20),
        name="spread_heads",
    )(inward)


def on_device_split(
    axes,
    query_self,
    key_self,
    value_self,
    positions,
    query_cross,
    key_vision,
    value_vision,
    media_range,
    gate_scale,
):
    inner = key_self.shape[1] // HD
    heads = query_self.shape[1] // key_self.shape[1]
    rows = query_self.shape[0]
    group = heads * HD
    columns = axes["head"]
    devices = axes["ctx"]
    plane_count = devices // inner

    def place_of(device):
        return device // inner, device % inner

    def send(values, turn, flip, upward=0):
        pairs = []
        for device in range(devices):
            plane, place = place_of(device)
            target = plane ^ turn
            if upward == 0 or target ^ upward < target:
                pairs.append((device, target * inner + (place ^ flip)))
        return lax.ppermute(values, "ctx", pairs)

    exponents = np.arange(HD // 2) * (2.0 / HD)
    frequency = jnp.asarray(np.power(rope_base, -exponents), jnp.float32)
    sources = (positions, frequency, key_vision, value_vision, query_cross, query_self, key_self)
    near_out, other = prepare(media_range, *sources, value_self, inner, True)
    partner = send(other, 0, 1)
    near = send(near_out, 1, 0)
    value_self, near_out, other = lax.optimization_barrier((value_self, near_out, other))
    beside_out, own, own_self, across_out = prepare(media_range, *sources, value_self, inner, False)
    beside = send(beside_out, 0, 1)
    packets = jnp.concatenate([own, partner], axis=0)
    far = send(packets, 2, 0)
    across_out, partner = lax.optimization_barrier((across_out, partner))
    across = send(across_out, 1, 1)
    tail = slice(rows * heads, rows * heads + 2 * rows)
    last = send(jnp.concatenate([own[tail], partner[tail]], axis=0), 3, 0, upward=3)

    queries = (own, partner, far)
    count = own.shape[0]
    table = [values[count - TBLOCK, : 2 * (rows // TBLOCK) + 1] for values in queries]
    table.append(far[2 * count - TBLOCK, : 2 * (rows // TBLOCK) + 1])
    first_table = jnp.concatenate(table[:2]).astype(jnp.int32)
    table = jnp.concatenate(table).astype(jnp.int32)
    frames = (near_out, beside, near, across)
    sizes = (rows, inner, heads)
    units = ((0, (0, 2)), (1, (0, 2)), (2, ()), (3, ()))
    state = cross_part(first_table, queries, frames, units, (), "state", *sizes)
    units = ((0, ()), (1, ()), (2, (0, 2)), (3, (0, 2)))
    state = cross_part(table, queries, frames, units, state, "state", *sizes)
    units = ((0, (1,)), (1, (1,)), (2, (1,)), (3, (1,)))
    state = cross_part(table, queries, frames, units, state, "state", *sizes)
    units = ((2, (3,)), (3, (3,)))
    (outgoing,) = cross_part(table, queries, frames, units, state, "packed", *sizes)
    outgoing, last = lax.optimization_barrier((outgoing, last))
    returned = send(outgoing, 2, 0)
    outgoing, table, own_self = lax.optimization_barrier((outgoing, table, own_self))
    units = ((0, (3,)), (1, (3,)))
    mixed, stat = cross_part(table, queries, frames, units, state, "own", *sizes)
    self_rows = self_part(
        own_self, beside, (own, partner, near, across, far, last), *sizes
    )
    planes = [
        [
            (plane * inner + place) * columns + column
            for column in range(columns)
            for place in range(inner)
        ]
        for plane in range(plane_count)
    ]

    def exchange(outward):
        inward = lax.all_to_all(
            outward.reshape(-1, outward.shape[2]),
            ("ctx", "head"),
            0,
            0,
            axis_index_groups=planes,
            tiled=True,
        )
        return spread(inward.reshape(outward.shape))

    self_context = exchange(self_rows)
    cross_context = exchange(combine(gate_scale, mixed, stat, returned, inner, heads))
    return self_context, cross_context


def on_device(axes, *arguments):
    query_self, key_self, _, _, _, key_vision, _, media_range, _ = arguments
    inner = key_self.shape[1] // HD
    heads = query_self.shape[1] // key_self.shape[1]
    rows = query_self.shape[0]
    suited = (
        inner == 2
        and axes["ctx"] == 4 * inner
        and heads * TBLOCK == HD
        and key_vision.shape[0] == FRAME_LEN
        and rows == axes["head"] * TBLOCK
        and media_range.shape[0] * TBLOCK == rows
    )
    if suited:
        return on_device_split(axes, *arguments)
    return on_device_gathered(*arguments)


def solution(mesh):
    placed = (
        P("ctx", "head"),
        P("ctx", "head"),
        P("ctx", "head"),
        P("ctx"),
        P("ctx", "head"),
        P("ctx", "head"),
        P("ctx", "head"),
        P("ctx", None),
        P(),
    )
    return jax.shard_map(
        functools.partial(on_device, dict(mesh.shape)),
        mesh=mesh,
        in_specs=placed,
        out_specs=(P(("ctx", "head"), None), P(("ctx", "head"), None)),
        check_vma=False,
    )
```

```python
import functools

import jax
import jax.numpy as jnp
import numpy as np
from jax import lax
from jax.experimental import pallas as pl
from jax.experimental.pallas import tpu as pltpu
from jax.sharding import PartitionSpec as P

HD = 128
TBLOCK = 16
FRAME_LEN = 896


rope_base = 500000.0
lowest = -1e30


def rotate(values, positions):
    half_width = values.shape[-1] // 2
    exponents = jnp.arange(half_width, dtype=jnp.float32) * (2.0 / values.shape[-1])
    frequency = jnp.power(rope_base, -exponents)
    angles = positions.astype(jnp.float32)[:, None] * frequency[None, :]
    cosine = jnp.cos(angles)[:, None, :]
    sine_part = jnp.sin(angles)[:, None, :]
    first_half = values[..., :half_width]
    second_half = values[..., half_width:]
    return jnp.concatenate(
        [
            first_half * cosine - second_half * sine_part,
            second_half * cosine + first_half * sine_part,
        ],
        axis=-1,
    )


def key_block(key_count):
    block_size = min(key_count, 1024)
    while key_count % block_size != 0:
        block_size = block_size - 1
    return block_size


def attend_block(state_in, queries, key_rows, value_rows, allowed):
    maxima, totals, accumulated = state_in
    scale_factor = queries.shape[-1] ** (-0.5)
    scores = (
        jnp.einsum("rkgd,nkd->kgrn", queries, key_rows, preferred_element_type=jnp.float32)
        * scale_factor
    )
    visible = allowed[None, None, :, :]
    scores = jnp.where(visible, scores, lowest)
    new_maxima = jnp.maximum(maxima, jnp.max(scores, axis=-1))
    weights = jnp.where(visible, jnp.exp(scores - new_maxima[..., None]), 0.0)
    factor = jnp.exp(maxima - new_maxima)
    totals = totals * factor + jnp.sum(weights, axis=-1)
    accumulated = accumulated * factor[..., None] + jnp.einsum(
        "kgrn,nkd->kgrd",
        weights.astype(jnp.bfloat16),
        value_rows,
        preferred_element_type=jnp.float32,
    )
    return (new_maxima, totals, accumulated)


def attend(state_in, queries, key_rows, value_rows, allowed):
    key_count = key_rows.shape[0]
    block_size = key_block(key_count)
    if block_size == key_count:
        return attend_block(state_in, queries, key_rows, value_rows, allowed)

    def step_block(block_index, state_now):
        row_begin = block_index * block_size
        key_part = lax.dynamic_slice_in_dim(key_rows, row_begin, block_size, 0)
        value_part = lax.dynamic_slice_in_dim(value_rows, row_begin, block_size, 0)
        allowed_part = lax.dynamic_slice_in_dim(allowed, row_begin, block_size, 1)
        return attend_block(state_now, queries, key_part, value_part, allowed_part)

    return lax.fori_loop(0, key_count // block_size, step_block, state_in)


def keep_state(current):
    return current


def empty_state(row_count, kv_heads, group_size, head_size):
    maxima = jnp.full((kv_heads, group_size, row_count), lowest, jnp.float32)
    totals = jnp.zeros((kv_heads, group_size, row_count), jnp.float32)
    accumulated = jnp.zeros((kv_heads, group_size, row_count, head_size), jnp.float32)
    return (maxima, totals, accumulated)


def finish(state_in):
    maxima, totals, accumulated = state_in
    safe_totals = jnp.where(totals > 0.0, totals, 1.0)
    result = accumulated / safe_totals[..., None]
    kv_heads, group_size, row_count, head_size = result.shape
    return jnp.transpose(result, (2, 0, 1, 3)).reshape(row_count, kv_heads * group_size * head_size)


def causal_group(current, group, key_rows, value_rows, key_index, offset):
    queries, row_index = group
    allowed = key_index[None, :] <= row_index[:, None]

    def causal_compute(state_in):
        return attend(state_in, queries, key_rows, value_rows, allowed)

    return lax.cond(offset <= jnp.max(row_index), causal_compute, keep_state, current)


def frame_mask(frame_index, lower_frame, upper_frame):
    return jnp.logical_and(
        frame_index[None, :] >= lower_frame[:, None], frame_index[None, :] < upper_frame[:, None]
    )


def on_device_gathered(
    query_self,
    key_self,
    value_self,
    positions,
    query_cross,
    key_vision,
    value_vision,
    media_range,
    gate_scale,
):
    head_size = HD
    kv_heads = key_self.shape[1] // head_size
    group_size = query_self.shape[1] // key_self.shape[1]
    row_count = query_self.shape[0]
    vision_count = key_vision.shape[0]
    device = lax.axis_index("ctx")
    own_rows = device * row_count + jnp.arange(row_count, dtype=jnp.int32)
    rotated_query = rotate(
        query_self.astype(jnp.float32).reshape(row_count, kv_heads * group_size, head_size),
        positions,
    )
    rotated_query = rotated_query.astype(jnp.bfloat16).reshape(
        row_count, kv_heads, group_size, head_size
    )
    rotated_key = rotate(
        key_self.astype(jnp.float32).reshape(row_count, kv_heads, head_size), positions
    ).astype(jnp.bfloat16)
    self_values = value_self.reshape(row_count, kv_heads, head_size)
    vision_keys = key_vision.reshape(vision_count, kv_heads, head_size)
    vision_values = value_vision.reshape(vision_count, kv_heads, head_size)
    cross_queries = query_cross.reshape(row_count, kv_heads, group_size, head_size)
    lower_frame = jnp.repeat(media_range[:, 0], TBLOCK)
    upper_frame = jnp.repeat(media_range[:, 1], TBLOCK)
    has_frames = upper_frame > lower_frame
    query_groups = ((rotated_query, own_rows),)
    self_start = tuple(
        (empty_state(group[1].shape[0], kv_heads, group_size, head_size) for group in query_groups)
    )
    cross_start = empty_state(row_count, kv_heads, group_size, head_size)
    offset = jnp.int32(0)
    key_rows = lax.all_gather(rotated_key, "ctx", axis=0, tiled=True)
    value_rows = lax.all_gather(self_values, "ctx", axis=0, tiled=True)
    key_index = jnp.arange(key_rows.shape[0], dtype=jnp.int32)
    updated = []
    for current, group in zip(self_start, query_groups):
        updated.append(causal_group(current, group, key_rows, value_rows, key_index, offset))
    self_states = tuple(updated)
    key_rows = lax.all_gather(vision_keys, "ctx", axis=0, tiled=True)
    value_rows = lax.all_gather(vision_values, "ctx", axis=0, tiled=True)
    frame_index = jnp.arange(key_rows.shape[0], dtype=jnp.int32) // FRAME_LEN
    allowed = frame_mask(frame_index, lower_frame, upper_frame)
    touching = jnp.logical_and(lower_frame <= frame_index[-1], upper_frame > frame_index[0])
    needed = jnp.any(jnp.logical_and(has_frames, touching))

    def fold_compute(state_in):
        return attend(state_in, cross_queries, key_rows, value_rows, allowed)

    cross_state = lax.cond(needed, fold_compute, keep_state, cross_start)
    self_rows = finish(self_states[0]).astype(jnp.bfloat16)
    cross_rows = jnp.where(
        has_frames[:, None], jnp.tanh(gate_scale[0]) * finish(cross_state), 0.0
    ).astype(jnp.bfloat16)
    self_context, cross_context = (
        lax.all_to_all(self_rows, "head", split_axis=0, concat_axis=1, tiled=True),
        lax.all_to_all(cross_rows, "head", split_axis=0, concat_axis=1, tiled=True),
    )
    return (self_context, cross_context)


log2e = 1.4426950408889634
stat_rows = 16
score_limit = 100.0
unseen = -1e30
contract_last = (((1,), (1,)), ((), ()))


def whole(count):
    return [pl.BlockSpec(memory_space=pltpu.VMEM)] * count


def largest_square(values):
    sums = lax.dot_general(
        jnp.ones((8, values.shape[1]), jnp.bfloat16),
        values * values,
        contract_last,
        preferred_element_type=jnp.float32,
    )
    return jnp.max(jnp.max(sums, axis=0, keepdims=True), axis=1, keepdims=True)


def prepare_kernel(
    inner,
    first,
    range_ref,
    position_ref,
    frequency_ref,
    vision_key_ref,
    vision_value_ref,
    cross_ref,
    query_ref,
    key_ref,
    value_ref,
    *refs,
):
    if first:
        vision_out, packet_out = refs[:2]
    else:
        vision_out, packet_out, self_out, across_out = refs[:4]
    range_table, position_row, frequency_row, vision_rows, cross_rows = refs[-13:-8]
    query_rows, key_rows = refs[-8:-6]
    value_rows, packet_rows, self_rows, pair_rows, in_semaphores, out_semaphores = refs[-6:]
    rows, group = cross_rows.shape
    heads = group // HD
    vision = vision_key_ref.shape[0]
    stacked = heads * rows
    place = lax.rem(lax.axis_index("ctx"), inner)
    sides = (place, 1 - place)
    vision_side, packet_side = (sides[0], sides[1]) if first else (sides[1], sides[0])

    def head_columns(head):
        return pl.ds(pl.multiple_of(head * HD, HD), HD)

    def load(source, target):
        copy = pltpu.make_async_copy(source, target, in_semaphores.at[len(loads)])
        copy.start()
        loads.append(copy)

    def store(source, target):
        copy = pltpu.make_async_copy(source, target, out_semaphores.at[len(stores)])
        copy.start()
        stores.append(copy)

    loads, stores = [], []
    load(position_ref, position_row)
    load(frequency_ref, frequency_row)
    load(range_ref, range_table)
    load(cross_ref.at[:, pl.ds(pl.multiple_of(packet_side * group, group), group)], cross_rows)
    load(key_ref, key_rows)
    load(value_ref, value_rows)
    for slot, source in enumerate((vision_key_ref, vision_value_ref)):
        load(
            source.at[:, head_columns(vision_side)], vision_rows.at[pl.ds(slot * vision, vision), :]
        )
    if not first:
        load(query_ref, query_rows)

    def stack(target, head, block):
        for step in range(rows // TBLOCK):
            row = (step * heads + head) * TBLOCK
            target[row : row + TBLOCK, :] = block[step * TBLOCK : (step + 1) * TBLOCK]

    for copy in loads[:2]:
        copy.wait()
    place_of_row = jnp.broadcast_to(position_row[...].astype(jnp.float32), (HD, rows)).T
    frequency = jnp.concatenate([frequency_row[...]] * 2, axis=1)
    angles = place_of_row * frequency
    cosine = jnp.cos(angles)
    column = lax.broadcasted_iota(jnp.int32, angles.shape, 1)
    sine = jnp.sin(angles) * jnp.where(column < HD // 2, -1.0, 1.0)

    def turned(block):
        block = block.astype(jnp.float32)
        return (block * cosine + pltpu.roll(block, HD // 2, 1) * sine).astype(jnp.bfloat16)

    for copy in loads[2:6]:
        copy.wait()
    lane = lax.broadcasted_iota(jnp.int32, (TBLOCK, HD), 1)
    ranges = jnp.zeros((TBLOCK, HD), jnp.int32)
    for item in range(2 * rows // TBLOCK):
        ranges = jnp.where(lane == item, range_table[item % 2, item // 2], ranges)
    ranges = ranges.astype(jnp.float32)
    for head in range(heads):
        stack(packet_rows, head, cross_rows[:, head * HD : (head + 1) * HD])
    packet_rows[stacked : stacked + rows, :] = turned(key_rows[:, head_columns(packet_side)])
    packet_rows[stacked + rows : stacked + 2 * rows, :] = value_rows[:, head_columns(packet_side)]
    largest = largest_square(packet_rows[:stacked, :]) * 1.02 + 2.0
    ranges = jnp.where(lane == 2 * rows // TBLOCK, largest, ranges).astype(jnp.bfloat16)
    packet_rows[stacked + 2 * rows :, :] = ranges
    store(packet_rows, packet_out)
    with_self = vision_out if first else across_out
    pair_rows[:rows, :] = turned(key_rows[:, head_columns(vision_side)])
    pair_rows[rows:, :] = value_rows[:, head_columns(vision_side)]
    store(pair_rows, with_self.at[pl.ds(2 * vision, 2 * rows), :])
    for slot, copy in enumerate(loads[6:8]):
        span = pl.ds(slot * vision, vision)
        copy.wait()
        store(vision_rows.at[span, :], vision_out.at[span, :])
        if not first:
            store(vision_rows.at[span, :], across_out.at[span, :])
    if not first:
        loads[8].wait()
        tails = (vision_out.at[pl.ds(2 * vision, stacked), :], self_out)
        for side, target in zip((1, 0), tails):
            part = self_rows.at[pl.ds(side * stacked, stacked), :]
            for head in range(heads):
                stack(part, head, turned(query_rows[:, head_columns(sides[side] * heads + head)]))
            store(part, target)
    for copy in stores:
        copy.wait()


def prepare(ranges, positions, frequency, vision_keys, vision_values, cross, query, key, value, inner, first):
    rows, columns = query.shape
    group = columns // inner
    stacked = rows * (group // HD)
    vision = vision_keys.shape[0]
    packet = stacked + 2 * rows + TBLOCK
    counts = [2 * vision + 2 * rows, packet]
    if not first:
        counts = [2 * vision + stacked, packet, stacked, 2 * vision + 2 * rows]
    return pl.pallas_call(
        functools.partial(prepare_kernel, inner, first),
        out_shape=[jax.ShapeDtypeStruct((count, HD), jnp.bfloat16) for count in counts],
        in_specs=[pl.BlockSpec(memory_space=pl.ANY)] * 9,
        out_specs=[pl.BlockSpec(memory_space=pl.ANY)] * len(counts),
        scratch_shapes=[
            pltpu.SMEM((2, ranges.shape[0]), jnp.int32),
            pltpu.VMEM((1, rows), jnp.int32),
            pltpu.VMEM((1, HD // 2), jnp.float32),
            pltpu.VMEM((2 * vision, HD), jnp.bfloat16),
            pltpu.VMEM((rows, group), jnp.bfloat16),
            pltpu.VMEM(query.shape, jnp.bfloat16),
            pltpu.VMEM(key.shape, jnp.bfloat16),
            pltpu.VMEM(value.shape, jnp.bfloat16),
            pltpu.VMEM((packet, HD), jnp.bfloat16),
            pltpu.VMEM((2 * stacked, HD), jnp.bfloat16),
            pltpu.VMEM((2 * rows, HD), jnp.bfloat16),
            pltpu.SemaphoreType.DMA((9,)),
            pltpu.SemaphoreType.DMA((8,)),
        ],
        compiler_params=pltpu.CompilerParams(vmem_limit_bytes=60 * 2**20),
        name="prepare_first" if first else "prepare_second",
    )(
        jnp.transpose(ranges),
        positions.reshape(1, rows),
        frequency.reshape(1, HD // 2),
        vision_keys,
        vision_values,
        cross,
        query,
        key,
        value,
    )


def fold_keys(keys, values_turned, jobs, bounded=False):
    scale = HD**-0.5 * log2e
    spans = []
    for job in jobs:
        width = min(256, job[0].shape[0])
        for begin in range(0, job[0].shape[0], width):
            spans.append((job, slice(begin, begin + width)))
    scores = [
        lax.dot_general(
            keys, stacked_ref[span, :], contract_last, preferred_element_type=jnp.float32
        )
        for (stacked_ref, _, _, _), span in spans
    ]
    for ((_, peak_ref, total_ref, visible), span), score in zip(spans, scores):
        peak = peak_ref[0:1, span]
        seen = visible[:, span]
        if seen.shape[0] == 1:
            highest = 0.0 if bounded else jnp.max(score, axis=0, keepdims=True) * scale
            new_peak = jnp.where(seen, jnp.maximum(peak, highest), peak)
            weights = jnp.exp2(score * scale - jnp.where(seen, new_peak, -unseen))
        else:
            score = jnp.where(seen, score * scale, unseen)
            new_peak = jnp.maximum(peak, jnp.max(score, axis=0, keepdims=True))
            weights = jnp.where(seen, jnp.exp2(score - new_peak), 0.0)
        total_ref[:, span] = total_ref[:, span] * jnp.exp2(peak - new_peak) + jnp.dot(
            values_turned, weights.astype(jnp.bfloat16), preferred_element_type=jnp.float32
        )
        peak_ref[0:1, span] = new_peak


def clear(peak_ref, total_ref):
    peak_ref[...] = jnp.full(peak_ref.shape, unseen, jnp.float32)
    total_ref[...] = jnp.zeros(total_ref.shape, jnp.float32)


def finish_columns(peak_ref, total_ref):
    sums = total_ref[HD : HD + 1, :]
    some = sums > 0.0
    safe = jnp.where(some, sums, 1.0)
    log_sum = jnp.where(some, peak_ref[0:1, :] + jnp.log2(safe), unseen)
    return total_ref[:HD, :] / safe, log_sum


def turn_values(value, target_ref):
    target_ref[:HD, :] = value.T
    target_ref[HD:, :] = jnp.ones((stat_rows, target_ref.shape[1]), jnp.bfloat16)


def frame_numbers(inner):
    device = lax.axis_index("ctx")
    plane, place = device // inner, lax.rem(device, inner)
    near = plane + 1 - 2 * lax.rem(plane, 2)
    return (
        plane * inner + place,
        plane * inner + 1 - place,
        near * inner + place,
        near * inner + 1 - place,
    )


def cross_kernel(inner, heads, columns, places, units, chosen, resumed, finish, table_source, *refs):
    refs = list(refs)
    arrays = sorted({places[number][0] for number, frames in units if frames})
    arrays = {array: refs.pop(0) for array in arrays}
    query_refs = {}
    for number, frames in units:
        if frames:
            array, row = places[number]
            query_refs[number] = arrays[array].at[pl.ds(row, columns), :]
    frame_refs = [refs.pop(0) for _ in chosen]
    state_refs = [refs.pop(0) for _ in range(2)] if resumed else None
    out_refs, (turned_ref, peaks_ref, totals_ref, table_ref, semaphore) = refs[:-5], refs[-5:]
    load = pltpu.make_async_copy(table_source, table_ref, semaphore)
    load.start()
    if finish == "state":
        peaks_ref, totals_ref = out_refs
    lanes = heads * TBLOCK
    blocks = columns // lanes
    frames = frame_numbers(inner)
    vision = turned_ref.shape[2]
    for turn, (number, _) in enumerate(units):
        if resumed:
            peaks_ref[turn] = state_refs[0][number]
            totals_ref[turn] = state_refs[1][number]
        else:
            clear(peaks_ref.at[turn], totals_ref.at[turn])

    def job(turn, number, flags):
        visible = jnp.concatenate([jnp.full((1, lanes), flag, jnp.int32) for flag in flags], axis=1)
        return query_refs[number], peaks_ref.at[turn], totals_ref.at[turn], visible > 0

    for slot, index in enumerate(chosen):
        turn_values(frame_refs[slot][vision : 2 * vision, :], turned_ref.at[slot])
        if slot == 0:
            load.wait()
        keys = frame_refs[slot][:vision, :]
        limit = largest_square(keys)[0, 0] * (1.05 * (HD**-0.5 * log2e / score_limit) ** 2)
        members = []
        for turn, (number, indices) in enumerate(units):
            if index not in indices:
                continue
            flags = []
            for block in range(blocks):
                at = number * (2 * blocks + 1) + 2 * block
                inside = jnp.logical_and(
                    table_ref[at] <= frames[index], frames[index] < table_ref[at + 1]
                )
                flags.append(inside.astype(jnp.int32))
            needed = functools.reduce(jnp.maximum, flags)
            square = table_ref[number * (2 * blocks + 1) + 2 * blocks].astype(jnp.float32)
            bounded = (square * limit < 1.0).astype(jnp.int32)
            members.append((turn, number, flags, needed * bounded, needed * (1 - bounded)))

        def fold(taken, bounded):
            jobs = [job(turn, number, flags) for turn, number, flags, _, _ in taken]
            fold_keys(frame_refs[slot][:vision, :], turned_ref[slot], jobs, bounded)

        for begin in range(0, len(members), 2):
            pair = members[begin : begin + 2]
            count = sum(member[3] for member in pair)
            if len(pair) == 2:
                pl.when(count == 2)(functools.partial(fold, pair, True))
            for member in pair:
                alone = jnp.logical_and(count == 1, member[3] == 1)
                pl.when(alone)(functools.partial(fold, [member], True))
                pl.when(member[4] == 1)(functools.partial(fold, [member], False))

    if finish == "state":
        return
    stats = []
    for turn in range(len(units)):
        mixed, log_sum = finish_columns(peaks_ref.at[turn], totals_ref.at[turn])
        for block in range(blocks):
            span = slice(block * lanes, (block + 1) * lanes)
            stats.append(log_sum[:, span])
            row = (turn * blocks + block) * HD
            out_refs[0][row : row + HD, :] = mixed[:, span].astype(out_refs[0].dtype)
    stat = jnp.concatenate(stats, axis=0)
    if finish == "packed":
        high = stat.astype(jnp.bfloat16)
        rest = stat - high.astype(jnp.float32)
        middle = rest.astype(jnp.bfloat16)
        low = rest - middle.astype(jnp.float32)
        rows = [high.astype(jnp.float32), middle.astype(jnp.float32), low, jnp.zeros_like(stat)]
        out_refs[0][len(stats) * HD :, :] = jnp.concatenate(rows, axis=0).astype(jnp.bfloat16)
    else:
        out_refs[1][...] = stat


def cross_part(table, queries, frames, units, state, finish, rows, inner, heads):
    lanes = heads * TBLOCK
    columns = rows * heads
    vision = FRAME_LEN
    count = len(units) * (rows // TBLOCK)
    chosen = tuple(sorted({index for _, indices in units for index in indices}))
    if finish == "state":
        out_shape = (
            jax.ShapeDtypeStruct((len(units), 8, columns), jnp.float32),
            jax.ShapeDtypeStruct((len(units), HD + stat_rows, columns), jnp.float32),
        )
    elif finish == "packed":
        out_shape = (jax.ShapeDtypeStruct((count * HD + 4 * count, lanes), jnp.bfloat16),)
    else:
        out_shape = (
            jax.ShapeDtypeStruct((count * HD, lanes), jnp.float32),
            jax.ShapeDtypeStruct((count, lanes), jnp.float32),
        )
    packet = columns + 2 * rows + TBLOCK
    places = ((0, 0), (1, 0), (2, 0), (2, packet))
    arrays = sorted({places[number][0] for number, indices in units if indices})
    arguments = [queries[array] for array in arrays]
    arguments += [*(frames[index] for index in chosen), *state]
    return pl.pallas_call(
        functools.partial(
            cross_kernel, inner, heads, columns, places, units, chosen, len(state) > 0, finish
        ),
        out_shape=out_shape,
        in_specs=[pl.BlockSpec(memory_space=pl.ANY)] + whole(len(arguments)),
        out_specs=whole(len(out_shape)),
        scratch_shapes=[
            pltpu.VMEM((len(chosen), HD + stat_rows, vision), jnp.bfloat16),
            pltpu.VMEM((len(units), 8, columns), jnp.float32),
            pltpu.VMEM((len(units), HD + stat_rows, columns), jnp.float32),
            pltpu.SMEM(table.shape, jnp.int32),
            pltpu.SemaphoreType.DMA,
        ],
        compiler_params=pltpu.CompilerParams(vmem_limit_bytes=28 * 2**20),
        name="cross_" + finish,
    )(table, *arguments)


def self_kernel(inner, heads, rows, own_ref, beside_ref, *refs):
    key_value_refs, out_ref = refs[:6], refs[6]
    key_ref, value_ref, turned_ref, peak_ref, total_ref = refs[7:]
    device = lax.axis_index("ctx")
    plane, place = device // inner, lax.rem(device, inner)
    lanes = heads * TBLOCK
    columns = rows * heads
    vision = beside_ref.shape[0] - columns
    own_kv, partner_kv, near_kv, across_kv, far_kv, last_kv = key_value_refs
    packet = own_kv.shape[0]
    vision_rows = near_kv.shape[0] - 2 * rows
    tails = [(own_kv, columns), (partner_kv, columns), (near_kv, vision_rows)]
    tails += [(across_kv, vision_rows), (far_kv, columns), (far_kv, packet + columns)]
    tails += [(last_kv, 0), (last_kv, 2 * rows)]
    for slot, (ref, begin) in enumerate(tails):
        span = slice(slot * rows, (slot + 1) * rows)
        key_ref[span, :] = ref[begin : begin + rows, :]
        value_ref[span, :] = ref[begin + rows : begin + 2 * rows, :]
    turn_values(value_ref[...], turned_ref)
    planes = (plane, plane + 1 - 2 * lax.rem(plane, 2), lax.rem(plane + 2, 4), 3 - plane)
    starts = []
    for source in planes:
        starts.append((source * inner + place) * rows)
        starts.append((source * inner + 1 - place) * rows)
    down = lax.broadcasted_iota(jnp.int32, (rows, columns), 0)
    key_index = jnp.concatenate([down + start for start in starts], axis=0)
    across = lax.broadcasted_iota(jnp.int32, key_index.shape, 1)
    token = (across // lanes) * TBLOCK + lax.rem(across, TBLOCK)
    queries = (own_ref, beside_ref.at[pl.ds(vision, columns), :])
    for slot, query_ref in enumerate(queries):
        side = place if slot == 0 else 1 - place
        clear(peak_ref, total_ref)
        visible = key_index <= token + (plane * inner + side) * rows
        fold_keys(key_ref[...], turned_ref[...], [(query_ref, peak_ref, total_ref, visible)])
        mixed, _ = finish_columns(peak_ref, total_ref)
        for block in range(rows // TBLOCK):
            part = mixed[:, block * lanes : (block + 1) * lanes].T.astype(jnp.bfloat16)
            for head in range(heads):
                out_ref[block * inner + side, :, head * HD : (head + 1) * HD] = part[
                    head * TBLOCK : (head + 1) * TBLOCK
                ]


def self_part(own, beside, key_values, rows, inner, heads):
    return pl.pallas_call(
        functools.partial(self_kernel, inner, heads, rows),
        out_shape=jax.ShapeDtypeStruct((inner * rows // TBLOCK, TBLOCK, heads * HD), jnp.bfloat16),
        in_specs=whole(2 + len(key_values)),
        out_specs=whole(1)[0],
        scratch_shapes=[
            pltpu.VMEM((8 * rows, HD), jnp.bfloat16),
            pltpu.VMEM((8 * rows, HD), jnp.bfloat16),
            pltpu.VMEM((HD + stat_rows, 8 * rows), jnp.bfloat16),
            pltpu.VMEM((8, rows * heads), jnp.float32),
            pltpu.VMEM((HD + stat_rows, rows * heads), jnp.float32),
        ],
        compiler_params=pltpu.CompilerParams(vmem_limit_bytes=24 * 2**20),
        name="self_attention",
    )(own, beside, *key_values)


def combine_kernel(inner, heads, gate_ref, mixed_ref, stat_ref, returned_ref, out_ref):
    count = stat_ref.shape[0]
    side = count // inner
    place = lax.rem(lax.axis_index("ctx"), inner)
    gate = jnp.tanh(jnp.full((1, heads * TBLOCK), gate_ref[0], jnp.float32))
    stats = returned_ref[count * HD :, :].astype(jnp.float32)
    far_stat = stats[:count] + stats[count : 2 * count] + stats[2 * count : 3 * count]
    own_stat = stat_ref[...]
    peak = jnp.maximum(own_stat, far_stat)
    own_weight = jnp.exp2(own_stat - peak)
    far_weight = jnp.exp2(far_stat - peak)
    ratio = gate / (own_weight + far_weight)
    own_weight, far_weight = own_weight * ratio, far_weight * ratio
    for block in range(count):
        target = (block % side) * inner + (place if block < side else 1 - place)
        span = slice(block * HD, (block + 1) * HD)
        mixed = mixed_ref[span, :] * own_weight[block : block + 1] + returned_ref[span, :].astype(
            jnp.float32
        ) * far_weight[block : block + 1]
        part = mixed.T.astype(jnp.bfloat16)
        for head in range(heads):
            out_ref[target, :, head * HD : (head + 1) * HD] = part[
                head * TBLOCK : (head + 1) * TBLOCK
            ]


def combine(gate_scale, mixed, stat, returned, inner, heads):
    return pl.pallas_call(
        functools.partial(combine_kernel, inner, heads),
        out_shape=jax.ShapeDtypeStruct((stat.shape[0], TBLOCK, heads * HD), jnp.bfloat16),
        in_specs=[pl.BlockSpec(memory_space=pltpu.SMEM)] + whole(3),
        out_specs=whole(1)[0],
        compiler_params=pltpu.CompilerParams(vmem_limit_bytes=16 * 2**20),
        name="combine_planes",
    )(gate_scale, mixed, stat, returned)


def spread_kernel(in_ref, out_ref):
    group = in_ref.shape[2]
    for head in range(in_ref.shape[0]):
        out_ref[:, head * group : (head + 1) * group] = in_ref[head]


def spread(inward):
    count, rows, columns = inward.shape
    return pl.pallas_call(
        spread_kernel,
        out_shape=jax.ShapeDtypeStruct((rows, count * columns), inward.dtype),
        in_specs=whole(1),
        out_specs=whole(1)[0],
        compiler_params=pltpu.CompilerParams(vmem_limit_bytes=16 * 2**20),
        name="spread_heads",
    )(inward)


def on_device_split(
    axes,
    query_self,
    key_self,
    value_self,
    positions,
    query_cross,
    key_vision,
    value_vision,
    media_range,
    gate_scale,
):
    inner = key_self.shape[1] // HD
    heads = query_self.shape[1] // key_self.shape[1]
    rows = query_self.shape[0]
    group = heads * HD
    columns = axes["head"]
    devices = axes["ctx"]
    plane_count = devices // inner

    def place_of(device):
        return device // inner, device % inner

    def send(values, turn, flip, upward=0):
        pairs = []
        for device in range(devices):
            plane, place = place_of(device)
            target = plane ^ turn
            if upward == 0 or target ^ upward < target:
                pairs.append((device, target * inner + (place ^ flip)))
        return lax.ppermute(values, "ctx", pairs)

    exponents = np.arange(HD // 2) * (2.0 / HD)
    frequency = jnp.asarray(np.power(rope_base, -exponents), jnp.float32)
    sources = (positions, frequency, key_vision, value_vision, query_cross, query_self, key_self)
    near_out, other = prepare(media_range, *sources, value_self, inner, True)
    partner = send(other, 0, 1)
    near = send(near_out, 1, 0)
    value_self, near_out, other = lax.optimization_barrier((value_self, near_out, other))
    beside_out, own, own_self, across_out = prepare(media_range, *sources, value_self, inner, False)
    beside = send(beside_out, 0, 1)
    packets = jnp.concatenate([own, partner], axis=0)
    far = send(packets, 2, 0)
    across_out, partner = lax.optimization_barrier((across_out, partner))
    across = send(across_out, 1, 1)
    tail = slice(rows * heads, rows * heads + 2 * rows)
    last = send(jnp.concatenate([own[tail], partner[tail]], axis=0), 3, 0, upward=3)

    queries = (own, partner, far)
    count = own.shape[0]
    table = [values[count - TBLOCK, : 2 * (rows // TBLOCK) + 1] for values in queries]
    table.append(far[2 * count - TBLOCK, : 2 * (rows // TBLOCK) + 1])
    first_table = jnp.concatenate(table[:2]).astype(jnp.int32)
    table = jnp.concatenate(table).astype(jnp.int32)
    frames = (near_out, beside, near, across)
    sizes = (rows, inner, heads)
    units = ((0, (0, 2)), (1, (0, 2)), (2, ()), (3, ()))
    state = cross_part(first_table, queries, frames, units, (), "state", *sizes)
    units = ((0, ()), (1, ()), (2, (0, 2)), (3, (0, 2)))
    state = cross_part(table, queries, frames, units, state, "state", *sizes)
    units = ((0, (1,)), (1, (1,)), (2, (1,)), (3, (1,)))
    state = cross_part(table, queries, frames, units, state, "state", *sizes)
    units = ((2, (3,)), (3, (3,)))
    (outgoing,) = cross_part(table, queries, frames, units, state, "packed", *sizes)
    outgoing, last = lax.optimization_barrier((outgoing, last))
    returned = send(outgoing, 2, 0)
    outgoing, table, own_self = lax.optimization_barrier((outgoing, table, own_self))
    units = ((0, (3,)), (1, (3,)))
    mixed, stat = cross_part(table, queries, frames, units, state, "own", *sizes)
    self_rows = self_part(
        own_self, beside, (own, partner, near, across, far, last), *sizes
    )
    planes = [
        [
            (plane * inner + place) * columns + column
            for column in range(columns)
            for place in range(inner)
        ]
        for plane in range(plane_count)
    ]

    def exchange(outward):
        inward = lax.all_to_all(
            outward.reshape(-1, outward.shape[2]),
            ("ctx", "head"),
            0,
            0,
            axis_index_groups=planes,
            tiled=True,
        )
        return spread(inward.reshape(outward.shape))

    self_context = exchange(self_rows)
    cross_context = exchange(combine(gate_scale, mixed, stat, returned, inner, heads))
    return self_context, cross_context


def on_device(axes, *arguments):
    query_self, key_self, _, _, _, key_vision, _, media_range, _ = arguments
    inner = key_self.shape[1] // HD
    heads = query_self.shape[1] // key_self.shape[1]
    rows = query_self.shape[0]
    suited = (
        inner == 2
        and axes["ctx"] == 4 * inner
        and heads * TBLOCK == HD
        and key_vision.shape[0] == FRAME_LEN
        and rows == axes["head"] * TBLOCK
        and media_range.shape[0] * TBLOCK == rows
    )
    if suited:
        return on_device_split(axes, *arguments)
    return on_device_gathered(*arguments)


def solution(mesh):
    placed = (
        P("ctx", "head"),
        P("ctx", "head"),
        P("ctx", "head"),
        P("ctx"),
        P("ctx", "head"),
        P("ctx", "head"),
        P("ctx", "head"),
        P("ctx", None),
        P(),
    )
    return jax.shard_map(
        functools.partial(on_device, dict(mesh.shape)),
        mesh=mesh,
        in_specs=placed,
        out_specs=(P(("ctx", "head"), None), P(("ctx", "head"), None)),
        check_vma=False,
    )
```

```python
import functools

import jax
import jax.numpy as jnp
import numpy as np
from jax import lax
from jax.experimental import pallas as pl
from jax.experimental.pallas import tpu as pltpu
from jax.sharding import PartitionSpec as P

HD = 128
TBLOCK = 16
FRAME_LEN = 896


rope_base = 500000.0
lowest = -1e30


def rotate(values, positions):
    half_width = values.shape[-1] // 2
    exponents = jnp.arange(half_width, dtype=jnp.float32) * (2.0 / values.shape[-1])
    frequency = jnp.power(rope_base, -exponents)
    angles = positions.astype(jnp.float32)[:, None] * frequency[None, :]
    cosine = jnp.cos(angles)[:, None, :]
    sine_part = jnp.sin(angles)[:, None, :]
    first_half = values[..., :half_width]
    second_half = values[..., half_width:]
    return jnp.concatenate(
        [
            first_half * cosine - second_half * sine_part,
            second_half * cosine + first_half * sine_part,
        ],
        axis=-1,
    )


def key_block(key_count):
    block_size = min(key_count, 1024)
    while key_count % block_size != 0:
        block_size = block_size - 1
    return block_size


def attend_block(state_in, queries, key_rows, value_rows, allowed):
    maxima, totals, accumulated = state_in
    scale_factor = queries.shape[-1] ** (-0.5)
    scores = (
        jnp.einsum("rkgd,nkd->kgrn", queries, key_rows, preferred_element_type=jnp.float32)
        * scale_factor
    )
    visible = allowed[None, None, :, :]
    scores = jnp.where(visible, scores, lowest)
    new_maxima = jnp.maximum(maxima, jnp.max(scores, axis=-1))
    weights = jnp.where(visible, jnp.exp(scores - new_maxima[..., None]), 0.0)
    factor = jnp.exp(maxima - new_maxima)
    totals = totals * factor + jnp.sum(weights, axis=-1)
    accumulated = accumulated * factor[..., None] + jnp.einsum(
        "kgrn,nkd->kgrd",
        weights.astype(jnp.bfloat16),
        value_rows,
        preferred_element_type=jnp.float32,
    )
    return (new_maxima, totals, accumulated)


def attend(state_in, queries, key_rows, value_rows, allowed):
    key_count = key_rows.shape[0]
    block_size = key_block(key_count)
    if block_size == key_count:
        return attend_block(state_in, queries, key_rows, value_rows, allowed)

    def step_block(block_index, state_now):
        row_begin = block_index * block_size
        key_part = lax.dynamic_slice_in_dim(key_rows, row_begin, block_size, 0)
        value_part = lax.dynamic_slice_in_dim(value_rows, row_begin, block_size, 0)
        allowed_part = lax.dynamic_slice_in_dim(allowed, row_begin, block_size, 1)
        return attend_block(state_now, queries, key_part, value_part, allowed_part)

    return lax.fori_loop(0, key_count // block_size, step_block, state_in)


def keep_state(current):
    return current


def empty_state(row_count, kv_heads, group_size, head_size):
    maxima = jnp.full((kv_heads, group_size, row_count), lowest, jnp.float32)
    totals = jnp.zeros((kv_heads, group_size, row_count), jnp.float32)
    accumulated = jnp.zeros((kv_heads, group_size, row_count, head_size), jnp.float32)
    return (maxima, totals, accumulated)


def finish(state_in):
    maxima, totals, accumulated = state_in
    safe_totals = jnp.where(totals > 0.0, totals, 1.0)
    result = accumulated / safe_totals[..., None]
    kv_heads, group_size, row_count, head_size = result.shape
    return jnp.transpose(result, (2, 0, 1, 3)).reshape(row_count, kv_heads * group_size * head_size)


def causal_group(current, group, key_rows, value_rows, key_index, offset):
    queries, row_index = group
    allowed = key_index[None, :] <= row_index[:, None]

    def causal_compute(state_in):
        return attend(state_in, queries, key_rows, value_rows, allowed)

    return lax.cond(offset <= jnp.max(row_index), causal_compute, keep_state, current)


def frame_mask(frame_index, lower_frame, upper_frame):
    return jnp.logical_and(
        frame_index[None, :] >= lower_frame[:, None], frame_index[None, :] < upper_frame[:, None]
    )


def on_device_gathered(
    query_self,
    key_self,
    value_self,
    positions,
    query_cross,
    key_vision,
    value_vision,
    media_range,
    gate_scale,
):
    head_size = HD
    kv_heads = key_self.shape[1] // head_size
    group_size = query_self.shape[1] // key_self.shape[1]
    row_count = query_self.shape[0]
    vision_count = key_vision.shape[0]
    device = lax.axis_index("ctx")
    own_rows = device * row_count + jnp.arange(row_count, dtype=jnp.int32)
    rotated_query = rotate(
        query_self.astype(jnp.float32).reshape(row_count, kv_heads * group_size, head_size),
        positions,
    )
    rotated_query = rotated_query.astype(jnp.bfloat16).reshape(
        row_count, kv_heads, group_size, head_size
    )
    rotated_key = rotate(
        key_self.astype(jnp.float32).reshape(row_count, kv_heads, head_size), positions
    ).astype(jnp.bfloat16)
    self_values = value_self.reshape(row_count, kv_heads, head_size)
    vision_keys = key_vision.reshape(vision_count, kv_heads, head_size)
    vision_values = value_vision.reshape(vision_count, kv_heads, head_size)
    cross_queries = query_cross.reshape(row_count, kv_heads, group_size, head_size)
    lower_frame = jnp.repeat(media_range[:, 0], TBLOCK)
    upper_frame = jnp.repeat(media_range[:, 1], TBLOCK)
    has_frames = upper_frame > lower_frame
    query_groups = ((rotated_query, own_rows),)
    self_start = tuple(
        (empty_state(group[1].shape[0], kv_heads, group_size, head_size) for group in query_groups)
    )
    cross_start = empty_state(row_count, kv_heads, group_size, head_size)
    offset = jnp.int32(0)
    key_rows = lax.all_gather(rotated_key, "ctx", axis=0, tiled=True)
    value_rows = lax.all_gather(self_values, "ctx", axis=0, tiled=True)
    key_index = jnp.arange(key_rows.shape[0], dtype=jnp.int32)
    updated = []
    for current, group in zip(self_start, query_groups):
        updated.append(causal_group(current, group, key_rows, value_rows, key_index, offset))
    self_states = tuple(updated)
    key_rows = lax.all_gather(vision_keys, "ctx", axis=0, tiled=True)
    value_rows = lax.all_gather(vision_values, "ctx", axis=0, tiled=True)
    frame_index = jnp.arange(key_rows.shape[0], dtype=jnp.int32) // FRAME_LEN
    allowed = frame_mask(frame_index, lower_frame, upper_frame)
    touching = jnp.logical_and(lower_frame <= frame_index[-1], upper_frame > frame_index[0])
    needed = jnp.any(jnp.logical_and(has_frames, touching))

    def fold_compute(state_in):
        return attend(state_in, cross_queries, key_rows, value_rows, allowed)

    cross_state = lax.cond(needed, fold_compute, keep_state, cross_start)
    self_rows = finish(self_states[0]).astype(jnp.bfloat16)
    cross_rows = jnp.where(
        has_frames[:, None], jnp.tanh(gate_scale[0]) * finish(cross_state), 0.0
    ).astype(jnp.bfloat16)
    self_context, cross_context = (
        lax.all_to_all(self_rows, "head", split_axis=0, concat_axis=1, tiled=True),
        lax.all_to_all(cross_rows, "head", split_axis=0, concat_axis=1, tiled=True),
    )
    return (self_context, cross_context)


log2e = 1.4426950408889634
stat_rows = 16
score_limit = 100.0
unseen = -1e30
contract_last = (((1,), (1,)), ((), ()))


def whole(count):
    return [pl.BlockSpec(memory_space=pltpu.VMEM)] * count


def largest_square(values):
    sums = lax.dot_general(
        jnp.ones((8, values.shape[1]), jnp.bfloat16),
        values * values,
        contract_last,
        preferred_element_type=jnp.float32,
    )
    return jnp.max(jnp.max(sums, axis=0, keepdims=True), axis=1, keepdims=True)


def prepare_kernel(
    inner,
    first,
    range_ref,
    position_ref,
    frequency_ref,
    vision_key_ref,
    vision_value_ref,
    cross_ref,
    query_ref,
    key_ref,
    value_ref,
    *refs,
):
    if first:
        vision_out, packet_out = refs[:2]
    else:
        vision_out, packet_out, self_out, across_out = refs[:4]
    range_table, position_row, frequency_row, vision_rows, cross_rows = refs[-13:-8]
    query_rows, key_rows = refs[-8:-6]
    value_rows, packet_rows, self_rows, pair_rows, in_semaphores, out_semaphores = refs[-6:]
    rows, group = cross_rows.shape
    heads = group // HD
    vision = vision_key_ref.shape[0]
    stacked = heads * rows
    place = lax.rem(lax.axis_index("ctx"), inner)
    sides = (place, 1 - place)
    vision_side, packet_side = (sides[0], sides[1]) if first else (sides[1], sides[0])

    def head_columns(head):
        return pl.ds(pl.multiple_of(head * HD, HD), HD)

    def load(source, target):
        copy = pltpu.make_async_copy(source, target, in_semaphores.at[len(loads)])
        copy.start()
        loads.append(copy)

    def store(source, target):
        copy = pltpu.make_async_copy(source, target, out_semaphores.at[len(stores)])
        copy.start()
        stores.append(copy)

    loads, stores = [], []
    load(position_ref, position_row)
    load(frequency_ref, frequency_row)
    load(range_ref, range_table)
    load(cross_ref.at[:, pl.ds(pl.multiple_of(packet_side * group, group), group)], cross_rows)
    load(key_ref, key_rows)
    load(value_ref, value_rows)
    for slot, source in enumerate((vision_key_ref, vision_value_ref)):
        load(
            source.at[:, head_columns(vision_side)], vision_rows.at[pl.ds(slot * vision, vision), :]
        )
    if not first:
        load(query_ref, query_rows)

    def stack(target, head, block):
        for step in range(rows // TBLOCK):
            row = (step * heads + head) * TBLOCK
            target[row : row + TBLOCK, :] = block[step * TBLOCK : (step + 1) * TBLOCK]

    for copy in loads[:2]:
        copy.wait()
    place_of_row = jnp.broadcast_to(position_row[...].astype(jnp.float32), (HD, rows)).T
    frequency = jnp.concatenate([frequency_row[...]] * 2, axis=1)
    angles = place_of_row * frequency
    cosine = jnp.cos(angles)
    column = lax.broadcasted_iota(jnp.int32, angles.shape, 1)
    sine = jnp.sin(angles) * jnp.where(column < HD // 2, -1.0, 1.0)

    def turned(block):
        block = block.astype(jnp.float32)
        return (block * cosine + pltpu.roll(block, HD // 2, 1) * sine).astype(jnp.bfloat16)

    for copy in loads[2:6]:
        copy.wait()
    lane = lax.broadcasted_iota(jnp.int32, (TBLOCK, HD), 1)
    ranges = jnp.zeros((TBLOCK, HD), jnp.int32)
    for item in range(2 * rows // TBLOCK):
        ranges = jnp.where(lane == item, range_table[item % 2, item // 2], ranges)
    ranges = ranges.astype(jnp.float32)
    for head in range(heads):
        stack(packet_rows, head, cross_rows[:, head * HD : (head + 1) * HD])
    packet_rows[stacked : stacked + rows, :] = turned(key_rows[:, head_columns(packet_side)])
    packet_rows[stacked + rows : stacked + 2 * rows, :] = value_rows[:, head_columns(packet_side)]
    largest = largest_square(packet_rows[:stacked, :]) * 1.02 + 2.0
    ranges = jnp.where(lane == 2 * rows // TBLOCK, largest, ranges).astype(jnp.bfloat16)
    packet_rows[stacked + 2 * rows :, :] = ranges
    store(packet_rows, packet_out)
    with_self = vision_out if first else across_out
    pair_rows[:rows, :] = turned(key_rows[:, head_columns(vision_side)])
    pair_rows[rows:, :] = value_rows[:, head_columns(vision_side)]
    store(pair_rows, with_self.at[pl.ds(2 * vision, 2 * rows), :])
    for slot, copy in enumerate(loads[6:8]):
        span = pl.ds(slot * vision, vision)
        copy.wait()
        store(vision_rows.at[span, :], vision_out.at[span, :])
        if not first:
            store(vision_rows.at[span, :], across_out.at[span, :])
    if not first:
        loads[8].wait()
        tails = (vision_out.at[pl.ds(2 * vision, stacked), :], self_out)
        for side, target in zip((1, 0), tails):
            part = self_rows.at[pl.ds(side * stacked, stacked), :]
            for head in range(heads):
                stack(part, head, turned(query_rows[:, head_columns(sides[side] * heads + head)]))
            store(part, target)
    for copy in stores:
        copy.wait()


def prepare(ranges, positions, frequency, vision_keys, vision_values, cross, query, key, value, inner, first):
    rows, columns = query.shape
    group = columns // inner
    stacked = rows * (group // HD)
    vision = vision_keys.shape[0]
    packet = stacked + 2 * rows + TBLOCK
    counts = [2 * vision + 2 * rows, packet]
    if not first:
        counts = [2 * vision + stacked, packet, stacked, 2 * vision + 2 * rows]
    return pl.pallas_call(
        functools.partial(prepare_kernel, inner, first),
        out_shape=[jax.ShapeDtypeStruct((count, HD), jnp.bfloat16) for count in counts],
        in_specs=[pl.BlockSpec(memory_space=pl.ANY)] * 9,
        out_specs=[pl.BlockSpec(memory_space=pl.ANY)] * len(counts),
        scratch_shapes=[
            pltpu.SMEM((2, ranges.shape[0]), jnp.int32),
            pltpu.VMEM((1, rows), jnp.int32),
            pltpu.VMEM((1, HD // 2), jnp.float32),
            pltpu.VMEM((2 * vision, HD), jnp.bfloat16),
            pltpu.VMEM((rows, group), jnp.bfloat16),
            pltpu.VMEM(query.shape, jnp.bfloat16),
            pltpu.VMEM(key.shape, jnp.bfloat16),
            pltpu.VMEM(value.shape, jnp.bfloat16),
            pltpu.VMEM((packet, HD), jnp.bfloat16),
            pltpu.VMEM((2 * stacked, HD), jnp.bfloat16),
            pltpu.VMEM((2 * rows, HD), jnp.bfloat16),
            pltpu.SemaphoreType.DMA((9,)),
            pltpu.SemaphoreType.DMA((8,)),
        ],
        compiler_params=pltpu.CompilerParams(vmem_limit_bytes=60 * 2**20),
        name="prepare_first" if first else "prepare_second",
    )(
        jnp.transpose(ranges),
        positions.reshape(1, rows),
        frequency.reshape(1, HD // 2),
        vision_keys,
        vision_values,
        cross,
        query,
        key,
        value,
    )


def fold_keys(keys, values_turned, jobs, bounded=False):
    scale = HD**-0.5 * log2e
    spans = []
    for job in jobs:
        width = min(256, job[0].shape[0])
        for begin in range(0, job[0].shape[0], width):
            spans.append((job, slice(begin, begin + width)))
    scores = [
        lax.dot_general(
            keys, stacked_ref[span, :], contract_last, preferred_element_type=jnp.float32
        )
        for (stacked_ref, *_), span in spans
    ]
    for (job, span), score in zip(spans, scores):
        _, peak_ref, total_ref, visible, old_peak_ref, old_total_ref = job
        peak = old_peak_ref[0:1, span]
        seen = visible[:, span]
        if seen.shape[0] == 1:
            highest = 0.0 if bounded else jnp.max(score, axis=0, keepdims=True) * scale
            new_peak = jnp.where(seen, jnp.maximum(peak, highest), peak)
            weights = jnp.exp2(score * scale - jnp.where(seen, new_peak, -unseen))
        else:
            score = jnp.where(seen, score * scale, unseen)
            new_peak = jnp.maximum(peak, jnp.max(score, axis=0, keepdims=True))
            weights = jnp.where(seen, jnp.exp2(score - new_peak), 0.0)
        total_ref[:, span] = old_total_ref[:, span] * jnp.exp2(peak - new_peak) + jnp.dot(
            values_turned, weights.astype(jnp.bfloat16), preferred_element_type=jnp.float32
        )
        peak_ref[0:1, span] = new_peak


def clear(peak_ref, total_ref):
    peak_ref[...] = jnp.full(peak_ref.shape, unseen, jnp.float32)
    total_ref[...] = jnp.zeros(total_ref.shape, jnp.float32)


def finish_columns(peak_ref, total_ref):
    sums = total_ref[HD : HD + 1, :]
    some = sums > 0.0
    safe = jnp.where(some, sums, 1.0)
    log_sum = jnp.where(some, peak_ref[0:1, :] + jnp.log2(safe), unseen)
    return total_ref[:HD, :] / safe, log_sum


def turn_values(value, target_ref):
    target_ref[:HD, :] = value.T
    target_ref[HD:, :] = jnp.ones((stat_rows, target_ref.shape[1]), jnp.bfloat16)


def frame_numbers(inner):
    device = lax.axis_index("ctx")
    plane, place = device // inner, lax.rem(device, inner)
    near = plane + 1 - 2 * lax.rem(plane, 2)
    return (
        plane * inner + place,
        plane * inner + 1 - place,
        near * inner + place,
        near * inner + 1 - place,
    )


def cross_kernel(inner, heads, columns, places, units, chosen, resumed, finish, table_source, *refs):
    refs = list(refs)
    arrays = sorted({places[number][0] for number, frames in units if frames})
    arrays = {array: refs.pop(0) for array in arrays}
    query_refs = {}
    for number, frames in units:
        if frames:
            array, row = places[number]
            query_refs[number] = arrays[array].at[pl.ds(row, columns), :]
    frame_refs = [refs.pop(0) for _ in chosen]
    state_refs = [refs.pop(0) for _ in range(2)] if resumed else None
    out_refs, (turned_ref, peaks_ref, totals_ref, table_ref, semaphore) = refs[:-5], refs[-5:]
    load = pltpu.make_async_copy(table_source, table_ref, semaphore)
    load.start()
    if finish == "state":
        peaks_ref, totals_ref = out_refs
    lanes = heads * TBLOCK
    blocks = columns // lanes
    frames = frame_numbers(inner)
    vision = turned_ref.shape[2]

    def resume(turn, number):
        peaks_ref[turn] = state_refs[0][number]
        totals_ref[turn] = state_refs[1][number]

    for turn, (number, _) in enumerate(units):
        if resumed and not units[turn][1]:
            resume(turn, number)
        elif not resumed:
            clear(peaks_ref.at[turn], totals_ref.at[turn])

    def job(turn, number, flags, index):
        visible = jnp.concatenate([jnp.full((1, lanes), flag, jnp.int32) for flag in flags], axis=1)
        here = (peaks_ref.at[turn], totals_ref.at[turn])
        begins = resumed and index == units[turn][1][0]
        before = (state_refs[0].at[number], state_refs[1].at[number]) if begins else here
        return query_refs[number], *here, visible > 0, *before

    for slot, index in enumerate(chosen):
        turn_values(frame_refs[slot][vision : 2 * vision, :], turned_ref.at[slot])
        if slot == 0:
            load.wait()
        keys = frame_refs[slot][:vision, :]
        limit = largest_square(keys)[0, 0] * (1.05 * (HD**-0.5 * log2e / score_limit) ** 2)
        members = []
        for turn, (number, indices) in enumerate(units):
            if index not in indices:
                continue
            flags = []
            for block in range(blocks):
                at = number * (2 * blocks + 1) + 2 * block
                inside = jnp.logical_and(
                    table_ref[at] <= frames[index], frames[index] < table_ref[at + 1]
                )
                flags.append(inside.astype(jnp.int32))
            needed = functools.reduce(jnp.maximum, flags)
            if resumed and index == indices[0]:
                pl.when(needed == 0)(functools.partial(resume, turn, number))
            square = table_ref[number * (2 * blocks + 1) + 2 * blocks].astype(jnp.float32)
            bounded = (square * limit < 1.0).astype(jnp.int32)
            members.append((turn, number, flags, needed * bounded, needed * (1 - bounded)))

        def fold(taken, bounded):
            jobs = [job(turn, number, flags, index) for turn, number, flags, _, _ in taken]
            fold_keys(frame_refs[slot][:vision, :], turned_ref[slot], jobs, bounded)

        for begin in range(0, len(members), 2):
            pair = members[begin : begin + 2]
            count = sum(member[3] for member in pair)
            if len(pair) == 2:
                pl.when(count == 2)(functools.partial(fold, pair, True))
            for member in pair:
                alone = jnp.logical_and(count == 1, member[3] == 1)
                pl.when(alone)(functools.partial(fold, [member], True))
                pl.when(member[4] == 1)(functools.partial(fold, [member], False))

    if finish == "state":
        return
    stats = []
    for turn in range(len(units)):
        mixed, log_sum = finish_columns(peaks_ref.at[turn], totals_ref.at[turn])
        for block in range(blocks):
            span = slice(block * lanes, (block + 1) * lanes)
            stats.append(log_sum[:, span])
            row = (turn * blocks + block) * HD
            out_refs[0][row : row + HD, :] = mixed[:, span].astype(out_refs[0].dtype)
    stat = jnp.concatenate(stats, axis=0)
    if finish == "packed":
        high = stat.astype(jnp.bfloat16)
        rest = stat - high.astype(jnp.float32)
        middle = rest.astype(jnp.bfloat16)
        low = rest - middle.astype(jnp.float32)
        rows = [high.astype(jnp.float32), middle.astype(jnp.float32), low, jnp.zeros_like(stat)]
        out_refs[0][len(stats) * HD :, :] = jnp.concatenate(rows, axis=0).astype(jnp.bfloat16)
    else:
        out_refs[1][...] = stat


def cross_part(table, queries, frames, units, state, finish, rows, inner, heads):
    lanes = heads * TBLOCK
    columns = rows * heads
    vision = FRAME_LEN
    count = len(units) * (rows // TBLOCK)
    chosen = tuple(sorted({index for _, indices in units for index in indices}))
    if finish == "state":
        out_shape = (
            jax.ShapeDtypeStruct((len(units), 8, columns), jnp.float32),
            jax.ShapeDtypeStruct((len(units), HD + stat_rows, columns), jnp.float32),
        )
    elif finish == "packed":
        out_shape = (jax.ShapeDtypeStruct((count * HD + 4 * count, lanes), jnp.bfloat16),)
    else:
        out_shape = (
            jax.ShapeDtypeStruct((count * HD, lanes), jnp.float32),
            jax.ShapeDtypeStruct((count, lanes), jnp.float32),
        )
    packet = columns + 2 * rows + TBLOCK
    places = ((0, 0), (1, 0), (2, 0), (2, packet))
    arrays = sorted({places[number][0] for number, indices in units if indices})
    arguments = [queries[array] for array in arrays]
    arguments += [*(frames[index] for index in chosen), *state]
    return pl.pallas_call(
        functools.partial(
            cross_kernel, inner, heads, columns, places, units, chosen, len(state) > 0, finish
        ),
        out_shape=out_shape,
        in_specs=[pl.BlockSpec(memory_space=pl.ANY)] + whole(len(arguments)),
        out_specs=whole(len(out_shape)),
        scratch_shapes=[
            pltpu.VMEM((len(chosen), HD + stat_rows, vision), jnp.bfloat16),
            pltpu.VMEM((len(units), 8, columns), jnp.float32),
            pltpu.VMEM((len(units), HD + stat_rows, columns), jnp.float32),
            pltpu.SMEM(table.shape, jnp.int32),
            pltpu.SemaphoreType.DMA,
        ],
        compiler_params=pltpu.CompilerParams(vmem_limit_bytes=28 * 2**20),
        name="cross_" + finish,
    )(table, *arguments)


def self_kernel(inner, heads, rows, own_ref, beside_ref, *refs):
    key_value_refs, out_ref = refs[:6], refs[6]
    key_ref, value_ref, turned_ref, peak_ref, total_ref = refs[7:]
    device = lax.axis_index("ctx")
    plane, place = device // inner, lax.rem(device, inner)
    lanes = heads * TBLOCK
    columns = rows * heads
    vision = beside_ref.shape[0] - columns
    own_kv, partner_kv, near_kv, across_kv, far_kv, last_kv = key_value_refs
    packet = own_kv.shape[0]
    vision_rows = near_kv.shape[0] - 2 * rows
    tails = [(own_kv, columns), (partner_kv, columns), (near_kv, vision_rows)]
    tails += [(across_kv, vision_rows), (far_kv, columns), (far_kv, packet + columns)]
    tails += [(last_kv, 0), (last_kv, 2 * rows)]
    for slot, (ref, begin) in enumerate(tails):
        span = slice(slot * rows, (slot + 1) * rows)
        key_ref[span, :] = ref[begin : begin + rows, :]
        value_ref[span, :] = ref[begin + rows : begin + 2 * rows, :]
    turn_values(value_ref[...], turned_ref)
    planes = (plane, plane + 1 - 2 * lax.rem(plane, 2), lax.rem(plane + 2, 4), 3 - plane)
    starts = []
    for source in planes:
        starts.append((source * inner + place) * rows)
        starts.append((source * inner + 1 - place) * rows)
    down = lax.broadcasted_iota(jnp.int32, (rows, columns), 0)
    key_index = jnp.concatenate([down + start for start in starts], axis=0)
    across = lax.broadcasted_iota(jnp.int32, key_index.shape, 1)
    token = (across // lanes) * TBLOCK + lax.rem(across, TBLOCK)
    queries = (own_ref, beside_ref.at[pl.ds(vision, columns), :])
    for slot, query_ref in enumerate(queries):
        side = place if slot == 0 else 1 - place
        clear(peak_ref, total_ref)
        visible = key_index <= token + (plane * inner + side) * rows
        fold_keys(key_ref[...], turned_ref[...], [(query_ref, peak_ref, total_ref, visible, peak_ref, total_ref)])
        mixed, _ = finish_columns(peak_ref, total_ref)
        for block in range(rows // TBLOCK):
            part = mixed[:, block * lanes : (block + 1) * lanes].T.astype(jnp.bfloat16)
            for head in range(heads):
                out_ref[block * inner + side, :, head * HD : (head + 1) * HD] = part[
                    head * TBLOCK : (head + 1) * TBLOCK
                ]


def self_part(own, beside, key_values, rows, inner, heads):
    return pl.pallas_call(
        functools.partial(self_kernel, inner, heads, rows),
        out_shape=jax.ShapeDtypeStruct((inner * rows // TBLOCK, TBLOCK, heads * HD), jnp.bfloat16),
        in_specs=whole(2 + len(key_values)),
        out_specs=whole(1)[0],
        scratch_shapes=[
            pltpu.VMEM((8 * rows, HD), jnp.bfloat16),
            pltpu.VMEM((8 * rows, HD), jnp.bfloat16),
            pltpu.VMEM((HD + stat_rows, 8 * rows), jnp.bfloat16),
            pltpu.VMEM((8, rows * heads), jnp.float32),
            pltpu.VMEM((HD + stat_rows, rows * heads), jnp.float32),
        ],
        compiler_params=pltpu.CompilerParams(vmem_limit_bytes=24 * 2**20),
        name="self_attention",
    )(own, beside, *key_values)


def combine_kernel(inner, heads, gate_ref, mixed_ref, stat_ref, returned_ref, out_ref):
    count = stat_ref.shape[0]
    side = count // inner
    place = lax.rem(lax.axis_index("ctx"), inner)
    gate = jnp.tanh(jnp.full((1, heads * TBLOCK), gate_ref[0], jnp.float32))
    stats = returned_ref[count * HD :, :].astype(jnp.float32)
    far_stat = stats[:count] + stats[count : 2 * count] + stats[2 * count : 3 * count]
    own_stat = stat_ref[...]
    peak = jnp.maximum(own_stat, far_stat)
    own_weight = jnp.exp2(own_stat - peak)
    far_weight = jnp.exp2(far_stat - peak)
    ratio = gate / (own_weight + far_weight)
    own_weight, far_weight = own_weight * ratio, far_weight * ratio
    for block in range(count):
        target = (block % side) * inner + (place if block < side else 1 - place)
        span = slice(block * HD, (block + 1) * HD)
        mixed = mixed_ref[span, :] * own_weight[block : block + 1] + returned_ref[span, :].astype(
            jnp.float32
        ) * far_weight[block : block + 1]
        part = mixed.T.astype(jnp.bfloat16)
        for head in range(heads):
            out_ref[target, :, head * HD : (head + 1) * HD] = part[
                head * TBLOCK : (head + 1) * TBLOCK
            ]


def combine(gate_scale, mixed, stat, returned, inner, heads):
    return pl.pallas_call(
        functools.partial(combine_kernel, inner, heads),
        out_shape=jax.ShapeDtypeStruct((stat.shape[0], TBLOCK, heads * HD), jnp.bfloat16),
        in_specs=[pl.BlockSpec(memory_space=pltpu.SMEM)] + whole(3),
        out_specs=whole(1)[0],
        compiler_params=pltpu.CompilerParams(vmem_limit_bytes=16 * 2**20),
        name="combine_planes",
    )(gate_scale, mixed, stat, returned)


def spread_kernel(in_ref, out_ref):
    group = in_ref.shape[2]
    for head in range(in_ref.shape[0]):
        out_ref[:, head * group : (head + 1) * group] = in_ref[head]


def spread(inward):
    count, rows, columns = inward.shape
    return pl.pallas_call(
        spread_kernel,
        out_shape=jax.ShapeDtypeStruct((rows, count * columns), inward.dtype),
        in_specs=whole(1),
        out_specs=whole(1)[0],
        compiler_params=pltpu.CompilerParams(vmem_limit_bytes=16 * 2**20),
        name="spread_heads",
    )(inward)


def on_device_split(
    axes,
    query_self,
    key_self,
    value_self,
    positions,
    query_cross,
    key_vision,
    value_vision,
    media_range,
    gate_scale,
):
    inner = key_self.shape[1] // HD
    heads = query_self.shape[1] // key_self.shape[1]
    rows = query_self.shape[0]
    group = heads * HD
    columns = axes["head"]
    devices = axes["ctx"]
    plane_count = devices // inner

    def place_of(device):
        return device // inner, device % inner

    def send(values, turn, flip, upward=0):
        pairs = []
        for device in range(devices):
            plane, place = place_of(device)
            target = plane ^ turn
            if upward == 0 or target ^ upward < target:
                pairs.append((device, target * inner + (place ^ flip)))
        return lax.ppermute(values, "ctx", pairs)

    exponents = np.arange(HD // 2) * (2.0 / HD)
    frequency = jnp.asarray(np.power(rope_base, -exponents), jnp.float32)
    sources = (positions, frequency, key_vision, value_vision, query_cross, query_self, key_self)
    near_out, other = prepare(media_range, *sources, value_self, inner, True)
    partner = send(other, 0, 1)
    near = send(near_out, 1, 0)
    value_self, near_out, other = lax.optimization_barrier((value_self, near_out, other))
    beside_out, own, own_self, across_out = prepare(media_range, *sources, value_self, inner, False)
    beside = send(beside_out, 0, 1)
    packets = jnp.concatenate([own, partner], axis=0)
    far = send(packets, 2, 0)
    across_out, partner = lax.optimization_barrier((across_out, partner))
    across = send(across_out, 1, 1)
    tail = slice(rows * heads, rows * heads + 2 * rows)
    last = send(jnp.concatenate([own[tail], partner[tail]], axis=0), 3, 0, upward=3)

    queries = (own, partner, far)
    count = own.shape[0]
    table = [values[count - TBLOCK, : 2 * (rows // TBLOCK) + 1] for values in queries]
    table.append(far[2 * count - TBLOCK, : 2 * (rows // TBLOCK) + 1])
    first_table = jnp.concatenate(table[:2]).astype(jnp.int32)
    table = jnp.concatenate(table).astype(jnp.int32)
    frames = (near_out, beside, near, across)
    sizes = (rows, inner, heads)
    units = ((0, (0, 2)), (1, (0, 2)), (2, ()), (3, ()))
    state = cross_part(first_table, queries, frames, units, (), "state", *sizes)
    units = ((0, ()), (1, ()), (2, (0, 2)), (3, (0, 2)))
    state = cross_part(table, queries, frames, units, state, "state", *sizes)
    units = ((0, (1,)), (1, (1,)), (2, (1,)), (3, (1,)))
    state = cross_part(table, queries, frames, units, state, "state", *sizes)
    units = ((2, (3,)), (3, (3,)))
    (outgoing,) = cross_part(table, queries, frames, units, state, "packed", *sizes)
    outgoing, last = lax.optimization_barrier((outgoing, last))
    returned = send(outgoing, 2, 0)
    outgoing, table, own_self = lax.optimization_barrier((outgoing, table, own_self))
    units = ((0, (3,)), (1, (3,)))
    mixed, stat = cross_part(table, queries, frames, units, state, "own", *sizes)
    self_rows = self_part(
        own_self, beside, (own, partner, near, across, far, last), *sizes
    )
    planes = [
        [
            (plane * inner + place) * columns + column
            for column in range(columns)
            for place in range(inner)
        ]
        for plane in range(plane_count)
    ]

    def exchange(outward):
        inward = lax.all_to_all(
            outward.reshape(-1, outward.shape[2]),
            ("ctx", "head"),
            0,
            0,
            axis_index_groups=planes,
            tiled=True,
        )
        return spread(inward.reshape(outward.shape))

    self_context = exchange(self_rows)
    cross_context = exchange(combine(gate_scale, mixed, stat, returned, inner, heads))
    return self_context, cross_context


def on_device(axes, *arguments):
    query_self, key_self, _, _, _, key_vision, _, media_range, _ = arguments
    inner = key_self.shape[1] // HD
    heads = query_self.shape[1] // key_self.shape[1]
    rows = query_self.shape[0]
    suited = (
        inner == 2
        and axes["ctx"] == 4 * inner
        and heads * TBLOCK == HD
        and key_vision.shape[0] == FRAME_LEN
        and rows == axes["head"] * TBLOCK
        and media_range.shape[0] * TBLOCK == rows
    )
    if suited:
        return on_device_split(axes, *arguments)
    return on_device_gathered(*arguments)


def solution(mesh):
    placed = (
        P("ctx", "head"),
        P("ctx", "head"),
        P("ctx", "head"),
        P("ctx"),
        P("ctx", "head"),
        P("ctx", "head"),
        P("ctx", "head"),
        P("ctx", None),
        P(),
    )
    return jax.shard_map(
        functools.partial(on_device, dict(mesh.shape)),
        mesh=mesh,
        in_specs=placed,
        out_specs=(P(("ctx", "head"), None), P(("ctx", "head"), None)),
        check_vma=False,
    )
```
